32 devices in a mesh: code: 2 (over core), aa: 8 (over z, y), ba: 2 (over x).
Axes of the slice: x: 2, y: 2, z: 4, core: 2. Of those that a mesh axis runs over, the one named last changes fastest.
Arguments:
- states: float32 [2, 64, 65536], P('code', 'ba', 'aa'), may hold values from -4 to 4, as said below
- coupled: float32 [2, 3, 64, 65536], P('code', None, 'ba', 'aa'), may hold values from -2 to 2, as said below
- facies: int32 [2, 64, 65536], P('code', 'ba', 'aa'), may hold values from 0 to 5, as said below
- injectors: int32 [2, 64, 65536], P('code', 'ba', 'aa'), may hold values from 0 to 1, as said below
- producers: int32 [2, 64, 65536], P('code', 'ba', 'aa'), may hold values from 0 to 1, as said below
- perm_table: float32 [6], replicated, may hold values from 0.1 to 10
- cond_table: float32 [6], replicated, may hold values from 0.1 to 1
Outputs:
- stepped_states: float32 [2, 64, 65536], P('code', 'ba', 'aa')
- new_coupled: float32 [2, 3, 64, 65536], P('code', None, 'ba', 'aa')
The draws below stay inside these ranges and needn't reach their ends.
Inputs may be any that keep to these rules, and one draw needn't show every extreme that they name: Slice 1 of states lies in [0, 1]. Slice 0 of coupled lies in [0.2, 1]. `facies`: both slices hold the same class map of the grid, each in its group's layout. `injectors`: 0 or 1; both slices mark the same cells; no cell is both an injector and a producer. `producers`: 0 or 1; both slices mark the same cells; no cell is both an injector and a producer.
All inputs are finite; a program needn't handle non-finite values.
Results may differ from the reference program's by a relative error of at most 0.00002.
Values sent between devices are 32-bit elements; how exact they have to be, the bound alone decides.
No kernel may reach another device: no remote copies, remote signals or barrier semaphores. Data moves between devices by JAX's collectives and lax.ppermute only.
A program may use at most 128 MiB of HBM per device.

```python
import math
import jax
import jax.numpy as jnp

W = 64
NF = 6
ITERS = 4
NX = 1024


def both_layouts(grid):
    return jnp.stack([grid.reshape(W, NX * W), jnp.transpose(grid, (2, 1, 0)).reshape(W, NX * W)])


def well_codes(key):
    return jax.random.randint(key, (W, NX, W), 0, 32)


def draw_facies(key, part):
    key = jax.random.fold_in(key, 5)
    classes = jax.random.randint(key, (W, NX, W), 0, NF)
    return both_layouts(classes).astype(jnp.int32)


def draw_injectors(key, part):
    codes = well_codes(key)
    return both_layouts(jnp.where(codes == 0, 1, 0)).astype(jnp.int32)


def draw_producers(key, part):
    codes = well_codes(key)
    return both_layouts(jnp.where(codes == 1, 1, 0)).astype(jnp.int32)


def draw_states(key, part):
    key = jax.random.fold_in(key, 11)
    key_one, key_two = jax.random.split(key)
    pressure = jnp.clip(jax.random.normal(key_one, (W, NX * W), jnp.float32), -4.0, 4.0)
    heat = jax.random.uniform(key_two, (W, NX * W), jnp.float32)
    return jnp.stack([pressure, heat]).astype(jnp.float32)


def draw_coupled(key, part):
    key = jax.random.fold_in(key, 17)
    key_one, key_two = jax.random.split(key)
    fluid = jax.random.uniform(key_one, (3, W, NX * W), jnp.float32, 0.2, 1.0)
    drops = jax.random.uniform(key_two, (3, W, NX * W), jnp.float32, -2.0, 2.0)
    return jnp.stack([fluid, drops]).astype(jnp.float32)


def setup_inputs(seed: int = 0) -> dict:
    splits = jax.random.split(jax.random.key(seed), 8)
    return {
        "states": draw_states(jax.random.fold_in(splits[7], 71), 0),
        "coupled": draw_coupled(jax.random.fold_in(splits[7], 71), 0),
        "facies": draw_facies(jax.random.fold_in(splits[7], 71), 0),
        "injectors": draw_injectors(jax.random.fold_in(splits[7], 71), 0),
        "producers": draw_producers(jax.random.fold_in(splits[7], 71), 0),
        "perm_table": jnp.clip(jnp.exp(jax.random.uniform(splits[5], (NF,), jnp.float32, math.log(0.1), math.log(10.0))), 0.1, 10.0),
        "cond_table": jnp.clip(jnp.exp(jax.random.uniform(splits[6], (NF,), jnp.float32, math.log(0.1), math.log(1.0))), 0.1, 1.0),
    }


STORAGE = 0.5
LOWER_BOUND = 0.05
INJECTION = 2.0
PRODUCT_INDEX = 1.0
WELL_PRESSURE = -1.0
FLOW_RATE = 1.0
CHILLED_INFLOW = 0.1
TIME_STEP = 0.05


def brine_flowability(matrix_heat_level):
    return 0.2 + 0.8 * jax.nn.sigmoid(6.0 * (matrix_heat_level - 0.5))


def harmonic(left_val, eastern_neighbor_number, face_mask):
    return face_mask * 2.0 * left_val * eastern_neighbor_number / (left_val + eastern_neighbor_number + 1.0 - face_mask)


def accumulate(terms):
    result = terms[0]
    for term in terms[1:]:
        result = result + term
    return result


def sweep_weights():
    centre_val = (2.0 + LOWER_BOUND) / 2.0
    half_width = (2.0 - LOWER_BOUND) / 2.0
    quotient_number = centre_val / half_width
    rho_old = 1.0 / quotient_number
    chebyshev = [(1.0 / centre_val, 0.0)]
    for index_k in range(1, ITERS):
        rho_new = 1.0 / (2.0 * quotient_number - rho_old)
        chebyshev.append((2.0 * rho_new / half_width, rho_new * rho_old))
        rho_old = rho_new
    explicit = []
    for index_k in range(ITERS):
        if index_k % 2 == 0:
            explicit.append((TIME_STEP, 0.0))
        else:
            explicit.append((0.5 * TIME_STEP, -0.5))
    return chebyshev, explicit


def pressure_terms(center, beside_all):
    masks = [center[2] * beside_all[direction][2] for direction in range(6)]
    perm_faces = [harmonic(center[1], beside_all[direction][1], masks[direction]) for direction in range(6)]
    mobility = []
    for direction in range(6):
        field_component = 5 + direction // 2
        if direction % 2 == 0:
            mobility.append(center[field_component] * masks[direction])
        else:
            mobility.append(beside_all[direction][field_component] * masks[direction])
    coefficient = [perm_faces[direction] * mobility[direction] for direction in range(6)]
    diagonal_entries = accumulate(coefficient) + STORAGE + center[4]
    forcing = center[3] + STORAGE * center[0]
    scaling = 1.0 / diagonal_entries
    outgoing = [perm_faces[direction] * (center[0] - beside_all[direction][0]) for direction in (0, 2, 4)]
    return coefficient, diagonal_entries, forcing, scaling, outgoing


def heat_terms(center, beside_all):
    masks = [center[2] * beside_all[direction][2] for direction in range(6)]
    conduct_faces = [harmonic(center[1], beside_all[direction][1], masks[direction]) for direction in range(6)]
    own_fluid = brine_flowability(center[0])
    fluid_faces = [harmonic(own_fluid, brine_flowability(beside_all[direction][0]), masks[direction]) for direction in range(6)]
    velocity = []
    for direction in range(6):
        field_component = 5 + direction // 2
        if direction % 2 == 0:
            velocity.append(center[field_component] * fluid_faces[direction])
        else:
            velocity.append(-beside_all[direction][field_component] * fluid_faces[direction])
    coefficient = [conduct_faces[direction] - jnp.minimum(velocity[direction], 0.0) for direction in range(6)]
    outflow = accumulate([jnp.maximum(velocity[direction], 0.0) for direction in range(6)])
    diagonal_entries = accumulate(conduct_faces) + outflow + center[4]
    forcing = center[3]
    scaling = jnp.ones_like(diagonal_entries)
    outgoing = [fluid_faces[direction] for direction in (0, 2, 4)]
    return coefficient, diagonal_entries, forcing, scaling, outgoing


def neighbours(values):
    widths = [(0, 0)] * (values.ndim - 3) + [(1, 1)] * 3
    padded = jnp.pad(values, widths)
    return [padded[..., 2:, 1:-1, 1:-1], padded[..., :-2, 1:-1, 1:-1],
            padded[..., 1:-1, 2:, 1:-1], padded[..., 1:-1, :-2, 1:-1],
            padded[..., 1:-1, 1:-1, 2:], padded[..., 1:-1, 1:-1, :-2]]


def group_step(group_id, states, coupled, facies, injectors, producers, lithology_lookup):
    grid_shape = (W, NX, W)
    own_field = states[group_id].reshape(grid_shape)
    own_classes = facies[group_id].reshape(grid_shape)
    property_field = accumulate([jnp.where(own_classes == index_c, lithology_lookup[index_c], 0.0) for index_c in range(NF)])
    inject_cells = injectors[group_id].reshape(grid_shape).astype(jnp.float32)
    produce_cells = producers[group_id].reshape(grid_shape).astype(jnp.float32)
    if group_id == 0:
        source = inject_cells * INJECTION + produce_cells * (PRODUCT_INDEX * WELL_PRESSURE)
        well_sink = produce_cells * PRODUCT_INDEX + inject_cells * 0.0
    else:
        source = inject_cells * (FLOW_RATE * CHILLED_INFLOW) + produce_cells * 0.0
        well_sink = produce_cells * FLOW_RATE + inject_cells * FLOW_RATE
    inside = jnp.ones_like(own_field)
    center = jnp.stack([own_field, property_field, inside, source, well_sink]
                       + [coupled[group_id, index_c].reshape(grid_shape) for index_c in range(3)])
    beside_all = neighbours(center)
    if group_id == 0:
        coefficient, diagonal_entries, forcing, scaling, outgoing = pressure_terms(center, beside_all)
    else:
        coefficient, diagonal_entries, forcing, scaling, outgoing = heat_terms(center, beside_all)
    chebyshev, explicit = sweep_weights()
    weights = chebyshev if group_id == 0 else explicit
    present_iterate = own_field
    previous = own_field
    for index_k in range(ITERS):
        around_v = neighbours(present_iterate)
        applied = diagonal_entries * present_iterate - accumulate([coefficient[direction] * around_v[direction] for direction in range(6)])
        residual = scaling * (forcing - applied)
        updated = present_iterate + weights[index_k][0] * residual + weights[index_k][1] * (present_iterate - previous)
        previous = present_iterate
        present_iterate = updated
    flipped = jnp.transpose(jnp.stack(outgoing[::-1]), (0, 3, 2, 1)).reshape(3, W, NX * W)
    return present_iterate.reshape(W, NX * W), flipped


def reference(states, coupled, facies, injectors, producers, perm_table, cond_table):
    press_new, press_send = group_step(0, states, coupled, facies, injectors, producers, perm_table)
    heat_new, heat_send = group_step(1, states, coupled, facies, injectors, producers, cond_table)
    stepped_states = jnp.stack([press_new, heat_new])
    new_coupled = jnp.stack([heat_send, press_send])
    return stepped_states, new_coupled
```

```python
import jax
import jax.numpy as jnp
from jax import lax
from jax.experimental import pallas as pl
from jax.experimental.pallas import tpu as pltpu
from jax.sharding import PartitionSpec as P

W = 64
NF = 6
ITERS = 4


STORAGE = 0.5
LOWER_BOUND = 0.05
INJECTION = 2.0
PRODUCT_INDEX = 1.0
WELL_PRESSURE = -1.0
FLOW_RATE = 1.0
CHILLED_INFLOW = 0.1
TIME_STEP = 0.05


def extended(block, sides, width):
    for axis, dim in sides:
        count = lax.axis_size(axis)
        forward = [(i, i + 1) for i in range(count - 1)]
        backward = [(target, source) for source, target in forward]
        low = lax.ppermute(
            lax.slice_in_dim(block, block.shape[dim] - width, None, axis=dim), axis, forward
        )
        high = lax.ppermute(lax.slice_in_dim(block, 0, width, axis=dim), axis, backward)
        block = jnp.concatenate([low, block, high], axis=dim)
    return block


def from_partner(value, axis, stride):
    mask = 2**stride
    pairs = [(source, source ^ mask) for source in range(lax.axis_size(axis))]
    return lax.ppermute(value, axis, pairs)


def brine_flowability(matrix_heat_level):
    return 0.2 + 0.8 * jax.nn.sigmoid(6.0 * (matrix_heat_level - 0.5))


def harmonic(left_val, eastern_neighbor_number, face_mask):
    return (
        face_mask
        * 2.0
        * left_val
        * eastern_neighbor_number
        / (left_val + eastern_neighbor_number + 1.0 - face_mask)
    )


def accumulate(terms):
    result = terms[0]
    for term in terms[1:]:
        result = result + term
    return result


def sweep_weights():
    centre_val = (2.0 + LOWER_BOUND) / 2.0
    half_width = (2.0 - LOWER_BOUND) / 2.0
    quotient_number = centre_val / half_width
    rho_old = 1.0 / quotient_number
    chebyshev = [(1.0 / centre_val, 0.0)]
    for index_k in range(1, ITERS):
        rho_new = 1.0 / (2.0 * quotient_number - rho_old)
        chebyshev.append((2.0 * rho_new / half_width, rho_new * rho_old))
        rho_old = rho_new
    explicit = []
    for index_k in range(ITERS):
        if index_k % 2 == 0:
            explicit.append((TIME_STEP, 0.0))
        else:
            explicit.append((0.5 * TIME_STEP, -0.5))
    return (chebyshev, explicit)


def pressure_terms(center, beside_all):
    masks = [center[2] * beside_all[direction][2] for direction in range(6)]
    perm_faces = [
        harmonic(center[1], beside_all[direction][1], masks[direction]) for direction in range(6)
    ]
    mobility = []
    for direction in range(6):
        field_component = 5 + direction // 2
        if direction % 2 == 0:
            mobility.append(center[field_component] * masks[direction])
        else:
            mobility.append(beside_all[direction][field_component] * masks[direction])
    coefficient = [perm_faces[direction] * mobility[direction] for direction in range(6)]
    diagonal_entries = accumulate(coefficient) + STORAGE + center[4]
    forcing = center[3] + STORAGE * center[0]
    scaling = 1.0 / diagonal_entries
    outgoing = [
        perm_faces[direction] * (center[0] - beside_all[direction][0]) for direction in (0, 2, 4)
    ]
    return (coefficient, diagonal_entries, forcing, scaling, outgoing)


def heat_terms(center, beside_all):
    masks = [center[2] * beside_all[direction][2] for direction in range(6)]
    conduct_faces = [
        harmonic(center[1], beside_all[direction][1], masks[direction]) for direction in range(6)
    ]
    own_fluid = brine_flowability(center[0])
    fluid_faces = [
        harmonic(own_fluid, brine_flowability(beside_all[direction][0]), masks[direction])
        for direction in range(6)
    ]
    velocity = []
    for direction in range(6):
        field_component = 5 + direction // 2
        if direction % 2 == 0:
            velocity.append(center[field_component] * fluid_faces[direction])
        else:
            velocity.append(-beside_all[direction][field_component] * fluid_faces[direction])
    coefficient = [
        conduct_faces[direction] - jnp.minimum(velocity[direction], 0.0) for direction in range(6)
    ]
    outflow = accumulate([jnp.maximum(velocity[direction], 0.0) for direction in range(6)])
    diagonal_entries = accumulate(conduct_faces) + outflow + center[4]
    forcing = center[3]
    scaling = jnp.ones_like(diagonal_entries)
    outgoing = [fluid_faces[direction] for direction in (0, 2, 4)]
    return (coefficient, diagonal_entries, forcing, scaling, outgoing)


def crop(values, margin):
    row_count = values.shape[-2]
    col_count = values.shape[-1]
    return values[..., margin : row_count - margin, margin * W : col_count - margin * W]


def beside(values):
    row_count = values.shape[-2]
    col_count = values.shape[-1]
    inner_cols = col_count - 2 * W
    column_pos = lax.broadcasted_iota(jnp.int32, (row_count - 2, inner_cols), 1) % W
    lower_mask = (column_pos > 0).astype(values.dtype)
    upper_mask = (column_pos < W - 1).astype(values.dtype)
    center = values[..., 1 : row_count - 1, W : col_count - W]
    beside_all = [
        values[..., 2:, W : col_count - W],
        values[..., : row_count - 2, W : col_count - W],
        values[..., 1 : row_count - 1, 2 * W :],
        values[..., 1 : row_count - 1, : col_count - 2 * W],
        values[..., 1 : row_count - 1, W + 1 : col_count - W + 1] * upper_mask,
        values[..., 1 : row_count - 1, W - 1 : col_count - W - 1] * lower_mask,
    ]
    return (beside_all, center)


def extend(values, margin):
    row_ext = extended(values, (("ba", 1),), margin)
    return extended(row_ext, (("aa", 2),), margin * W)


def regroup_layout(received_block):
    components = received_block.shape[0]
    turned = jnp.transpose(received_block, (0, 3, 2, 1))
    return turned.reshape(
        components, received_block.shape[3], received_block.shape[2] * received_block.shape[1]
    )


def body(states, coupled, facies, injectors, producers, perm_table, cond_table):
    is_press = lax.axis_index("code") == 0
    own_field = states[0]
    row_count = own_field.shape[0]
    col_count = own_field.shape[1]
    lithology_lookup = jnp.where(is_press, perm_table, cond_table)
    other_table = jnp.where(is_press, cond_table, perm_table)
    own_classes = facies[0]
    property_field = accumulate(
        [jnp.where(own_classes == index_c, lithology_lookup[index_c], 0.0) for index_c in range(NF)]
    )
    other_property = accumulate(
        [jnp.where(own_classes == index_c, other_table[index_c], 0.0) for index_c in range(NF)]
    )
    inject_cells = injectors[0].astype(jnp.float32)
    produce_cells = producers[0].astype(jnp.float32)
    source = inject_cells * jnp.where(
        is_press, INJECTION, FLOW_RATE * CHILLED_INFLOW
    ) + produce_cells * jnp.where(is_press, PRODUCT_INDEX * WELL_PRESSURE, 0.0)
    well_sink = produce_cells * jnp.where(
        is_press, PRODUCT_INDEX, FLOW_RATE
    ) + inject_cells * jnp.where(is_press, 0.0, FLOW_RATE)
    inside = jnp.ones_like(own_field)
    stacked = jnp.concatenate(
        [
            jnp.stack([own_field, property_field, inside, source, well_sink]),
            coupled[0],
            other_property[None],
        ],
        axis=0,
    )
    halo_depth = 1
    widened_stack = extend(stacked, halo_depth)
    beside_all, center = beside(widened_stack)
    coefficient, diagonal_entries, forcing, scaling, outgoing_list = lax.cond(
        is_press, pressure_terms, heat_terms, center, beside_all
    )
    outgoing = jnp.stack([crop(face_item, halo_depth - 1) for face_item in outgoing_list])
    payload = outgoing[::-1].reshape(3, row_count, col_count // W, W)
    regrouped = regroup_layout(
        lax.all_to_all(payload, "ba", split_axis=3, concat_axis=1, tiled=True)
    )
    received = from_partner(regrouped, "code", 0)
    chebyshev, explicit = sweep_weights()
    present_iterate = own_field
    previous = None
    prev_depth = 0
    counter = 0
    for sweep_block in range(ITERS // halo_depth):
        widened = extend(present_iterate[None], halo_depth)[0]
        if previous is None:
            previous = widened
            prev_depth = halo_depth
        region = halo_depth
        region = region - 1
        around_v, center_v = beside(widened)
        index_shift = halo_depth - 1 - region
        applied = crop(diagonal_entries, index_shift) * center_v - accumulate(
            [
                crop(coefficient[direction], index_shift) * around_v[direction]
                for direction in range(6)
            ]
        )
        residual = crop(scaling, index_shift) * (crop(forcing, index_shift) - applied)
        weight_new = jnp.where(is_press, chebyshev[counter][0], explicit[counter][0])
        weight_old = jnp.where(is_press, chebyshev[counter][1], explicit[counter][1])
        updated = (
            center_v
            + weight_new * residual
            + weight_old * (center_v - crop(previous, prev_depth - region))
        )
        previous = widened
        prev_depth = region + 1
        widened = updated
        counter = counter + 1
        present_iterate = widened
    return (present_iterate[None], received[None])


TINY = 1e-30
LANES = 128
HALF = 64
XH = 4
VM = pl.BlockSpec(memory_space=pltpu.VMEM)
SM = pl.BlockSpec(memory_space=pltpu.SMEM)
HB = pl.BlockSpec(memory_space=pltpu.HBM)
UNROLL = 4
LEAN = pltpu.CompilerParams(vmem_limit_bytes=6 * 2**20)


def params(megabytes):
    return pltpu.CompilerParams(vmem_limit_bytes=megabytes * 2**20)


def cost(micros):
    return pl.CostEstimate(flops=0, bytes_accessed=int(micros * 3.2e6), transcendentals=0)


def in_vmem(shape):
    return pltpu.VMEM(shape, jnp.float32)


def held(value):
    return pltpu.with_memory_space_constraint(value, pltpu.VMEM)


def lanes_at(tile, base=0):
    return pl.ds(pl.multiple_of(base + tile * LANES, LANES), LANES)


def lane_index(shape):
    return lax.broadcasted_iota(jnp.int32, shape, len(shape) - 1)


def inverse(value):
    return pl.reciprocal(value, approx=False)


def face_mean(left, right):
    return 2.0 * left * right * inverse(jnp.maximum(left + right, TINY))


def flowability(level):
    return 0.2 + 0.8 * inverse(1.0 + jnp.exp(-6.0 * (level - 0.5)))


def half_turn(value):
    return pltpu.roll(value, HALF, 1)


def next_lane(value):
    return pltpu.roll(value, LANES - 1, 1)


def prev_lane(value):
    return pltpu.roll(value, 1, 1)


def next_row(value):
    return pltpu.roll(value, value.shape[0] - 1, 0)


def prev_row(value):
    return pltpu.roll(value, 1, 0)


def class_table(table_ref, shape):
    lane = lane_index(shape)
    table = jnp.zeros(shape, jnp.float32)
    for index_c in range(NF):
        table = jnp.where(lane == index_c + 1, table_ref[index_c], table)
    return table


def look_up(table, codes):
    return jnp.take_along_axis(table, codes, axis=1)


def placed_pair(pair, is_low):
    blank = jnp.zeros((6, pair.shape[1]), pair.dtype)
    return jnp.where(
        is_low, jnp.concatenate([pair, blank], 0), jnp.concatenate([blank, pair], 0)
    )


def placed_row(row, is_low):
    blank = jnp.zeros((7, row.shape[1]), row.dtype)
    return jnp.where(is_low, jnp.concatenate([row, blank], 0), jnp.concatenate([blank, row], 0))


def edges_kernel(
    where_ref, st, cp, fa, ij, pr, to_right, to_left, across, across_right, across_left,
    left_f, right_f, row_f, left_i, right_i, row_i, sems,
):
    is_low = where_ref[1] == 0
    rows, cols = st.shape[1], st.shape[2]
    wide = XH * W
    first = pl.multiple_of(jnp.where(is_low, rows - 8, 0), 8)
    floats = [st.at[0]] + [cp.at[0, c] for c in range(3)]
    ints = [fa.at[0], ij.at[0], pr.at[0]]
    copies = []
    for group, (left, right, row) in (
        (floats, (left_f, right_f, row_f)),
        (ints, (left_i, right_i, row_i)),
    ):
        for index, field in enumerate(group):
            for source, target in (
                (field.at[pl.ds(first, 8), :], row.at[index]),
                (field.at[:, pl.ds(0, wide)], left.at[index]),
                (field.at[:, pl.ds(cols - wide, wide)], right.at[index]),
            ):
                copy = pltpu.make_async_copy(source, target, sems.at[len(copies)])
                copy.start()
                copies.append(copy)
    for copy in copies:
        copy.wait()
    for target, floats_ref, ints_ref in ((to_right, right_f, right_i), (to_left, left_f, left_i)):
        parts = [
            floats_ref[0],
            (ints_ref[0] + 1).astype(jnp.float32),
            floats_ref[1],
            floats_ref[2],
            floats_ref[3],
            ints_ref[1].astype(jnp.float32),
            ints_ref[2].astype(jnp.float32),
        ]
        for index, part in enumerate(parts):
            target[:, index * wide : (index + 1) * wide] = part

    def pair(value):
        return jnp.where(is_low, value[6:8], value[0:2])

    def near(value):
        return jnp.where(is_low, value[7:8], value[0:1])

    slots = [
        pair(row_f[0]),
        pair((row_i[0] + 1).astype(jnp.float32)),
        pair(row_f[1]),
        jnp.concatenate([near(row_f[2]), near(row_f[3])], 0),
        jnp.concatenate(
            [near(row_i[1].astype(jnp.float32)), near(row_i[2].astype(jnp.float32))], 0
        ),
    ]
    for index, slot in enumerate(slots):
        across[:, index * cols : (index + 1) * cols] = slot
        across_right[:, index * wide : (index + 1) * wide] = slot[:, cols - wide :]
        across_left[:, index * wide : (index + 1) * wide] = slot[:, :wide]


def turn_kernel(
    where_ref, st_in, cp_in, fa_in, ij_in, pr_in, st, cp, fa, ij, pr, own, other_a, other_b, sems
):
    copies = [
        pltpu.make_async_copy(source, target, sems.at[index])
        for index, (source, target) in enumerate(
            ((st_in, st), (cp_in, cp), (fa_in, fa), (ij_in, ij), (pr_in, pr))
        )
    ]
    for copy in copies:
        copy.start()
    copies[0].wait()
    is_heat = where_ref[0] == 1
    is_low = where_ref[1] == 0
    groups = st.shape[2] // (4 * LANES)
    half = groups // 2
    extra = groups * 2 * LANES
    row = lax.broadcasted_iota(jnp.int32, (32, LANES), 0)

    def step(group, rims):
        tall = jnp.concatenate(
            [st[0, :, lanes_at(4 * group + q)] for q in range(4)], axis=0
        )
        tall = jnp.where(is_heat, flowability(tall), tall)
        turned = tall.T
        for par in range(2):
            low = turned[par * HALF : par * HALF + 32]
            high = turned[par * HALF + 32 : par * HALF + 64]
            own[:, lanes_at(group, par * groups * LANES)] = jnp.where(is_low, low, high)
            away = jnp.where(is_low, high, low)
            rim = high[0:1]

            @pl.when(group < half)
            def _(away=away, par=par):
                other_a[:, lanes_at(group, par * half * LANES)] = away

            @pl.when(group >= half)
            def _(away=away, par=par):
                other_b[:, lanes_at(group - half, par * half * LANES)] = away

            rims = jnp.where(row == par * groups + group, rim, rims)
        return rims

    rims = lax.fori_loop(0, groups, step, jnp.zeros((32, LANES), jnp.float32), unroll=UNROLL)
    own[:, extra : extra + LANES] = jnp.where(is_low, rims, 0.0)
    other_b[:, half * 2 * LANES : half * 2 * LANES + LANES] = jnp.where(is_low, 0.0, rims)
    for copy in copies[1:]:
        copy.wait()


def plane_kernel(where_ref, from_right, own_in, other_in, *rest):
    own, other = rest[-2:]
    is_heat = where_ref[0] == 1
    is_low = where_ref[1] == 0
    wide = XH * W
    value = from_right[:, 0:LANES]
    inside = from_right[:, wide : wide + LANES] > 0.5
    value = jnp.where(is_heat, jnp.where(inside, flowability(value), 0.0), value)
    tall = jnp.concatenate([value, jnp.zeros((96, LANES), jnp.float32)], 0).T
    low, high = tall[0:32], tall[32:64]
    own[...] = own_in[...]
    other[...] = other_in[...]
    own[:, own.shape[1] - LANES :] = jnp.where(is_low, low, high)
    other[:, other.shape[1] - LANES :] = jnp.where(is_low, high, low)


def sweep(tiles, coeffs, force, diag, now, last, target, weight, pull):
    first, stop = tiles
    low_lanes = lane_index((now.shape[1], LANES)) < HALF

    def step(e, carry):
        before, here = carry
        value = now[e + 1]
        after = half_turn(now[e + 2])
        total = force[e + 1]
        total += coeffs[0, e + 1] * next_row(value)
        total += coeffs[1, e + 1] * prev_row(value)
        total += coeffs[2, e + 1] * jnp.where(low_lanes, here, after)
        total += coeffs[3, e + 1] * jnp.where(low_lanes, before, here)
        total += coeffs[4, e + 1] * next_lane(value)
        total += coeffs[5, e + 1] * prev_lane(value)
        if diag is None:
            result = (1.0 + pull - weight) * value + weight * total
        else:
            result = (1.0 + pull) * value + weight * (total - diag[e + 1] * value)
        if pull != 0.0:
            result -= pull * last[e + 1]
        target(e, result)
        return here, after

    lax.fori_loop(
        first, stop, step, (half_turn(now[first]), half_turn(now[first + 1])),
        unroll=UNROLL,
    )


def store_in(ref):
    def put(e, value):
        ref[e + 1] = value

    return put


def main_kernel(
    where_ref, perm_ref, cond_ref, st, cp, fa, ij, pr,
    from_left, from_right, across, corner_left, corner_right,
    v1, v2, coeffs, force, diag, faces, boundary,
    v0, prop, rock, c0, c1, c2, src, snk, fluid,
):
    is_press = where_ref[0] == 0
    is_low = where_ref[1] == 0
    cols = st.shape[2]
    tiles = cols // LANES
    ext = v0.shape[0] - 2
    height = v0.shape[1]
    wide = XH * W
    side = XH // 2
    own_at = pl.multiple_of(jnp.where(is_low, 0, 8), 8)
    rim_at = pl.multiple_of(jnp.where(is_low, 32, 0), 8)
    own_rows, rim_rows = pl.ds(own_at, 32), pl.ds(rim_at, 8)
    perm = class_table(perm_ref, (32, LANES))
    cond = class_table(cond_ref, (32, LANES))
    own_table = jnp.where(is_press, perm, cond)

    def put_cells(e, rows, state, codes, f0, f1, f2, inject, produce):
        count = state.shape[0]
        v0[e + 1, rows, :] = state
        prop[e + 1, rows, :] = look_up(own_table[:count], codes)
        rock[e + 1, rows, :] = look_up(perm[:count], codes)
        c0[e + 1, rows, :] = f0
        c1[e + 1, rows, :] = f1
        c2[e + 1, rows, :] = f2
        src[e + 1, rows, :] = jnp.where(is_press, 2.0 * inject - produce, 0.1 * inject)
        snk[e + 1, rows, :] = jnp.where(is_press, produce, produce + inject)

    def put_rim(e, message, slots, at):
        def pair(index):
            return placed_pair(message[:, lanes_at(at, index * slots)], is_low)

        def near(index, row):
            return placed_row(message[row : row + 1, lanes_at(at, index * slots)], is_low)

        put_cells(
            e, rim_rows, pair(0), pair(1).astype(jnp.int32), pair(2),
            near(3, 0), near(3, 1), near(4, 0), near(4, 1),
        )

    def put_side(e, message, at):
        parts = [message[:, lanes_at(at, index * wide)] for index in range(7)]
        put_cells(e, own_rows, parts[0], parts[1].astype(jnp.int32), *parts[2:])

    for ref in (v0, prop, rock):
        for e in (0, ext + 1):
            ref[e] = jnp.zeros((height, LANES), jnp.float32)
    for ref in (v1, v2):
        for e in (0, ext + 1):
            ref[e] = jnp.zeros((height, LANES), jnp.float32)

    def fill(t, carry):
        at = lanes_at(t)
        put_cells(
            t + side, own_rows, st[0, :, at], fa[0, :, at] + 1,
            cp[0, 0, :, at], cp[0, 1, :, at], cp[0, 2, :, at],
            ij[0, :, at].astype(jnp.float32), pr[0, :, at].astype(jnp.float32),
        )
        put_rim(t + side, across, cols, t)
        return carry

    lax.fori_loop(0, tiles, fill, 0, unroll=UNROLL)
    for at in range(side):
        put_side(at, from_left, at)
        put_rim(at, corner_left, wide, at)
        put_side(tiles + side + at, from_right, at)
        put_rim(tiles + side + at, corner_right, wide, at)

    lane = lane_index((height, LANES))
    low_lanes = lane < HALF
    not_last = lane % W != W - 1

    def next_cells(value, after):
        return (
            next_row(value),
            jnp.where(low_lanes, half_turn(value), half_turn(after)),
            jnp.where(not_last, next_lane(value), 0.0),
        )

    blank = jnp.zeros((height, LANES), jnp.float32)
    chebyshev, explicit = sweep_weights()

    @pl.when(is_press)
    def _():
        def step(e, before):
            value = prop[e + 1]
            means = [face_mean(value, other) for other in next_cells(value, prop[e + 2])]
            plus = [mean * ref[e + 1] for mean, ref in zip(means, (c0, c1, c2))]
            turned = half_turn(plus[1])
            minus = [
                prev_row(plus[0]),
                jnp.where(low_lanes, before, turned),
                prev_lane(plus[2]),
            ]
            total = accumulate(plus + minus) + STORAGE + snk[e + 1]
            scale = inverse(total)
            for dim in range(3):
                coeffs[2 * dim, e + 1] = scale * plus[dim]
                coeffs[2 * dim + 1, e + 1] = scale * minus[dim]
            force[e + 1] = scale * (src[e + 1] + STORAGE * v0[e + 1])
            return turned

        lax.fori_loop(0, ext, step, blank, unroll=UNROLL)
        (w0, u0), (w1, u1) = chebyshev[:2]
        sweep((0, ext), coeffs, force, None, v0, v0, store_in(v1), w0, u0)
        sweep((0, ext), coeffs, force, None, v1, v0, store_in(v2), w1, u1)

    @pl.when(jnp.logical_not(is_press))
    def _():
        fluid[0] = blank
        fluid[ext + 1] = blank

        def levels(e, carry):
            fluid[e + 1] = jnp.where(prop[e + 1] > 0.0, flowability(v0[e + 1]), 0.0)
            return carry

        lax.fori_loop(0, ext, levels, 0, unroll=UNROLL)

        def step(e, before):
            value = prop[e + 1]
            means = [face_mean(value, other) for other in next_cells(value, prop[e + 2])]
            value = fluid[e + 1]
            flows = [face_mean(value, other) for other in next_cells(value, fluid[e + 2])]
            value = rock[e + 1]
            for dim, other in enumerate(next_cells(value, rock[e + 2])):
                faces[dim, e + 1] = face_mean(value, other)
            speed = [flow * ref[e + 1] for flow, ref in zip(flows, (c0, c1, c2))]
            gain = [mean + jnp.maximum(rate, 0.0) for mean, rate in zip(means, speed)]
            loss = [up - rate for up, rate in zip(gain, speed)]
            turned = half_turn(gain[1]), half_turn(loss[1])
            minus = [
                prev_row(gain[0]),
                jnp.where(low_lanes, before[0], turned[0]),
                prev_lane(gain[2]),
            ]
            behind = [
                prev_row(loss[0]),
                jnp.where(low_lanes, before[1], turned[1]),
                prev_lane(loss[2]),
            ]
            diag[e + 1] = accumulate(gain + behind) + snk[e + 1]
            for dim in range(3):
                coeffs[2 * dim, e + 1] = loss[dim]
                coeffs[2 * dim + 1, e + 1] = minus[dim]
            force[e + 1] = src[e + 1]
            return turned

        lax.fori_loop(0, ext, step, (blank, blank), unroll=UNROLL)
        (w0, u0), (w1, u1) = explicit[:2]
        sweep((0, ext), coeffs, force, diag, v0, v0, store_in(v1), w0, u0)
        sweep((0, ext), coeffs, force, diag, v1, v0, store_in(v2), w1, u1)

    def send(e, carry):
        value = v2[e + 1]
        boundary[:, lanes_at(e)] = jnp.where(is_low, value[30:32], value[8:10])
        return carry

    lax.fori_loop(0, ext, send, 0, unroll=UNROLL)


def finish_kernel(where_ref, v1, v2, coeffs, force, diag, boundary, out, now, later):
    is_press = where_ref[0] == 0
    is_low = where_ref[1] == 0
    ext = v2.shape[0] - 2
    side = XH // 2
    rim_at = pl.multiple_of(jnp.where(is_low, 32, 0), 8)
    blank = jnp.zeros(v2.shape[1:], jnp.float32)
    for ref in (now, later):
        ref[0] = blank
        ref[ext + 1] = blank

    def fill(e, carry):
        now[e + 1] = v2[e + 1]
        now[e + 1, pl.ds(rim_at, 8), :] = placed_pair(boundary[:, lanes_at(e)], is_low)
        return carry

    lax.fori_loop(0, ext, fill, 0, unroll=UNROLL)
    chebyshev, explicit = sweep_weights()

    def put_out(e, value):
        out[0, :, lanes_at(e - side)] = jnp.where(is_low, value[0:32], value[8:40])

    for chosen, weights, centre in (
        (is_press, chebyshev, None),
        (jnp.logical_not(is_press), explicit, diag),
    ):

        @pl.when(chosen)
        def _(weights=weights, centre=centre):
            (w2, u2), (w3, u3) = weights[2:]
            sweep((0, ext), coeffs, force, centre, now, v1, store_in(later), w2, u2)
            sweep((side, ext - side), coeffs, force, centre, later, now, put_out, w3, u3)


def regrouped(pieces):
    lane = lane_index(pieces[0].shape)
    result = []
    for q in range(4):
        value = None
        for place in range(4):
            piece = pieces[place]
            if place != q:
                piece = pltpu.roll(piece, ((place - q) * 32) % LANES, 1)
            value = piece if value is None else jnp.where(lane >= place * 32, piece, value)
        result.append(value)
    return result


def faces_kernel(where_ref, own, other_a, other_b, faces, out, field, rim):
    is_press = where_ref[0] == 0
    is_low = where_ref[1] == 0
    tiles = out.shape[3] // LANES
    groups = tiles // 4
    half = groups // 2
    side = XH // 2
    extra = groups * 2 * LANES
    extra_other = half * 2 * LANES
    own_at = pl.multiple_of(jnp.where(is_low, 0, 8), 8)

    def ordered(mine, theirs):
        return [jnp.where(is_low, mine, theirs), jnp.where(is_low, theirs, mine)]

    pieces = []
    for par in range(2):
        pieces += ordered(
            own[par * groups : (par + 1) * groups, extra : extra + LANES],
            other_b[par * groups : (par + 1) * groups, extra_other : extra_other + LANES],
        )
    for q, value in enumerate(regrouped(pieces)):
        rim[q] = value
    plane = ordered(own[:, extra + LANES :], other_b[:, extra_other + LANES :])
    lane = lane_index((32, LANES))
    field[tiles, 0:32, :] = jnp.where(lane < 32, plane[0], pltpu.roll(plane[1], 32, 1))

    def gather(other, first):
        def step(group, carry):
            pieces = []
            for par in range(2):
                pieces += ordered(
                    own[:, lanes_at(group + first, par * groups * LANES)],
                    other[:, lanes_at(group, par * half * LANES)],
                )
            for q, value in enumerate(regrouped(pieces)):
                field[4 * (group + first) + q, 0:32, :] = value
                field[4 * (group + first) + q, 32:33, :] = rim[q, pl.ds(group + first, 1), :]
            return carry

        lax.fori_loop(0, half, step, 0, unroll=UNROLL)

    gather(other_a, 0)
    gather(other_b, half)
    low_lanes = lane < HALF
    not_last = lane % W != W - 1

    def around(t):
        value = field[t]
        here = value[0:32]
        after = field[t + 1, 0:32, :]
        return here, (
            next_row(value)[0:32],
            jnp.where(low_lanes, half_turn(here), half_turn(after)),
            next_lane(here),
        )

    @pl.when(is_press)
    def _():
        def step(t, carry):
            here, others = around(t)
            others = (others[0], others[1], jnp.where(not_last, others[2], 0.0))
            for dim in range(3):
                out[0, dim, :, lanes_at(t)] = face_mean(here, others[dim])
            return carry

        lax.fori_loop(0, tiles, step, 0, unroll=UNROLL)

    @pl.when(jnp.logical_not(is_press))
    def _():
        def step(t, carry):
            here, others = around(t)
            for dim in range(3):
                mean = faces[dim, t + side + 1, pl.ds(own_at, 32), :]
                out[0, dim, :, lanes_at(t)] = mean * (here - others[dim])
            return carry

        lax.fori_loop(0, tiles, step, 0, unroll=UNROLL)


def paired_body(states, coupled, facies, injectors, producers, perm_table, cond_table):
    rows, cols = states.shape[1], states.shape[2]
    tiles = cols // LANES
    ext = tiles + XH
    wide = XH * W
    groups = tiles // 4
    place = jnp.stack([lax.axis_index("code"), lax.axis_index("ba")]).astype(jnp.int32)
    count = lax.axis_size("aa")
    up = [(i, i + 1) for i in range(count - 1)]
    down = [(b, a) for a, b in up]
    swap = [(0, 1), (1, 0)]
    up_across = [(2 * a + c, 2 * b + 1 - c) for a, b in up for c in range(2)]
    down_across = [(b, a) for a, b in up_across]
    opposite = [(0, 3), (1, 2), (2, 1), (3, 0)]
    f32, i32 = jnp.float32, jnp.int32
    states, coupled, facies, injectors, producers = [
        pltpu.with_memory_space_constraint(value, pltpu.HBM)
        for value in (states, coupled, facies, injectors, producers)
    ]

    to_right, to_left, across, across_right, across_left = pl.pallas_call(
        edges_kernel,
        out_shape=[
            in_vmem((rows, 7 * wide)),
            in_vmem((rows, 7 * wide)),
            in_vmem((2, 5 * cols)),
            in_vmem((2, 5 * wide)),
            in_vmem((2, 5 * wide)),
        ],
        in_specs=[SM] + [HB] * 5,
        out_specs=[VM] * 5,
        scratch_shapes=[
            pltpu.VMEM((4, rows, wide), f32),
            pltpu.VMEM((4, rows, wide), f32),
            pltpu.VMEM((4, 8, cols), f32),
            pltpu.VMEM((3, rows, wide), i32),
            pltpu.VMEM((3, rows, wide), i32),
            pltpu.VMEM((3, 8, cols), i32),
            pltpu.SemaphoreType.DMA((21,)),
        ],
        compiler_params=LEAN,
        cost_estimate=cost(1),
        name="edges",
    )(place, states, coupled, facies, injectors, producers)
    from_left = held(lax.ppermute(to_right, "aa", up))
    from_right = held(lax.ppermute(to_left, "aa", down))
    from_across = held(lax.ppermute(across, "ba", swap))
    corner_left = held(lax.ppermute(across_right, ("aa", "ba"), up_across))
    corner_right = held(lax.ppermute(across_left, ("aa", "ba"), down_across))

    st, cp, fa, ij, pr, turned_own, turned_a, turned_b = pl.pallas_call(
        turn_kernel,
        out_shape=[
            in_vmem(states.shape),
            in_vmem(coupled.shape),
            pltpu.VMEM(facies.shape, i32),
            pltpu.VMEM(facies.shape, i32),
            pltpu.VMEM(facies.shape, i32),
            in_vmem((32, (2 * groups + 2) * LANES)),
            in_vmem((32, groups * LANES)),
            in_vmem((32, (groups + 2) * LANES)),
        ],
        in_specs=[SM] + [HB] * 5,
        out_specs=[VM] * 8,
        scratch_shapes=[pltpu.SemaphoreType.DMA((5,))],
        compiler_params=LEAN,
        cost_estimate=cost(3),
        name="turn",
    )(place, states, coupled, facies, injectors, producers)
    other_a = held(lax.ppermute(turned_a, ("code", "ba"), opposite))
    turned_own, turned_b = pl.pallas_call(
        plane_kernel,
        out_shape=[in_vmem(turned_own.shape), in_vmem(turned_b.shape)],
        in_specs=[SM] + [VM] * 7,
        out_specs=[VM] * 2,
        compiler_params=LEAN,
        cost_estimate=cost(1),
        name="plane",
    )(
        place, from_right, turned_own, turned_b, from_left, from_across, corner_left, corner_right
    )
    other_b = held(lax.ppermute(turned_b, ("code", "ba"), opposite))
    own = held(lax.ppermute(turned_own, "code", swap))

    field = (ext + 2, rows + 8, LANES)
    v1, v2, coeffs, force, diag, faces, boundary = pl.pallas_call(
        main_kernel,
        out_shape=[
            in_vmem(field),
            in_vmem(field),
            in_vmem((6,) + field),
            in_vmem(field),
            in_vmem(field),
            in_vmem((3,) + field),
            in_vmem((2, ext * LANES)),
        ],
        in_specs=[SM, SM, SM] + [VM] * 10,
        out_specs=[VM] * 7,
        scratch_shapes=[pltpu.VMEM(field, f32)] * 9,
        compiler_params=params(18),
        cost_estimate=cost(12),
        name="main",
    )(
        place, perm_table, cond_table, st, cp, fa, ij, pr,
        from_left, from_right, from_across, corner_left, corner_right,
    )
    boundary = held(lax.ppermute(boundary, "ba", swap))
    stepped = pl.pallas_call(
        finish_kernel,
        out_shape=jax.ShapeDtypeStruct(states.shape, f32),
        in_specs=[SM] + [VM] * 6,
        out_specs=VM,
        scratch_shapes=[pltpu.VMEM(field, f32)] * 2,
        compiler_params=params(8),
        cost_estimate=cost(6),
        name="finish",
    )(place, v1, v2, coeffs, force, diag, boundary)
    received = pl.pallas_call(
        faces_kernel,
        out_shape=jax.ShapeDtypeStruct(coupled.shape, f32),
        in_specs=[SM] + [VM] * 4,
        out_specs=VM,
        scratch_shapes=[
            pltpu.VMEM((tiles + 1, rows + 8, LANES), f32),
            pltpu.VMEM((4, groups, LANES), f32),
        ],
        compiler_params=params(8),
        cost_estimate=cost(5),
        name="faces",
    )(place, own, other_a, other_b, faces)
    return (stepped, received)


def solution(mesh):
    paired = mesh.shape["ba"] == 2 and mesh.shape["code"] == 2
    return jax.shard_map(
        paired_body if paired else body,
        mesh=mesh,
        in_specs=(
            P("code", "ba", "aa"),
            P("code", None, "ba", "aa"),
            P("code", "ba", "aa"),
            P("code", "ba", "aa"),
            P("code", "ba", "aa"),
            P(),
            P(),
        ),
        out_specs=(P("code", "ba", "aa"), P("code", None, "ba", "aa")),
        check_vma=False,
    )
```

```python
import jax
import jax.numpy as jnp
from jax import lax
from jax.experimental import pallas as pl
from jax.experimental.pallas import tpu as pltpu
from jax.sharding import PartitionSpec as P

W = 64
NF = 6
ITERS = 4


STORAGE = 0.5
LOWER_BOUND = 0.05
INJECTION = 2.0
PRODUCT_INDEX = 1.0
WELL_PRESSURE = -1.0
FLOW_RATE = 1.0
CHILLED_INFLOW = 0.1
TIME_STEP = 0.05


def extended(block, sides, width):
    for axis, dim in sides:
        count = lax.axis_size(axis)
        forward = [(i, i + 1) for i in range(count - 1)]
        backward = [(target, source) for source, target in forward]
        low = lax.ppermute(
            lax.slice_in_dim(block, block.shape[dim] - width, None, axis=dim), axis, forward
        )
        high = lax.ppermute(lax.slice_in_dim(block, 0, width, axis=dim), axis, backward)
        block = jnp.concatenate([low, block, high], axis=dim)
    return block


def from_partner(value, axis, stride):
    mask = 2**stride
    pairs = [(source, source ^ mask) for source in range(lax.axis_size(axis))]
    return lax.ppermute(value, axis, pairs)


def brine_flowability(matrix_heat_level):
    return 0.2 + 0.8 * jax.nn.sigmoid(6.0 * (matrix_heat_level - 0.5))


def harmonic(left_val, eastern_neighbor_number, face_mask):
    return (
        face_mask
        * 2.0
        * left_val
        * eastern_neighbor_number
        / (left_val + eastern_neighbor_number + 1.0 - face_mask)
    )


def accumulate(terms):
    result = terms[0]
    for term in terms[1:]:
        result = result + term
    return result


def sweep_weights():
    centre_val = (2.0 + LOWER_BOUND) / 2.0
    half_width = (2.0 - LOWER_BOUND) / 2.0
    quotient_number = centre_val / half_width
    rho_old = 1.0 / quotient_number
    chebyshev = [(1.0 / centre_val, 0.0)]
    for index_k in range(1, ITERS):
        rho_new = 1.0 / (2.0 * quotient_number - rho_old)
        chebyshev.append((2.0 * rho_new / half_width, rho_new * rho_old))
        rho_old = rho_new
    explicit = []
    for index_k in range(ITERS):
        if index_k % 2 == 0:
            explicit.append((TIME_STEP, 0.0))
        else:
            explicit.append((0.5 * TIME_STEP, -0.5))
    return (chebyshev, explicit)


def pressure_terms(center, beside_all):
    masks = [center[2] * beside_all[direction][2] for direction in range(6)]
    perm_faces = [
        harmonic(center[1], beside_all[direction][1], masks[direction]) for direction in range(6)
    ]
    mobility = []
    for direction in range(6):
        field_component = 5 + direction // 2
        if direction % 2 == 0:
            mobility.append(center[field_component] * masks[direction])
        else:
            mobility.append(beside_all[direction][field_component] * masks[direction])
    coefficient = [perm_faces[direction] * mobility[direction] for direction in range(6)]
    diagonal_entries = accumulate(coefficient) + STORAGE + center[4]
    forcing = center[3] + STORAGE * center[0]
    scaling = 1.0 / diagonal_entries
    outgoing = [
        perm_faces[direction] * (center[0] - beside_all[direction][0]) for direction in (0, 2, 4)
    ]
    return (coefficient, diagonal_entries, forcing, scaling, outgoing)


def heat_terms(center, beside_all):
    masks = [center[2] * beside_all[direction][2] for direction in range(6)]
    conduct_faces = [
        harmonic(center[1], beside_all[direction][1], masks[direction]) for direction in range(6)
    ]
    own_fluid = brine_flowability(center[0])
    fluid_faces = [
        harmonic(own_fluid, brine_flowability(beside_all[direction][0]), masks[direction])
        for direction in range(6)
    ]
    velocity = []
    for direction in range(6):
        field_component = 5 + direction // 2
        if direction % 2 == 0:
            velocity.append(center[field_component] * fluid_faces[direction])
        else:
            velocity.append(-beside_all[direction][field_component] * fluid_faces[direction])
    coefficient = [
        conduct_faces[direction] - jnp.minimum(velocity[direction], 0.0) for direction in range(6)
    ]
    outflow = accumulate([jnp.maximum(velocity[direction], 0.0) for direction in range(6)])
    diagonal_entries = accumulate(conduct_faces) + outflow + center[4]
    forcing = center[3]
    scaling = jnp.ones_like(diagonal_entries)
    outgoing = [fluid_faces[direction] for direction in (0, 2, 4)]
    return (coefficient, diagonal_entries, forcing, scaling, outgoing)


def crop(values, margin):
    row_count = values.shape[-2]
    col_count = values.shape[-1]
    return values[..., margin : row_count - margin, margin * W : col_count - margin * W]


def beside(values):
    row_count = values.shape[-2]
    col_count = values.shape[-1]
    inner_cols = col_count - 2 * W
    column_pos = lax.broadcasted_iota(jnp.int32, (row_count - 2, inner_cols), 1) % W
    lower_mask = (column_pos > 0).astype(values.dtype)
    upper_mask = (column_pos < W - 1).astype(values.dtype)
    center = values[..., 1 : row_count - 1, W : col_count - W]
    beside_all = [
        values[..., 2:, W : col_count - W],
        values[..., : row_count - 2, W : col_count - W],
        values[..., 1 : row_count - 1, 2 * W :],
        values[..., 1 : row_count - 1, : col_count - 2 * W],
        values[..., 1 : row_count - 1, W + 1 : col_count - W + 1] * upper_mask,
        values[..., 1 : row_count - 1, W - 1 : col_count - W - 1] * lower_mask,
    ]
    return (beside_all, center)


def extend(values, margin):
    row_ext = extended(values, (("ba", 1),), margin)
    return extended(row_ext, (("aa", 2),), margin * W)


def regroup_layout(received_block):
    components = received_block.shape[0]
    turned = jnp.transpose(received_block, (0, 3, 2, 1))
    return turned.reshape(
        components, received_block.shape[3], received_block.shape[2] * received_block.shape[1]
    )


def body(states, coupled, facies, injectors, producers, perm_table, cond_table):
    is_press = lax.axis_index("code") == 0
    own_field = states[0]
    row_count = own_field.shape[0]
    col_count = own_field.shape[1]
    lithology_lookup = jnp.where(is_press, perm_table, cond_table)
    other_table = jnp.where(is_press, cond_table, perm_table)
    own_classes = facies[0]
    property_field = accumulate(
        [jnp.where(own_classes == index_c, lithology_lookup[index_c], 0.0) for index_c in range(NF)]
    )
    other_property = accumulate(
        [jnp.where(own_classes == index_c, other_table[index_c], 0.0) for index_c in range(NF)]
    )
    inject_cells = injectors[0].astype(jnp.float32)
    produce_cells = producers[0].astype(jnp.float32)
    source = inject_cells * jnp.where(
        is_press, INJECTION, FLOW_RATE * CHILLED_INFLOW
    ) + produce_cells * jnp.where(is_press, PRODUCT_INDEX * WELL_PRESSURE, 0.0)
    well_sink = produce_cells * jnp.where(
        is_press, PRODUCT_INDEX, FLOW_RATE
    ) + inject_cells * jnp.where(is_press, 0.0, FLOW_RATE)
    inside = jnp.ones_like(own_field)
    stacked = jnp.concatenate(
        [
            jnp.stack([own_field, property_field, inside, source, well_sink]),
            coupled[0],
            other_property[None],
        ],
        axis=0,
    )
    halo_depth = 1
    widened_stack = extend(stacked, halo_depth)
    beside_all, center = beside(widened_stack)
    coefficient, diagonal_entries, forcing, scaling, outgoing_list = lax.cond(
        is_press, pressure_terms, heat_terms, center, beside_all
    )
    outgoing = jnp.stack([crop(face_item, halo_depth - 1) for face_item in outgoing_list])
    payload = outgoing[::-1].reshape(3, row_count, col_count // W, W)
    regrouped = regroup_layout(
        lax.all_to_all(payload, "ba", split_axis=3, concat_axis=1, tiled=True)
    )
    received = from_partner(regrouped, "code", 0)
    chebyshev, explicit = sweep_weights()
    present_iterate = own_field
    previous = None
    prev_depth = 0
    counter = 0
    for sweep_block in range(ITERS // halo_depth):
        widened = extend(present_iterate[None], halo_depth)[0]
        if previous is None:
            previous = widened
            prev_depth = halo_depth
        region = halo_depth
        region = region - 1
        around_v, center_v = beside(widened)
        index_shift = halo_depth - 1 - region
        applied = crop(diagonal_entries, index_shift) * center_v - accumulate(
            [
                crop(coefficient[direction], index_shift) * around_v[direction]
                for direction in range(6)
            ]
        )
        residual = crop(scaling, index_shift) * (crop(forcing, index_shift) - applied)
        weight_new = jnp.where(is_press, chebyshev[counter][0], explicit[counter][0])
        weight_old = jnp.where(is_press, chebyshev[counter][1], explicit[counter][1])
        updated = (
            center_v
            + weight_new * residual
            + weight_old * (center_v - crop(previous, prev_depth - region))
        )
        previous = widened
        prev_depth = region + 1
        widened = updated
        counter = counter + 1
        present_iterate = widened
    return (present_iterate[None], received[None])


TINY = 1e-30
LANES = 128
HALF = 64
XH = 4
VM = pl.BlockSpec(memory_space=pltpu.VMEM)
SM = pl.BlockSpec(memory_space=pltpu.SMEM)
HB = pl.BlockSpec(memory_space=pltpu.HBM)
UNROLL = 4
PARTS = 4
LEAN = pltpu.CompilerParams(vmem_limit_bytes=6 * 2**20)


def params(megabytes):
    return pltpu.CompilerParams(vmem_limit_bytes=megabytes * 2**20)


def cost(micros):
    return pl.CostEstimate(flops=0, bytes_accessed=int(micros * 3.2e6), transcendentals=0)


def in_vmem(shape):
    return pltpu.VMEM(shape, jnp.float32)


def held(value):
    return pltpu.with_memory_space_constraint(value, pltpu.VMEM)


def lanes_at(tile, base=0):
    return pl.ds(pl.multiple_of(base + tile * LANES, LANES), LANES)


def lane_index(shape):
    return lax.broadcasted_iota(jnp.int32, shape, len(shape) - 1)


def inverse(value):
    return pl.reciprocal(value, approx=False)


def face_mean(left, right):
    return 2.0 * left * right * inverse(jnp.maximum(left + right, TINY))


def flowability(level):
    return 0.2 + 0.8 * inverse(1.0 + jnp.exp(-6.0 * (level - 0.5)))


def half_turn(value):
    return pltpu.roll(value, HALF, 1)


def next_lane(value):
    return pltpu.roll(value, LANES - 1, 1)


def prev_lane(value):
    return pltpu.roll(value, 1, 1)


def next_row(value):
    return pltpu.roll(value, value.shape[0] - 1, 0)


def prev_row(value):
    return pltpu.roll(value, 1, 0)


def look_up(table, codes):
    value = jnp.zeros(codes.shape, jnp.float32)
    for index_c in range(NF):
        value = jnp.where(codes == index_c + 1, table[index_c], value)
    return value


def placed_pair(pair, is_low):
    blank = jnp.zeros((6, pair.shape[1]), pair.dtype)
    return jnp.where(
        is_low, jnp.concatenate([pair, blank], 0), jnp.concatenate([blank, pair], 0)
    )


def placed_row(row, is_low):
    blank = jnp.zeros((7, row.shape[1]), row.dtype)
    return jnp.where(is_low, jnp.concatenate([row, blank], 0), jnp.concatenate([blank, row], 0))


def edges_kernel(
    where_ref, st, cp, fa, ij, pr, to_right, to_left, across, corners,
    left_f, right_f, row_f, left_i, right_i, row_i, sems,
):
    is_low = where_ref[1] == 0
    rows, cols = st.shape[1], st.shape[2]
    wide = XH * W
    first = pl.multiple_of(jnp.where(is_low, rows - 8, 0), 8)
    floats = [st.at[0]] + [cp.at[0, c] for c in range(3)]
    ints = [fa.at[0], ij.at[0], pr.at[0]]
    copies = []
    for group, (left, right, row) in (
        (floats, (left_f, right_f, row_f)),
        (ints, (left_i, right_i, row_i)),
    ):
        for index, field in enumerate(group):
            for source, target in (
                (field.at[pl.ds(first, 8), :], row.at[index]),
                (field.at[:, pl.ds(0, wide)], left.at[index]),
                (field.at[:, pl.ds(cols - wide, wide)], right.at[index]),
            ):
                copy = pltpu.make_async_copy(source, target, sems.at[len(copies)])
                copy.start()
                copies.append(copy)
    for copy in copies:
        copy.wait()
    for target, floats_ref, ints_ref in ((to_right, right_f, right_i), (to_left, left_f, left_i)):
        parts = [
            floats_ref[0],
            (ints_ref[0] + 1).astype(jnp.float32),
            floats_ref[1],
            floats_ref[2],
            floats_ref[3],
            ints_ref[1].astype(jnp.float32),
            ints_ref[2].astype(jnp.float32),
        ]
        for index, part in enumerate(parts):
            target[:, index * wide : (index + 1) * wide] = part

    def pair(value):
        return jnp.where(is_low, value[6:8], value[0:2])

    def near(value):
        return jnp.where(is_low, value[7:8], value[0:1])

    slots = [
        pair(row_f[0]),
        pair((row_i[0] + 1).astype(jnp.float32)),
        pair(row_f[1]),
        jnp.concatenate([near(row_f[2]), near(row_f[3])], 0),
        jnp.concatenate(
            [near(row_i[1].astype(jnp.float32)), near(row_i[2].astype(jnp.float32))], 0
        ),
    ]
    for index, slot in enumerate(slots):
        across[:, index * cols : (index + 1) * cols] = slot
        corners[:, 2 * index * wide : (2 * index + 1) * wide] = slot[:, :wide]
        corners[:, (2 * index + 1) * wide : (2 * index + 2) * wide] = slot[:, cols - wide :]


def pack_kernel(right_in, left_in, across_in, corners, to_right, to_left, across):
    across[...] = across_in[...]
    wide = XH * W
    for side, (source, target) in enumerate(((left_in, to_left), (right_in, to_right))):
        target[:, : 7 * wide] = source[...]
        target[:, 7 * wide :] = jnp.zeros((32, LANES), jnp.float32)
        for index in range(5):
            for row in range(2):
                for half in range(2):
                    start = (2 * index + side) * wide + half * LANES
                    place = index * 4 + row * 2 + half
                    target[place : place + 1, 7 * wide :] = corners[
                        row : row + 1, start : start + LANES
                    ]


def put_cells(refs, is_press, tables, e, rows, cells):
    v0, prop, rock, c0, c1, c2, src, snk = refs
    state, codes, f0, f1, f2, inject, produce = cells
    v0[e + 1, rows, :] = state
    prop[e + 1, rows, :] = look_up(tables[0], codes)
    rock[e + 1, rows, :] = look_up(tables[1], codes)
    c0[e + 1, rows, :] = f0
    c1[e + 1, rows, :] = f1
    c2[e + 1, rows, :] = f2
    src[e + 1, rows, :] = jnp.where(is_press, 2.0 * inject - produce, 0.1 * inject)
    snk[e + 1, rows, :] = jnp.where(is_press, produce, produce + inject)


def class_tables(is_press, perm_ref, cond_ref):
    perm = [perm_ref[index_c] for index_c in range(NF)]
    own = [jnp.where(is_press, perm[index_c], cond_ref[index_c]) for index_c in range(NF)]
    return own, perm


def turn_kernel(
    where_ref, perm_ref, cond_ref, st_in, cp_in, fa_in, ij_in, pr_in, corners,
    own, other, fluid, v0, prop, rock, c0, c1, c2, src, snk,
    st, cp, fa, ij, pr, sems,
):
    del corners
    copies = [
        pltpu.make_async_copy(source, target, sems.at[index])
        for index, (source, target) in enumerate(
            ((st_in, st), (cp_in, cp), (fa_in, fa), (ij_in, ij), (pr_in, pr))
        )
    ]
    for copy in copies:
        copy.start()
    copies[0].wait()
    is_heat = where_ref[0] == 1
    is_low = where_ref[1] == 0
    own_rows = pl.ds(pl.multiple_of(jnp.where(is_low, 0, 8), 8), 32)
    groups = st.shape[2] // (4 * LANES)
    extra = groups * 2 * LANES
    row = lax.broadcasted_iota(jnp.int32, (32, LANES), 0)

    def step(group, rims):
        tall = jnp.concatenate(
            [st[0, :, lanes_at(4 * group + q)] for q in range(4)], axis=0
        )
        tall = jnp.where(is_heat, flowability(tall), tall)
        for q in range(4):
            fluid[4 * group + q + XH // 2 + 1, own_rows, :] = tall[32 * q : 32 * q + 32]
        turned = tall.T
        for par in range(2):
            low = turned[par * HALF : par * HALF + 32]
            high = turned[par * HALF + 32 : par * HALF + 64]
            own[:, lanes_at(group, par * groups * LANES)] = jnp.where(is_low, low, high)
            away = jnp.where(is_low, high, low)
            rim = high[0:1]

            other[:, lanes_at(group, par * groups * LANES)] = away
            rims = jnp.where(row == par * groups + group, rim, rims)
        return rims

    rims = lax.fori_loop(0, groups, step, jnp.zeros((32, LANES), jnp.float32), unroll=8)
    own[:, extra : extra + LANES] = jnp.where(is_low, rims, 0.0)
    other[:, extra : extra + LANES] = jnp.where(is_low, 0.0, rims)
    for copy in copies[1:]:
        copy.wait()
    refs = (v0, prop, rock, c0, c1, c2, src, snk)
    is_press = where_ref[0] == 0
    tables = class_tables(is_press, perm_ref, cond_ref)
    tiles = st.shape[2] // LANES

    def fill(t, carry):
        at = lanes_at(t)
        cells = (
            st[0, :, at], fa[0, :, at] + 1, cp[0, 0, :, at], cp[0, 1, :, at], cp[0, 2, :, at],
            ij[0, :, at].astype(jnp.float32), pr[0, :, at].astype(jnp.float32),
        )
        put_cells(refs, is_press, tables, t + XH // 2, own_rows, cells)
        return carry

    lax.fori_loop(0, tiles, fill, 0, unroll=8)


def plane_kernel(where_ref, from_right, own_in, *rest):
    own, other = rest[-2:]
    is_heat = where_ref[0] == 1
    is_low = where_ref[1] == 0
    wide = XH * W
    value = from_right[:, 0:LANES]
    inside = from_right[:, wide : wide + LANES] > 0.5
    value = jnp.where(is_heat, jnp.where(inside, flowability(value), 0.0), value)
    tall = jnp.concatenate([value, jnp.zeros((96, LANES), jnp.float32)], 0).T
    low, high = tall[0:32], tall[32:64]
    own[...] = own_in[...]
    own[:, own.shape[1] - LANES :] = jnp.where(is_low, low, high)
    other[...] = jnp.zeros(other.shape, jnp.float32)
    other[:, :LANES] = jnp.where(is_low, high, low)


def sweep(tiles, coeffs, force, diag, now, last, target, weight, pull):
    first, stop = tiles
    low_lanes = lane_index((now.shape[1], LANES)) < HALF

    def step(e, carry):
        before, here = carry
        value = now[e + 1]
        after = half_turn(now[e + 2])
        total = force[e + 1]
        total += coeffs[0, e + 1] * next_row(value)
        total += coeffs[1, e + 1] * prev_row(value)
        total += coeffs[2, e + 1] * jnp.where(low_lanes, here, after)
        total += coeffs[3, e + 1] * jnp.where(low_lanes, before, here)
        total += coeffs[4, e + 1] * next_lane(value)
        total += coeffs[5, e + 1] * prev_lane(value)
        if diag is None:
            result = (1.0 + pull - weight) * value + weight * total
        else:
            result = (1.0 + pull) * value + weight * (total - diag[e + 1] * value)
        if pull != 0.0:
            result -= pull * last[e + 1]
        target(e, result)
        return here, after

    lax.fori_loop(
        first, stop, step, (half_turn(now[first]), half_turn(now[first + 1])),
        unroll=(stop - first) // 2,
    )


def store_in(ref):
    def put(e, value):
        ref[e + 1] = value

    return put


def rim_cells(is_low, read):
    def pair(index):
        return placed_pair(jnp.concatenate([read(index, 0), read(index, 1)], 0), is_low)

    def near(index, row):
        return placed_row(read(index, row), is_low)

    return (
        pair(0), pair(1).astype(jnp.int32), pair(2),
        near(3, 0), near(3, 1), near(4, 0), near(4, 1),
    )


def rim_rows(is_low):
    return pl.ds(pl.multiple_of(jnp.where(is_low, 32, 0), 8), 8)


def put_level(fluid, cells, e, rows):
    prop, state = cells[1][e + 1, rows, :], cells[0][e + 1, rows, :]
    fluid[e + 1, rows, :] = jnp.where(prop > 0.0, flowability(state), 0.0)


def clear(refs, places):
    for ref in refs:
        for e in places:
            ref[e] = jnp.zeros(ref.shape[1:], jnp.float32)


def face_terms(cells, made, is_press, ranges, long):
    v0, prop, rock, c0, c1, c2, src, snk = cells
    coeffs, force, diag, fluid = made
    shape = v0.shape[1:]
    lane = lane_index(shape)
    low_lanes = lane < HALF
    not_last = lane % W != W - 1
    blank = jnp.zeros(shape, jnp.float32)

    def next_cells(value, here, after):
        return (
            next_row(value),
            jnp.where(low_lanes, here, after),
            jnp.where(not_last, next_lane(value), 0.0),
        )

    def run(step, first, stop, start):
        if stop - first > 8:
            lax.fori_loop(first, stop, step, start(first), unroll=long)
        else:
            carry = start(first)
            for e in range(first, stop):
                carry = step(e, carry)

    @pl.when(is_press)
    def _():
        def plus_along(e, here, after):
            value = prop[e + 1]
            return face_mean(value, jnp.where(low_lanes, here, after)) * c1[e + 1]

        def start(first):
            here = half_turn(prop[first + 1])
            if first == 0:
                return blank, here
            return half_turn(plus_along(first - 1, half_turn(prop[first]), here)), here

        def step(e, carry):
            before, here = carry
            value, after = prop[e + 1], half_turn(prop[e + 2])
            means = [face_mean(value, other) for other in next_cells(value, here, after)]
            plus = [mean * ref[e + 1] for mean, ref in zip(means, (c0, c1, c2))]
            turned = half_turn(plus[1])
            minus = [
                prev_row(plus[0]),
                jnp.where(low_lanes, before, turned),
                prev_lane(plus[2]),
            ]
            total = accumulate(plus + minus) + STORAGE + snk[e + 1]
            scale = inverse(total)
            for dim in range(3):
                coeffs[2 * dim, e + 1] = scale * plus[dim]
                coeffs[2 * dim + 1, e + 1] = scale * minus[dim]
            force[e + 1] = scale * (src[e + 1] + STORAGE * v0[e + 1])
            return turned, after

        for first, stop in ranges:
            run(step, first, stop, start)

    @pl.when(jnp.logical_not(is_press))
    def _():
        def pair_of(mean, flow, field):
            speed = flow * field
            gain = mean + jnp.maximum(speed, 0.0)
            return gain, gain - speed

        def start(first):
            here = [half_turn(ref[first + 1]) for ref in (prop, fluid)]
            if first == 0:
                return (blank, blank), here
            means = [
                face_mean(ref[first], jnp.where(low_lanes, half_turn(ref[first]), after))
                for ref, after in zip((prop, fluid), here)
            ]
            gain, loss = pair_of(means[0], means[1], c1[first])
            return (half_turn(gain), half_turn(loss)), here

        def step(e, carry):
            before, here = carry
            after = [half_turn(ref[e + 2]) for ref in (prop, fluid)]
            value, level = prop[e + 1], fluid[e + 1]
            total = snk[e + 1]
            gain, loss = pair_of(
                face_mean(value, next_row(value)), face_mean(level, next_row(level)), c0[e + 1]
            )
            coeffs[0, e + 1] = loss
            coeffs[1, e + 1] = prev_row(gain)
            total += gain + prev_row(loss)
            gain, loss = pair_of(
                face_mean(value, jnp.where(not_last, next_lane(value), 0.0)),
                face_mean(level, jnp.where(not_last, next_lane(level), 0.0)),
                c2[e + 1],
            )
            coeffs[4, e + 1] = loss
            coeffs[5, e + 1] = prev_lane(gain)
            total += gain + prev_lane(loss)
            gain, loss = pair_of(
                face_mean(value, jnp.where(low_lanes, here[0], after[0])),
                face_mean(level, jnp.where(low_lanes, here[1], after[1])),
                c1[e + 1],
            )
            turned = half_turn(gain), half_turn(loss)
            coeffs[2, e + 1] = loss
            coeffs[3, e + 1] = jnp.where(low_lanes, before[0], turned[0])
            diag[e + 1] = total + gain + jnp.where(low_lanes, before[1], turned[1])
            force[e + 1] = src[e + 1]
            return turned, after

        for first, stop in ranges:
            run(step, first, stop, start)


def inner_kernel(where_ref, perm_ref, cond_ref, across, *refs):
    coeffs, force, diag, fluid = refs[-12:-8]
    cells = refs[-8:]
    is_press = where_ref[0] == 0
    is_low = where_ref[1] == 0
    ext = cells[0].shape[0] - 2
    side = XH // 2
    tiles = ext - XH
    cols = tiles * LANES
    rows = rim_rows(is_low)
    tables = class_tables(is_press, perm_ref, cond_ref)
    clear(tuple(cells[:3]) + (fluid,), (0, 1, 2, ext - 1, ext, ext + 1))

    def fill(t, carry):
        read = lambda index, row: across[row : row + 1, lanes_at(t, index * cols)]
        put_cells(cells, is_press, tables, t + side, rows, rim_cells(is_low, read))
        put_level(fluid, cells, t + side, rows)
        return carry

    lax.fori_loop(0, tiles, fill, 0, unroll=8)
    made = (coeffs, force, diag, fluid)
    face_terms(cells, made, is_press, [(side, ext - side)], UNROLL)


def main_kernel(where_ref, perm_ref, cond_ref, from_left, from_right, *refs):
    v1, v2, boundary = refs[12:15]
    coeffs, force, diag, fluid = refs[15:19]
    cells = refs[19:]
    v0 = cells[0]
    is_press = where_ref[0] == 0
    is_low = where_ref[1] == 0
    ext = v0.shape[0] - 2
    wide = XH * W
    side = XH // 2
    own_rows = pl.ds(pl.multiple_of(jnp.where(is_low, 0, 8), 8), 32)
    tables = class_tables(is_press, perm_ref, cond_ref)

    for e, message, at in (
        (0, from_left, 0), (1, from_left, 1), (ext - 2, from_right, 0), (ext - 1, from_right, 1)
    ):
        parts = [message[:, lanes_at(at, index * wide)] for index in range(7)]
        parts[1] = parts[1].astype(jnp.int32)
        put_cells(cells, is_press, tables, e, own_rows, parts)
        corner = message[:, 7 * wide :]
        read = lambda index, row, corner=corner, at=at: corner[
            index * 4 + row * 2 + at : index * 4 + row * 2 + at + 1
        ]
        put_cells(cells, is_press, tables, e, rim_rows(is_low), rim_cells(is_low, read))
        put_level(fluid, cells, e, slice(None))
    clear((v1, v2), (0, ext + 1))
    made = (coeffs, force, diag, fluid)
    face_terms(cells, made, is_press, [(0, side + 1), (ext - side - 1, ext)], UNROLL)
    chebyshev, explicit = sweep_weights()
    for chosen, weights, centre in (
        (is_press, chebyshev, None),
        (jnp.logical_not(is_press), explicit, diag),
    ):

        @pl.when(chosen)
        def _(weights=weights, centre=centre):
            (w0, u0), (w1, u1) = weights[:2]
            sweep((0, ext), coeffs, force, centre, v0, v0, store_in(v1), w0, u0)
            sweep((0, ext), coeffs, force, centre, v1, v0, store_in(v2), w1, u1)

    def send(e, carry):
        value = v2[e + 1]
        boundary[:, lanes_at(e)] = jnp.where(is_low, value[30:32], value[8:10])
        return carry

    lax.fori_loop(0, ext, send, 0, unroll=UNROLL)


def finish_kernel(where_ref, v1, v2, coeffs, force, diag, boundary, done, out, now, later):
    del done
    is_press = where_ref[0] == 0
    is_low = where_ref[1] == 0
    ext = v2.shape[0] - 2
    side = XH // 2
    rim_at = pl.multiple_of(jnp.where(is_low, 32, 0), 8)
    blank = jnp.zeros(v2.shape[1:], jnp.float32)
    for ref in (now, later):
        ref[0] = blank
        ref[ext + 1] = blank

    def fill(e, carry):
        now[e + 1] = v2[e + 1]
        now[e + 1, pl.ds(rim_at, 8), :] = placed_pair(boundary[:, lanes_at(e)], is_low)
        return carry

    lax.fori_loop(0, ext, fill, 0, unroll=UNROLL)
    chebyshev, explicit = sweep_weights()

    def put_out(e, value):
        out[0, :, lanes_at(e - side)] = jnp.where(is_low, value[0:32], value[8:40])

    for chosen, weights, centre in (
        (is_press, chebyshev, None),
        (jnp.logical_not(is_press), explicit, diag),
    ):

        @pl.when(chosen)
        def _(weights=weights, centre=centre):
            (w2, u2), (w3, u3) = weights[2:]
            sweep((0, ext), coeffs, force, centre, now, v1, store_in(later), w2, u2)
            sweep((side, ext - side), coeffs, force, centre, later, now, put_out, w3, u3)


def regrouped(pieces):
    lane = lane_index(pieces[0].shape)
    result = []
    for q in range(4):
        value = None
        for place in range(4):
            piece = pieces[place]
            if place != q:
                piece = pltpu.roll(piece, ((place - q) * 32) % LANES, 1)
            value = piece if value is None else jnp.where(lane >= place * 32, piece, value)
        result.append(value)
    return result


def faces_kernel(where_ref, own, other, plane_ref, rock, out_ref, token, field, rim, out, sems):
    token[...] = jnp.zeros(token.shape, jnp.float32)
    is_press = where_ref[0] == 0
    is_low = where_ref[1] == 0
    tiles = out.shape[2] // LANES
    groups = tiles // 4
    side = XH // 2
    extra = groups * 2 * LANES

    def ordered(mine, theirs):
        return [jnp.where(is_low, mine, theirs), jnp.where(is_low, theirs, mine)]

    pieces = []
    for par in range(2):
        pieces += ordered(
            own[par * groups : (par + 1) * groups, extra : extra + LANES],
            other[par * groups : (par + 1) * groups, extra : extra + LANES],
        )
    for q, value in enumerate(regrouped(pieces)):
        rim[q] = value
    plane = ordered(own[:, extra + LANES :], plane_ref[:, :LANES])
    lane = lane_index((32, LANES))
    field[tiles, 0:32, :] = jnp.where(lane < 32, plane[0], pltpu.roll(plane[1], 32, 1))

    def gather(group, carry):
        pieces = []
        for par in range(2):
            at = lanes_at(group, par * groups * LANES)
            pieces += ordered(own[:, at], other[:, at])
        for q, value in enumerate(regrouped(pieces)):
            field[4 * group + q, 0:32, :] = value
            field[4 * group + q, 32:33, :] = rim[q, pl.ds(group, 1), :]
        return carry

    lax.fori_loop(0, groups, gather, 0, unroll=8)
    low_lanes = lane < HALF
    not_last = lane % W != W - 1

    def around(t):
        value = field[t]
        here = value[0:32]
        after = field[t + 1, 0:32, :]
        return here, (
            next_row(value)[0:32],
            jnp.where(low_lanes, half_turn(here), half_turn(after)),
            next_lane(here),
        )

    def press(t, carry):
        here, others = around(t)
        others = (others[0], others[1], jnp.where(not_last, others[2], 0.0))
        for dim in range(3):
            out[dim, :, lanes_at(t)] = face_mean(here, others[dim])
        return carry

    def heat(t, carry):
        here, others = around(t)
        stone = rock[t + side + 1]
        after = rock[t + side + 2]
        near = (
            next_row(stone),
            jnp.where(tall_low, half_turn(stone), half_turn(after)),
            jnp.where(tall_not_last, next_lane(stone), 0.0),
        )
        for dim in range(3):
            mean = face_mean(stone, near[dim])
            mean = jnp.where(is_low, mean[0:32], mean[8:40])
            out[dim, :, lanes_at(t)] = mean * (here - others[dim])
        return carry

    tall_lane = lane_index(rock.shape[1:])
    tall_low = tall_lane < HALF
    tall_not_last = tall_lane % W != W - 1
    part = tiles // PARTS
    copies = []
    for index in range(PARTS):
        first = index * part

        @pl.when(is_press)
        def _(first=first):
            lax.fori_loop(first, first + part, press, 0, unroll=8)

        @pl.when(jnp.logical_not(is_press))
        def _(first=first):
            lax.fori_loop(first, first + part, heat, 0, unroll=8)

        at = pl.ds(first * LANES, part * LANES)
        copy = pltpu.make_async_copy(out.at[:, :, at], out_ref.at[0, :, :, at], sems.at[index])
        copy.start()
        copies.append(copy)
    for copy in copies:
        copy.wait()


def paired_body(states, coupled, facies, injectors, producers, perm_table, cond_table):
    rows, cols = states.shape[1], states.shape[2]
    tiles = cols // LANES
    ext = tiles + XH
    wide = XH * W
    groups = tiles // 4
    place = jnp.stack([lax.axis_index("code"), lax.axis_index("ba")]).astype(jnp.int32)
    count = lax.axis_size("aa")
    up = [(i, i + 1) for i in range(count - 1)]
    down = [(b, a) for a, b in up]
    swap = [(0, 1), (1, 0)]
    opposite = [(0, 3), (1, 2), (2, 1), (3, 0)]
    f32, i32 = jnp.float32, jnp.int32
    states, coupled, facies, injectors, producers = [
        pltpu.with_memory_space_constraint(value, pltpu.HBM)
        for value in (states, coupled, facies, injectors, producers)
    ]

    to_right, to_left, across, corners = pl.pallas_call(
        edges_kernel,
        out_shape=[
            in_vmem((rows, 7 * wide)),
            in_vmem((rows, 7 * wide)),
            in_vmem((2, 5 * cols)),
            in_vmem((2, 10 * wide)),
        ],
        in_specs=[SM] + [HB] * 5,
        out_specs=[VM] * 4,
        scratch_shapes=[
            pltpu.VMEM((4, rows, wide), f32),
            pltpu.VMEM((4, rows, wide), f32),
            pltpu.VMEM((4, 8, cols), f32),
            pltpu.VMEM((3, rows, wide), i32),
            pltpu.VMEM((3, rows, wide), i32),
            pltpu.VMEM((3, 8, cols), i32),
            pltpu.SemaphoreType.DMA((21,)),
        ],
        compiler_params=LEAN,
        cost_estimate=cost(1),
        name="edges",
    )(place, states, coupled, facies, injectors, producers)
    corners = held(lax.ppermute(corners, "ba", swap))
    to_right, to_left, across = pl.pallas_call(
        pack_kernel,
        out_shape=[
            in_vmem((rows, 7 * wide + LANES)),
            in_vmem((rows, 7 * wide + LANES)),
            in_vmem(across.shape),
        ],
        in_specs=[VM] * 4,
        out_specs=[VM] * 3,
        compiler_params=LEAN,
        cost_estimate=cost(1),
        name="pack",
    )(to_right, to_left, across, corners)
    from_left = held(lax.ppermute(to_right, "aa", up))
    from_right = held(lax.ppermute(to_left, "aa", down))
    from_across = held(lax.ppermute(across, "ba", swap))

    field = (ext + 2, rows + 8, LANES)
    turned = in_vmem((32, (2 * groups + 2) * LANES))
    turned_over = in_vmem((32, (2 * groups + 3) * LANES))
    turned_own, turned_other, fluid, *cells = pl.pallas_call(
        turn_kernel,
        out_shape=[turned, turned_over]
        + [in_vmem(field)] * 9,
        in_specs=[SM] * 3 + [HB] * 5 + [VM],
        out_specs=[VM] * 11,
        scratch_shapes=[
            pltpu.VMEM(states.shape, f32),
            pltpu.VMEM(coupled.shape, f32),
            pltpu.VMEM(facies.shape, i32),
            pltpu.VMEM(facies.shape, i32),
            pltpu.VMEM(facies.shape, i32),
            pltpu.SemaphoreType.DMA((5,)),
        ],
        compiler_params=params(10),
        cost_estimate=cost(6),
        name="turn",
    )(
        place, perm_table, cond_table, states, coupled, facies, injectors, producers,
        corners,
    )
    other = held(lax.ppermute(turned_other, ("code", "ba"), opposite))
    coeffs, force, diag, fluid, *cells = pl.pallas_call(
        inner_kernel,
        out_shape=[in_vmem((6,) + field)] + [in_vmem(field)] * 11,
        in_specs=[SM] * 3 + [VM] * 10,
        out_specs=[VM] * 12,
        input_output_aliases={4 + index: 3 + index for index in range(9)},
        compiler_params=params(2),
        cost_estimate=cost(6),
        name="inner",
    )(place, perm_table, cond_table, from_across, fluid, *cells)
    turned_own, plane = pl.pallas_call(
        plane_kernel,
        out_shape=[turned, in_vmem((32, 5 * LANES))],
        in_specs=[SM] + [VM] * 4,
        out_specs=[VM] * 2,
        compiler_params=LEAN,
        cost_estimate=cost(1),
        name="plane",
    )(place, from_right, turned_own, from_left, force)
    own = held(lax.ppermute(turned_own, "code", swap))
    plane_over = held(lax.ppermute(plane, ("code", "ba"), opposite))
    v1, v2, boundary, coeffs, force, diag, fluid, *cells = pl.pallas_call(
        main_kernel,
        out_shape=[in_vmem(field), in_vmem(field), in_vmem((2, ext * LANES))]
        + [in_vmem((6,) + field)]
        + [in_vmem(field)] * 11,
        in_specs=[SM] * 3 + [VM] * 14,
        out_specs=[VM] * 15,
        input_output_aliases={5 + index: 3 + index for index in range(12)},
        compiler_params=params(2),
        cost_estimate=cost(6),
        name="main",
    )(
        place, perm_table, cond_table, from_left, from_right,
        coeffs, force, diag, fluid, *cells,
    )
    rock = cells[2]
    boundary = held(lax.ppermute(boundary, "ba", swap))
    received, token = pl.pallas_call(
        faces_kernel,
        out_shape=[jax.ShapeDtypeStruct(coupled.shape, f32), in_vmem((8, LANES))],
        in_specs=[SM] + [VM] * 4,
        out_specs=[HB, VM],
        scratch_shapes=[
            pltpu.VMEM((tiles + 1, rows + 8, LANES), f32),
            pltpu.VMEM((4, groups, LANES), f32),
            pltpu.VMEM(coupled.shape[1:], f32),
            pltpu.SemaphoreType.DMA((PARTS,)),
        ],
        compiler_params=params(8),
        cost_estimate=cost(5),
        name="faces",
    )(place, own, other, plane_over, rock)
    stepped = pl.pallas_call(
        finish_kernel,
        out_shape=jax.ShapeDtypeStruct(states.shape, f32),
        in_specs=[SM] + [VM] * 7,
        out_specs=VM,
        scratch_shapes=[pltpu.VMEM(field, f32)] * 2,
        compiler_params=params(8),
        cost_estimate=cost(6),
        name="finish",
    )(place, v1, v2, coeffs, force, diag, boundary, token)
    return (stepped, received)


def solution(mesh):
    paired = mesh.shape["ba"] == 2 and mesh.shape["code"] == 2
    return jax.shard_map(
        paired_body if paired else body,
        mesh=mesh,
        in_specs=(
            P("code", "ba", "aa"),
            P("code", None, "ba", "aa"),
            P("code", "ba", "aa"),
            P("code", "ba", "aa"),
            P("code", "ba", "aa"),
            P(),
            P(),
        ),
        out_specs=(P("code", "ba", "aa"), P("code", None, "ba", "aa")),
        check_vma=False,
    )
```

```python
import jax
import jax.numpy as jnp
from jax import lax
from jax.experimental import pallas as pl
from jax.experimental.pallas import tpu as pltpu
from jax.sharding import PartitionSpec as P

W = 64
NF = 6
ITERS = 4


STORAGE = 0.5
LOWER_BOUND = 0.05
INJECTION = 2.0
PRODUCT_INDEX = 1.0
WELL_PRESSURE = -1.0
FLOW_RATE = 1.0
CHILLED_INFLOW = 0.1
TIME_STEP = 0.05


def extended(block, sides, width):
    for axis, dim in sides:
        count = lax.axis_size(axis)
        forward = [(i, i + 1) for i in range(count - 1)]
        backward = [(target, source) for source, target in forward]
        low = lax.ppermute(
            lax.slice_in_dim(block, block.shape[dim] - width, None, axis=dim), axis, forward
        )
        high = lax.ppermute(lax.slice_in_dim(block, 0, width, axis=dim), axis, backward)
        block = jnp.concatenate([low, block, high], axis=dim)
    return block


def from_partner(value, axis, stride):
    mask = 2**stride
    pairs = [(source, source ^ mask) for source in range(lax.axis_size(axis))]
    return lax.ppermute(value, axis, pairs)


def brine_flowability(matrix_heat_level):
    return 0.2 + 0.8 * jax.nn.sigmoid(6.0 * (matrix_heat_level - 0.5))


def harmonic(left_val, eastern_neighbor_number, face_mask):
    return (
        face_mask
        * 2.0
        * left_val
        * eastern_neighbor_number
        / (left_val + eastern_neighbor_number + 1.0 - face_mask)
    )


def accumulate(terms):
    result = terms[0]
    for term in terms[1:]:
        result = result + term
    return result


def sweep_weights():
    centre_val = (2.0 + LOWER_BOUND) / 2.0
    half_width = (2.0 - LOWER_BOUND) / 2.0
    quotient_number = centre_val / half_width
    rho_old = 1.0 / quotient_number
    chebyshev = [(1.0 / centre_val, 0.0)]
    for index_k in range(1, ITERS):
        rho_new = 1.0 / (2.0 * quotient_number - rho_old)
        chebyshev.append((2.0 * rho_new / half_width, rho_new * rho_old))
        rho_old = rho_new
    explicit = []
    for index_k in range(ITERS):
        if index_k % 2 == 0:
            explicit.append((TIME_STEP, 0.0))
        else:
            explicit.append((0.5 * TIME_STEP, -0.5))
    return (chebyshev, explicit)


def pressure_terms(center, beside_all):
    masks = [center[2] * beside_all[direction][2] for direction in range(6)]
    perm_faces = [
        harmonic(center[1], beside_all[direction][1], masks[direction]) for direction in range(6)
    ]
    mobility = []
    for direction in range(6):
        field_component = 5 + direction // 2
        if direction % 2 == 0:
            mobility.append(center[field_component] * masks[direction])
        else:
            mobility.append(beside_all[direction][field_component] * masks[direction])
    coefficient = [perm_faces[direction] * mobility[direction] for direction in range(6)]
    diagonal_entries = accumulate(coefficient) + STORAGE + center[4]
    forcing = center[3] + STORAGE * center[0]
    scaling = 1.0 / diagonal_entries
    outgoing = [
        perm_faces[direction] * (center[0] - beside_all[direction][0]) for direction in (0, 2, 4)
    ]
    return (coefficient, diagonal_entries, forcing, scaling, outgoing)


def heat_terms(center, beside_all):
    masks = [center[2] * beside_all[direction][2] for direction in range(6)]
    conduct_faces = [
        harmonic(center[1], beside_all[direction][1], masks[direction]) for direction in range(6)
    ]
    own_fluid = brine_flowability(center[0])
    fluid_faces = [
        harmonic(own_fluid, brine_flowability(beside_all[direction][0]), masks[direction])
        for direction in range(6)
    ]
    velocity = []
    for direction in range(6):
        field_component = 5 + direction // 2
        if direction % 2 == 0:
            velocity.append(center[field_component] * fluid_faces[direction])
        else:
            velocity.append(-beside_all[direction][field_component] * fluid_faces[direction])
    coefficient = [
        conduct_faces[direction] - jnp.minimum(velocity[direction], 0.0) for direction in range(6)
    ]
    outflow = accumulate([jnp.maximum(velocity[direction], 0.0) for direction in range(6)])
    diagonal_entries = accumulate(conduct_faces) + outflow + center[4]
    forcing = center[3]
    scaling = jnp.ones_like(diagonal_entries)
    outgoing = [fluid_faces[direction] for direction in (0, 2, 4)]
    return (coefficient, diagonal_entries, forcing, scaling, outgoing)


def crop(values, margin):
    row_count = values.shape[-2]
    col_count = values.shape[-1]
    return values[..., margin : row_count - margin, margin * W : col_count - margin * W]


def beside(values):
    row_count = values.shape[-2]
    col_count = values.shape[-1]
    inner_cols = col_count - 2 * W
    column_pos = lax.broadcasted_iota(jnp.int32, (row_count - 2, inner_cols), 1) % W
    lower_mask = (column_pos > 0).astype(values.dtype)
    upper_mask = (column_pos < W - 1).astype(values.dtype)
    center = values[..., 1 : row_count - 1, W : col_count - W]
    beside_all = [
        values[..., 2:, W : col_count - W],
        values[..., : row_count - 2, W : col_count - W],
        values[..., 1 : row_count - 1, 2 * W :],
        values[..., 1 : row_count - 1, : col_count - 2 * W],
        values[..., 1 : row_count - 1, W + 1 : col_count - W + 1] * upper_mask,
        values[..., 1 : row_count - 1, W - 1 : col_count - W - 1] * lower_mask,
    ]
    return (beside_all, center)


def extend(values, margin):
    row_ext = extended(values, (("ba", 1),), margin)
    return extended(row_ext, (("aa", 2),), margin * W)


def regroup_layout(received_block):
    components = received_block.shape[0]
    turned = jnp.transpose(received_block, (0, 3, 2, 1))
    return turned.reshape(
        components, received_block.shape[3], received_block.shape[2] * received_block.shape[1]
    )


def body(states, coupled, facies, injectors, producers, perm_table, cond_table):
    is_press = lax.axis_index("code") == 0
    own_field = states[0]
    row_count = own_field.shape[0]
    col_count = own_field.shape[1]
    lithology_lookup = jnp.where(is_press, perm_table, cond_table)
    other_table = jnp.where(is_press, cond_table, perm_table)
    own_classes = facies[0]
    property_field = accumulate(
        [jnp.where(own_classes == index_c, lithology_lookup[index_c], 0.0) for index_c in range(NF)]
    )
    other_property = accumulate(
        [jnp.where(own_classes == index_c, other_table[index_c], 0.0) for index_c in range(NF)]
    )
    inject_cells = injectors[0].astype(jnp.float32)
    produce_cells = producers[0].astype(jnp.float32)
    source = inject_cells * jnp.where(
        is_press, INJECTION, FLOW_RATE * CHILLED_INFLOW
    ) + produce_cells * jnp.where(is_press, PRODUCT_INDEX * WELL_PRESSURE, 0.0)
    well_sink = produce_cells * jnp.where(
        is_press, PRODUCT_INDEX, FLOW_RATE
    ) + inject_cells * jnp.where(is_press, 0.0, FLOW_RATE)
    inside = jnp.ones_like(own_field)
    stacked = jnp.concatenate(
        [
            jnp.stack([own_field, property_field, inside, source, well_sink]),
            coupled[0],
            other_property[None],
        ],
        axis=0,
    )
    halo_depth = 1
    widened_stack = extend(stacked, halo_depth)
    beside_all, center = beside(widened_stack)
    coefficient, diagonal_entries, forcing, scaling, outgoing_list = lax.cond(
        is_press, pressure_terms, heat_terms, center, beside_all
    )
    outgoing = jnp.stack([crop(face_item, halo_depth - 1) for face_item in outgoing_list])
    payload = outgoing[::-1].reshape(3, row_count, col_count // W, W)
    regrouped = regroup_layout(
        lax.all_to_all(payload, "ba", split_axis=3, concat_axis=1, tiled=True)
    )
    received = from_partner(regrouped, "code", 0)
    chebyshev, explicit = sweep_weights()
    present_iterate = own_field
    previous = None
    prev_depth = 0
    counter = 0
    for sweep_block in range(ITERS // halo_depth):
        widened = extend(present_iterate[None], halo_depth)[0]
        if previous is None:
            previous = widened
            prev_depth = halo_depth
        region = halo_depth
        region = region - 1
        around_v, center_v = beside(widened)
        index_shift = halo_depth - 1 - region
        applied = crop(diagonal_entries, index_shift) * center_v - accumulate(
            [
                crop(coefficient[direction], index_shift) * around_v[direction]
                for direction in range(6)
            ]
        )
        residual = crop(scaling, index_shift) * (crop(forcing, index_shift) - applied)
        weight_new = jnp.where(is_press, chebyshev[counter][0], explicit[counter][0])
        weight_old = jnp.where(is_press, chebyshev[counter][1], explicit[counter][1])
        updated = (
            center_v
            + weight_new * residual
            + weight_old * (center_v - crop(previous, prev_depth - region))
        )
        previous = widened
        prev_depth = region + 1
        widened = updated
        counter = counter + 1
        present_iterate = widened
    return (present_iterate[None], received[None])


TINY = 1e-30
LANES = 128
HALF = 64
XH = 4
VM = pl.BlockSpec(memory_space=pltpu.VMEM)
SM = pl.BlockSpec(memory_space=pltpu.SMEM)
HB = pl.BlockSpec(memory_space=pltpu.HBM)
UNROLL = 4
PARTS = 4
LEAN = pltpu.CompilerParams(vmem_limit_bytes=6 * 2**20)


def params(megabytes):
    return pltpu.CompilerParams(vmem_limit_bytes=megabytes * 2**20)


def cost(micros):
    return pl.CostEstimate(
        flops=int(micros * 1.15e9), bytes_accessed=int(micros * 3.6e6), transcendentals=0
    )


def in_vmem(shape):
    return pltpu.VMEM(shape, jnp.float32)


def held(value):
    return pltpu.with_memory_space_constraint(value, pltpu.VMEM)


def lanes_at(tile, base=0):
    return pl.ds(pl.multiple_of(base + tile * LANES, LANES), LANES)


def lane_index(shape):
    return lax.broadcasted_iota(jnp.int32, shape, len(shape) - 1)


def inverse(value):
    return pl.reciprocal(value, approx=False)


def face_mean(left, right):
    return 2.0 * left * right * inverse(jnp.maximum(left + right, TINY))


def flowability(level):
    return 0.2 + 0.8 * inverse(1.0 + jnp.exp(-6.0 * (level - 0.5)))


def half_turn(value):
    return pltpu.roll(value, HALF, 1)


def next_lane(value):
    return pltpu.roll(value, LANES - 1, 1)


def prev_lane(value):
    return pltpu.roll(value, 1, 1)


def next_row(value):
    return pltpu.roll(value, value.shape[0] - 1, 0)


def prev_row(value):
    return pltpu.roll(value, 1, 0)


def look_up(table, codes):
    value = jnp.zeros(codes.shape, jnp.float32)
    for index_c in range(NF):
        value = jnp.where(codes == index_c + 1, table[index_c], value)
    return value


def placed_pair(pair, is_low):
    blank = jnp.zeros((6, pair.shape[1]), pair.dtype)
    return jnp.where(
        is_low, jnp.concatenate([pair, blank], 0), jnp.concatenate([blank, pair], 0)
    )


def placed_row(row, is_low):
    blank = jnp.zeros((7, row.shape[1]), row.dtype)
    return jnp.where(is_low, jnp.concatenate([row, blank], 0), jnp.concatenate([blank, row], 0))


def rim_slots(is_low, state, codes, f0, f1, f2, inject, produce):
    def pair(value):
        return jnp.where(is_low, value[6:8], value[0:2])

    def near(one, two):
        value = jnp.concatenate([one[0:8], two[0:8]], 0)
        return jnp.concatenate(
            [
                jnp.where(is_low, value[7:8], value[0:1]),
                jnp.where(is_low, value[15:16], value[8:9]),
            ],
            0,
        )

    return [
        pair(state),
        pair((codes + 1).astype(jnp.float32)),
        pair(f0),
        near(f1, f2),
        near(inject.astype(jnp.float32), produce.astype(jnp.float32)),
    ]


def corner_kernel(where_ref, st, cp, fa, ij, pr, corners, state, field, codes, sems):
    is_low = where_ref[1] == 0
    rows, cols = st.shape[1], st.shape[2]
    wide = XH * W
    at = pl.ds(pl.multiple_of(jnp.where(is_low, rows - 8, 0), 8), 8)
    copies = []
    for side, start in enumerate((0, cols - wide)):
        lanes = pl.ds(start, wide)
        for source, target in (
            (st.at[0, at, lanes], state.at[side]),
            (cp.at[0, :, at, lanes], field.at[side]),
            (fa.at[0, at, lanes], codes.at[side, 0]),
            (ij.at[0, at, lanes], codes.at[side, 1]),
            (pr.at[0, at, lanes], codes.at[side, 2]),
        ):
            copy = pltpu.make_async_copy(source, target, sems.at[len(copies)])
            copy.start()
            copies.append(copy)
    for copy in copies:
        copy.wait()
    for side in range(2):
        slots = rim_slots(
            is_low, state[side], codes[side, 0], field[side, 0], field[side, 1], field[side, 2],
            codes[side, 1], codes[side, 2],
        )
        for index, slot in enumerate(slots):
            start = (2 * index + side) * wide
            corners[:, start : start + wide] = slot


def edges_kernel(where_ref, st, cp, fa, ij, pr, to_right, to_left, across):
    is_low = where_ref[1] == 0
    rows, cols = st.shape[1], st.shape[2]
    wide = XH * W
    for target, start in ((to_right, cols - wide), (to_left, 0)):
        at = slice(start, start + wide)
        parts = [
            st[0, :, at],
            (fa[0, :, at] + 1).astype(jnp.float32),
            cp[0, 0, :, at],
            cp[0, 1, :, at],
            cp[0, 2, :, at],
            ij[0, :, at].astype(jnp.float32),
            pr[0, :, at].astype(jnp.float32),
        ]
        for index, part in enumerate(parts):
            target[:, index * wide : (index + 1) * wide] = part
    rim = pl.ds(pl.multiple_of(jnp.where(is_low, rows - 8, 0), 8), 8)
    slots = rim_slots(
        is_low, st[0, rim, :], fa[0, rim, :], cp[0, 0, rim, :], cp[0, 1, rim, :],
        cp[0, 2, rim, :], ij[0, rim, :], pr[0, rim, :],
    )
    for index, slot in enumerate(slots):
        across[:, index * cols : (index + 1) * cols] = slot


def pack_kernel(right_in, left_in, across_in, corners, to_right, to_left, across):
    across[...] = across_in[...]
    wide = XH * W
    for side, (source, target) in enumerate(((left_in, to_left), (right_in, to_right))):
        target[:, : 7 * wide] = source[...]
        target[:, 7 * wide :] = jnp.zeros((32, LANES), jnp.float32)
        for index in range(5):
            for row in range(2):
                for half in range(2):
                    start = (2 * index + side) * wide + half * LANES
                    place = index * 4 + row * 2 + half
                    target[place : place + 1, 7 * wide :] = corners[
                        row : row + 1, start : start + LANES
                    ]


def put_cells(refs, is_press, tables, e, rows, cells):
    v0, prop, rock, c0, c1, c2, src, snk = refs
    state, codes, f0, f1, f2, inject, produce = cells
    v0[e + 1, rows, :] = state
    prop[e + 1, rows, :] = look_up(tables[0], codes)
    rock[e + 1, rows, :] = look_up(tables[1], codes)
    c0[e + 1, rows, :] = f0
    c1[e + 1, rows, :] = f1
    c2[e + 1, rows, :] = f2
    src[e + 1, rows, :] = jnp.where(is_press, 2.0 * inject - produce, 0.1 * inject)
    snk[e + 1, rows, :] = jnp.where(is_press, produce, produce + inject)


def class_tables(is_press, perm_ref, cond_ref):
    perm = [perm_ref[index_c] for index_c in range(NF)]
    own = [jnp.where(is_press, perm[index_c], cond_ref[index_c]) for index_c in range(NF)]
    return own, perm


def turn_kernel(
    where_ref, perm_ref, cond_ref, st, cp, fa, ij, pr, corners,
    own, other, rim, fluid, v0, prop, rock, c0, c1, c2, src, snk,
):
    del corners
    is_heat = where_ref[0] == 1
    is_low = where_ref[1] == 0
    own_rows = pl.ds(pl.multiple_of(jnp.where(is_low, 0, 8), 8), 32)
    groups = st.shape[2] // (4 * LANES)
    extra = groups * 2 * LANES
    row = lax.broadcasted_iota(jnp.int32, (32, LANES), 0)

    def step(group, rims):
        tall = jnp.concatenate(
            [st[0, :, lanes_at(4 * group + q)] for q in range(4)], axis=0
        )
        tall = jnp.where(is_heat, flowability(tall), tall)
        for q in range(4):
            fluid[4 * group + q + XH // 2 + 1, own_rows, :] = tall[32 * q : 32 * q + 32]
        turned = tall.T
        for par in range(2):
            low = turned[par * HALF : par * HALF + 32]
            high = turned[par * HALF + 32 : par * HALF + 64]
            own[:, lanes_at(group, par * groups * LANES)] = jnp.where(is_low, low, high)
            away = jnp.where(is_low, high, low)
            rim = high[0:1]

            other[:, lanes_at(group, par * groups * LANES)] = away
            rims = jnp.where(row == par * groups + group, rim, rims)
        return rims

    rims = lax.fori_loop(0, groups, step, jnp.zeros((32, LANES), jnp.float32), unroll=8)
    rim[:, :LANES] = jnp.where(is_low, rims, 0.0)
    other[:, extra : extra + LANES] = jnp.where(is_low, 0.0, rims)
    refs = (v0, prop, rock, c0, c1, c2, src, snk)
    is_press = where_ref[0] == 0
    tables = class_tables(is_press, perm_ref, cond_ref)
    tiles = st.shape[2] // LANES

    def fill(t, carry):
        at = lanes_at(t)
        cells = (
            st[0, :, at], fa[0, :, at] + 1, cp[0, 0, :, at], cp[0, 1, :, at], cp[0, 2, :, at],
            ij[0, :, at].astype(jnp.float32), pr[0, :, at].astype(jnp.float32),
        )
        put_cells(refs, is_press, tables, t + XH // 2, own_rows, cells)
        return carry

    lax.fori_loop(0, tiles, fill, 0, unroll=8)


def plane_kernel(where_ref, from_right, own_in, *rest):
    del own_in
    own = rest[-1]
    is_heat = where_ref[0] == 1
    is_low = where_ref[1] == 0
    wide = XH * W
    value = from_right[:, 0:LANES]
    inside = from_right[:, wide : wide + LANES] > 0.5
    value = jnp.where(is_heat, jnp.where(inside, flowability(value), 0.0), value)
    tall = jnp.concatenate([value, value, jnp.zeros((64, LANES), jnp.float32)], 0).T
    low, high = tall[0:32], tall[32:64]
    keep = lane_index((32, LANES)) < 32
    own[:, own.shape[1] - LANES :] = jnp.where(keep == is_low, low, high)


def send_kernel(where_ref, v2, own, boundary):
    is_low = where_ref[1] == 0
    ext = v2.shape[0] - 2

    def send(e, carry):
        value = v2[e + 1]
        boundary[:, lanes_at(e)] = jnp.where(is_low, value[30:32], value[8:10])
        return carry

    lax.fori_loop(0, ext, send, 0, unroll=17)
    for index in range(16):
        start = (ext + index) * LANES
        boundary[:, start : start + LANES] = own[
            2 * index : 2 * index + 2, own.shape[1] - LANES :
        ]


def sweep(tiles, coeffs, force, diag, now, last, target, weight, pull):
    first, stop = tiles
    low_lanes = lane_index((now.shape[1], LANES)) < HALF

    def step(e, carry):
        before, here = carry
        value = now[e + 1]
        after = half_turn(now[e + 2])
        total = force[e + 1]
        total += coeffs[0, e + 1] * next_row(value)
        total += coeffs[1, e + 1] * prev_row(value)
        total += coeffs[2, e + 1] * jnp.where(low_lanes, here, after)
        total += coeffs[3, e + 1] * jnp.where(low_lanes, before, here)
        total += coeffs[4, e + 1] * next_lane(value)
        total += coeffs[5, e + 1] * prev_lane(value)
        if diag is None:
            result = (1.0 + pull - weight) * value + weight * total
        else:
            result = (1.0 + pull) * value + weight * (total - diag[e + 1] * value)
        if pull != 0.0:
            result -= pull * last[e + 1]
        target(e, result)
        return here, after

    lax.fori_loop(
        first, stop, step, (half_turn(now[first]), half_turn(now[first + 1])),
        unroll=stop - first,
    )


def store_in(ref):
    def put(e, value):
        ref[e + 1] = value

    return put


def rim_cells(is_low, read):
    def pair(index):
        return placed_pair(jnp.concatenate([read(index, 0), read(index, 1)], 0), is_low)

    def near(index, row):
        return placed_row(read(index, row), is_low)

    return (
        pair(0), pair(1).astype(jnp.int32), pair(2),
        near(3, 0), near(3, 1), near(4, 0), near(4, 1),
    )


def rim_rows(is_low):
    return pl.ds(pl.multiple_of(jnp.where(is_low, 32, 0), 8), 8)


def put_level(fluid, cells, e, rows):
    prop, state = cells[1][e + 1, rows, :], cells[0][e + 1, rows, :]
    fluid[e + 1, rows, :] = jnp.where(prop > 0.0, flowability(state), 0.0)


def clear(refs, places):
    for ref in refs:
        for e in places:
            ref[e] = jnp.zeros(ref.shape[1:], jnp.float32)


def face_terms(cells, made, is_press, ranges):
    v0, prop, rock, c0, c1, c2, src, snk = cells
    coeffs, force, diag, fluid = made
    shape = v0.shape[1:]
    lane = lane_index(shape)
    low_lanes = lane < HALF
    not_last = lane % W != W - 1
    blank = jnp.zeros(shape, jnp.float32)

    def run(step, first, stop, start):
        if stop - first > 8:
            unroll = max(n for n in range(1, 10) if (stop - first) % n == 0)
            return lax.fori_loop(first, stop, step, start, unroll=unroll)
        for e in range(first, stop):
            start = step(e, start)
        return start

    def beside(value, turns, after):
        return (
            jnp.where(low_lanes, turns[0], after[0]),
            jnp.where(not_last, turns[1], 0.0),
        )

    def press_range(first, stop):
        def turns(e):
            value = prop[e + 1]
            return half_turn(value), next_lane(value)

        def along(e, now, after):
            value = prop[e + 1]
            x_side, b_side = beside(value, now, after)
            return face_mean(value, x_side) * c1[e + 1], face_mean(value, b_side) * c2[e + 1]

        def close(e, before, plus, turned):
            value = prop[e + 1]
            plus = [face_mean(value, next_row(value)) * c0[e + 1], *plus]
            minus = [prev_row(plus[0]), jnp.where(low_lanes, before, turned[0]), turned[1]]
            scale = inverse(accumulate(plus + minus) + STORAGE + snk[e + 1])
            for dim in range(3):
                coeffs[2 * dim, e + 1] = scale * plus[dim]
                coeffs[2 * dim + 1, e + 1] = scale * minus[dim]
            force[e + 1] = scale * (src[e + 1] + STORAGE * v0[e + 1])

        def step(e, carry):
            before, plus, turned, now, after = carry
            close(e - 1, before, plus, turned)
            later = turns(e + 2)
            fresh = along(e, now, after)
            return turned[0], fresh, (half_turn(fresh[0]), prev_lane(fresh[1])), after, later

        now, after = turns(first), turns(first + 1)
        before = blank
        if first > 0:
            before = half_turn(along(first - 1, turns(first - 1), now)[0])
        fresh = along(first, now, after)
        carry = (
            before, fresh, (half_turn(fresh[0]), prev_lane(fresh[1])), after, turns(first + 2)
        )
        before, plus, turned, _, _ = run(step, first + 1, stop, carry)
        close(stop - 1, before, plus, turned)

    def heat_range(first, stop):
        def turns(e):
            value, level = prop[e + 1], fluid[e + 1]
            return half_turn(value), next_lane(value), half_turn(level), next_lane(level)

        def pair_of(mean, flow, field):
            speed = flow * field
            gain = mean + jnp.maximum(speed, 0.0)
            return gain, gain - speed

        def along(e, now, after):
            value, level = prop[e + 1], fluid[e + 1]
            x_value, b_value = beside(value, now[:2], after[:2])
            x_level, b_level = beside(level, now[2:], after[2:])
            return (
                pair_of(face_mean(value, x_value), face_mean(level, x_level), c1[e + 1]),
                pair_of(face_mean(value, b_value), face_mean(level, b_level), c2[e + 1]),
            )

        def turned_pairs(x_pair, b_pair):
            return (
                half_turn(x_pair[0]), half_turn(x_pair[1]),
                prev_lane(b_pair[0]), prev_lane(b_pair[1]),
            )

        def open_cell(e, x_pair, b_pair):
            coeffs[2, e + 1] = x_pair[1]
            coeffs[4, e + 1] = b_pair[1]
            return snk[e + 1] + x_pair[0] + b_pair[0]

        def close(e, before, turned, total):
            coeffs[3, e + 1] = jnp.where(low_lanes, before[0], turned[0])
            coeffs[5, e + 1] = turned[2]
            diag[e + 1] = total + turned[3] + jnp.where(low_lanes, before[1], turned[1])

        def step(e, carry):
            before, turned, total, now, after = carry
            close(e - 1, before, turned, total)
            later = turns(e + 2)
            x_pair, b_pair = along(e, now, after)
            total = open_cell(e, x_pair, b_pair)
            return turned[:2], turned_pairs(x_pair, b_pair), total, after, later

        def row_step(e, carry):
            value, level = prop[e + 1], fluid[e + 1]
            gain, loss = pair_of(
                face_mean(value, next_row(value)), face_mean(level, next_row(level)), c0[e + 1]
            )
            coeffs[0, e + 1] = loss
            coeffs[1, e + 1] = prev_row(gain)
            diag[e + 1] += gain + prev_row(loss)
            return carry

        now, after = turns(first), turns(first + 1)
        before = (blank, blank)
        if first > 0:
            gain, loss = along(first - 1, turns(first - 1), now)[0]
            before = half_turn(gain), half_turn(loss)
        x_pair, b_pair = along(first, now, after)
        total = open_cell(first, x_pair, b_pair)
        carry = (before, turned_pairs(x_pair, b_pair), total, after, turns(first + 2))
        before, turned, total, _, _ = run(step, first + 1, stop, carry)
        close(stop - 1, before, turned, total)
        run(row_step, first, stop, 0)

    @pl.when(is_press)
    def _():
        for first, stop in ranges:
            press_range(first, stop)

    @pl.when(jnp.logical_not(is_press))
    def _():
        for first, stop in ranges:
            heat_range(first, stop)


def inner_kernel(where_ref, perm_ref, cond_ref, across, *refs):
    coeffs, force, diag, fluid = refs[-12:-8]
    cells = refs[-8:]
    is_press = where_ref[0] == 0
    is_low = where_ref[1] == 0
    ext = cells[0].shape[0] - 2
    side = XH // 2
    tiles = ext - XH
    cols = tiles * LANES
    rows = rim_rows(is_low)
    tables = class_tables(is_press, perm_ref, cond_ref)
    clear(tuple(cells[:3]) + (fluid,), (0, 1, 2, ext - 1, ext, ext + 1))

    def fill(t, carry):
        read = lambda index, row: across[row : row + 1, lanes_at(t, index * cols)]
        put_cells(cells, is_press, tables, t + side, rows, rim_cells(is_low, read))
        put_level(fluid, cells, t + side, rows)
        return carry

    lax.fori_loop(0, tiles, fill, 0, unroll=8)
    made = (coeffs, force, diag, fluid)
    face_terms(cells, made, is_press, [(side, ext - side)])


def main_kernel(where_ref, perm_ref, cond_ref, from_left, from_right, *refs):
    v1, v2 = refs[12:14]
    coeffs, force, diag, fluid = refs[14:18]
    cells = refs[18:]
    v0 = cells[0]
    is_press = where_ref[0] == 0
    is_low = where_ref[1] == 0
    ext = v0.shape[0] - 2
    wide = XH * W
    side = XH // 2
    own_rows = pl.ds(pl.multiple_of(jnp.where(is_low, 0, 8), 8), 32)
    tables = class_tables(is_press, perm_ref, cond_ref)

    for e, message, at in (
        (0, from_left, 0), (1, from_left, 1), (ext - 2, from_right, 0), (ext - 1, from_right, 1)
    ):
        parts = [message[:, lanes_at(at, index * wide)] for index in range(7)]
        parts[1] = parts[1].astype(jnp.int32)
        put_cells(cells, is_press, tables, e, own_rows, parts)
        corner = message[:, 7 * wide :]
        read = lambda index, row, corner=corner, at=at: corner[
            index * 4 + row * 2 + at : index * 4 + row * 2 + at + 1
        ]
        put_cells(cells, is_press, tables, e, rim_rows(is_low), rim_cells(is_low, read))
        put_level(fluid, cells, e, slice(None))
    clear((v1, v2), (0, ext + 1))
    made = (coeffs, force, diag, fluid)
    face_terms(cells, made, is_press, [(0, side + 1), (ext - side - 1, ext)])
    chebyshev, explicit = sweep_weights()
    src = cells[6]
    for chosen, weights, centre, drive in (
        (is_press, chebyshev, None, force),
        (jnp.logical_not(is_press), explicit, diag, src),
    ):

        @pl.when(chosen)
        def _(weights=weights, centre=centre, force=drive):
            (w0, u0), (w1, u1) = weights[:2]
            sweep((0, ext), coeffs, force, centre, v0, v0, store_in(v1), w0, u0)
            sweep((0, ext), coeffs, force, centre, v1, v0, store_in(v2), w1, u1)


def finish_kernel(
    where_ref, v1, v2_in, received_in, coeffs, force, src, diag, boundary, edge, rim,
    out_ref, now, received, later, out, tile, sems,
):
    del v2_in, received_in
    is_press = where_ref[0] == 0
    is_low = where_ref[1] == 0
    ext = now.shape[0] - 2
    side = XH // 2
    tiles = ext - XH
    rows = rim_rows(is_low)
    clear((later,), (0, ext + 1))
    lane = lane_index((32, LANES))
    mine = rim[:, LANES:]
    start = boundary.shape[1] - 16 * LANES
    theirs = jnp.concatenate(
        [boundary[:, start + index * LANES : start + (index + 1) * LANES] for index in range(16)],
        0,
    )
    plane = jnp.where(
        is_low,
        jnp.where(lane < 32, mine, theirs),
        jnp.where(lane < 32, pltpu.roll(theirs, 96, 1), pltpu.roll(mine, 32, 1)),
    )
    here = edge[0]
    beside = jnp.where(lane < HALF, half_turn(here), half_turn(plane))
    tile[...] = jnp.where(is_press, face_mean(here, beside), edge[1] * (here - beside))
    last_tile = pl.ds((tiles - 1) * LANES, LANES)
    tile_copy = pltpu.make_async_copy(tile, received.at[0, 1, :, last_tile], sems.at[PARTS])
    tile_copy.start()

    def fill(e, carry):
        now[e + 1, rows, :] = placed_pair(boundary[:, lanes_at(e)], is_low)
        return carry

    lax.fori_loop(0, ext, fill, 0, unroll=17)
    chebyshev, explicit = sweep_weights()

    def put_out(e, value):
        out[:, lanes_at(e - side)] = jnp.where(is_low, value[0:32], value[8:40])

    for chosen, weights, centre, drive in (
        (is_press, chebyshev, None, force),
        (jnp.logical_not(is_press), explicit, diag, src),
    ):

        @pl.when(chosen)
        def _(weights=weights, centre=centre, force=drive):
            (w2, u2), (w3, u3) = weights[2:]
            sweep((0, ext), coeffs, force, centre, now, v1, store_in(later), w2, u2)
            part = tiles // PARTS
            copies = []
            for index in range(PARTS):
                first = side + index * part
                sweep((first, first + part), coeffs, force, centre, later, now, put_out, w3, u3)
                at = pl.ds(index * part * LANES, part * LANES)
                copy = pltpu.make_async_copy(
                    out.at[:, at], out_ref.at[0, :, at], sems.at[index]
                )
                copy.start()
                copies.append(copy)
            for copy in copies:
                copy.wait()
    tile_copy.wait()


def regrouped(pieces):
    lane = lane_index(pieces[0].shape)
    result = []
    for q in range(4):
        value = None
        for place in range(4):
            piece = pieces[place]
            if place != q:
                piece = pltpu.roll(piece, ((place - q) * 32) % LANES, 1)
            value = piece if value is None else jnp.where(lane >= place * 32, piece, value)
        result.append(value)
    return result


def faces_kernel(
    where_ref, own, other, own_rim, rock, out_ref, edge, field, rim, out, sems
):
    is_press = where_ref[0] == 0
    is_low = where_ref[1] == 0
    tiles = out.shape[2] // LANES
    groups = tiles // 4
    side = XH // 2
    extra = groups * 2 * LANES

    def ordered(mine, theirs):
        return [jnp.where(is_low, mine, theirs), jnp.where(is_low, theirs, mine)]

    pieces = []
    for par in range(2):
        pieces += ordered(
            own_rim[par * groups : (par + 1) * groups, :LANES],
            other[par * groups : (par + 1) * groups, extra : extra + LANES],
        )
    for q, value in enumerate(regrouped(pieces)):
        rim[q] = value
    lane = lane_index((32, LANES))
    field[tiles] = jnp.zeros(field.shape[1:], jnp.float32)

    def gather(group, carry):
        pieces = []
        for par in range(2):
            at = lanes_at(group, par * groups * LANES)
            pieces += ordered(own[:, at], other[:, at])
        for q, value in enumerate(regrouped(pieces)):
            field[4 * group + q, 0:32, :] = value
            field[4 * group + q, 32:33, :] = rim[q, pl.ds(group, 1), :]
        return carry

    lax.fori_loop(0, groups, gather, 0, unroll=8)
    low_lanes = lane < HALF
    not_last = lane % W != W - 1

    def around(t, turned):
        value = field[t]
        here = value[0:32]
        after = half_turn(field[t + 1, 0:32, :])
        others = next_row(value)[0:32], jnp.where(low_lanes, turned, after), next_lane(here)
        return here, others, after

    def press(t, carry):
        here, others, after = around(t, carry)
        others = (others[0], others[1], jnp.where(not_last, others[2], 0.0))
        for dim in range(3):
            out[dim, :, lanes_at(t)] = face_mean(here, others[dim])
        return after

    def heat(t, carry):
        here, others, after = around(t, carry[0])
        stone = rock[t + side + 1, own_rows, :]
        stone_after = half_turn(rock[t + side + 2, own_rows, :])
        rim_row = jnp.where(is_low, rock[t + side + 1, 32:33, :], 0.0)
        near = (
            jnp.where(last_row, rim_row, next_row(stone)),
            jnp.where(low_lanes, carry[1], stone_after),
            jnp.where(not_last, next_lane(stone), 0.0),
        )
        for dim in range(3):
            mean = face_mean(stone, near[dim])
            out[dim, :, lanes_at(t)] = mean * (here - others[dim])
        return after, stone_after

    own_rows = pl.ds(pl.multiple_of(jnp.where(is_low, 0, 8), 8), 32)
    last_row = lax.broadcasted_iota(jnp.int32, (32, LANES), 0) == 31
    part = tiles // PARTS
    copies = []
    edge[0] = field[tiles - 1, 0:32, :]
    stone = rock[tiles - 1 + side + 1, own_rows, :]
    stone_after = half_turn(rock[tiles + side + 1, own_rows, :])
    edge[1] = face_mean(stone, jnp.where(low_lanes, half_turn(stone), stone_after))
    for index in range(PARTS):
        first = index * part

        @pl.when(is_press)
        def _(first=first):
            start = half_turn(field[first, 0:32, :])
            lax.fori_loop(first, first + part, press, start, unroll=16)

        @pl.when(jnp.logical_not(is_press))
        def _(first=first):
            start = half_turn(field[first, 0:32, :]), half_turn(rock[first + side + 1, own_rows, :])
            lax.fori_loop(first, first + part, heat, start, unroll=16)

        at = pl.ds(first * LANES, part * LANES)
        copy = pltpu.make_async_copy(out.at[:, :, at], out_ref.at[0, :, :, at], sems.at[index])
        copy.start()
        copies.append(copy)
    for copy in copies:
        copy.wait()


def paired_body(states, coupled, facies, injectors, producers, perm_table, cond_table):
    rows, cols = states.shape[1], states.shape[2]
    tiles = cols // LANES
    ext = tiles + XH
    wide = XH * W
    groups = tiles // 4
    loaded = [held(value) for value in (states, coupled, facies, injectors, producers)]
    place = jnp.stack([lax.axis_index("code"), lax.axis_index("ba")]).astype(jnp.int32)
    count = lax.axis_size("aa")
    up = [(i, i + 1) for i in range(count - 1)]
    down = [(b, a) for a, b in up]
    swap = [(0, 1), (1, 0)]
    opposite = [(0, 3), (1, 2), (2, 1), (3, 0)]
    f32, i32 = jnp.float32, jnp.int32
    states, coupled, facies, injectors, producers = [
        pltpu.with_memory_space_constraint(value, pltpu.HBM)
        for value in (states, coupled, facies, injectors, producers)
    ]

    corners = pl.pallas_call(
        corner_kernel,
        out_shape=in_vmem((2, 10 * wide)),
        in_specs=[SM] + [HB] * 5,
        out_specs=VM,
        scratch_shapes=[
            pltpu.VMEM((2, 8, wide), f32),
            pltpu.VMEM((2, 3, 8, wide), f32),
            pltpu.VMEM((2, 3, 8, wide), i32),
            pltpu.SemaphoreType.DMA((10,)),
        ],
        compiler_params=LEAN,
        cost_estimate=cost(1),
        name="corner",
    )(place, states, coupled, facies, injectors, producers)
    corners = held(lax.ppermute(corners, "ba", swap))
    to_right, to_left, across = pl.pallas_call(
        edges_kernel,
        out_shape=[
            in_vmem((rows, 7 * wide)),
            in_vmem((rows, 7 * wide)),
            in_vmem((2, 5 * cols)),
        ],
        in_specs=[SM] + [VM] * 5,
        out_specs=[VM] * 3,
        compiler_params=LEAN,
        cost_estimate=cost(2),
        name="edges",
    )(place, *loaded)
    to_right, to_left, across = pl.pallas_call(
        pack_kernel,
        out_shape=[
            in_vmem((rows, 7 * wide + LANES)),
            in_vmem((rows, 7 * wide + LANES)),
            in_vmem(across.shape),
        ],
        in_specs=[VM] * 4,
        out_specs=[VM] * 3,
        compiler_params=LEAN,
        cost_estimate=cost(1),
        name="pack",
    )(to_right, to_left, across, corners)
    from_left = held(lax.ppermute(to_right, "aa", up))
    from_right = held(lax.ppermute(to_left, "aa", down))
    from_across = held(lax.ppermute(across, "ba", swap))

    field = (ext + 2, rows + 8, LANES)
    turned_own, turned_other, rim, fluid, *cells = pl.pallas_call(
        turn_kernel,
        out_shape=[
            in_vmem((32, 2 * groups * LANES)),
            in_vmem((32, (2 * groups + 1) * LANES)),
            in_vmem((32, 2 * LANES)),
        ]
        + [in_vmem(field)] * 9,
        in_specs=[SM] * 3 + [VM] * 6,
        out_specs=[VM] * 12,
        compiler_params=params(2),
        cost_estimate=cost(1),
        name="turn",
    )(
        place, perm_table, cond_table, *loaded, across,
    )
    other = held(lax.ppermute(turned_other, ("code", "ba"), opposite))
    own = held(lax.ppermute(turned_own, "code", swap))
    coeffs, force, diag, fluid, *cells = pl.pallas_call(
        inner_kernel,
        out_shape=[in_vmem((6,) + field)] + [in_vmem(field)] * 11,
        in_specs=[SM] * 3 + [VM] * 10,
        out_specs=[VM] * 12,
        input_output_aliases={4 + index: 3 + index for index in range(9)},
        compiler_params=params(2),
        cost_estimate=cost(10),
        name="inner",
    )(place, perm_table, cond_table, from_across, fluid, *cells)
    rim = pl.pallas_call(
        plane_kernel,
        out_shape=in_vmem(rim.shape),
        in_specs=[SM] + [VM] * 4,
        out_specs=VM,
        input_output_aliases={2: 0},
        compiler_params=LEAN,
        cost_estimate=cost(1),
        name="plane",
    )(place, from_right, rim, from_left, force)
    rim = held(lax.ppermute(rim, "code", swap))

    v1, v2, coeffs, force, diag, fluid, *cells = pl.pallas_call(
        main_kernel,
        out_shape=[in_vmem(field), in_vmem(field)]
        + [in_vmem((6,) + field)]
        + [in_vmem(field)] * 11,
        in_specs=[SM] * 3 + [VM] * 14,
        out_specs=[VM] * 14,
        input_output_aliases={5 + index: 2 + index for index in range(12)},
        compiler_params=params(2),
        cost_estimate=cost(10),
        name="main",
    )(
        place, perm_table, cond_table, from_left, from_right,
        coeffs, force, diag, fluid, *cells,
    )
    boundary = pl.pallas_call(
        send_kernel,
        out_shape=in_vmem((2, (ext + 16) * LANES)),
        in_specs=[SM] + [VM] * 2,
        out_specs=VM,
        compiler_params=LEAN,
        cost_estimate=cost(1),
        name="send",
    )(place, v2, rim)
    boundary = held(lax.ppermute(boundary, "ba", swap))
    received, edge = pl.pallas_call(
        faces_kernel,
        out_shape=[jax.ShapeDtypeStruct(coupled.shape, f32), in_vmem((2, 32, LANES))],
        in_specs=[SM] + [VM] * 4,
        out_specs=[HB, VM],
        scratch_shapes=[
            pltpu.VMEM((tiles + 1, rows + 8, LANES), f32),
            pltpu.VMEM((4, groups, LANES), f32),
            pltpu.VMEM(coupled.shape[1:], f32),
            pltpu.SemaphoreType.DMA((PARTS,)),
        ],
        compiler_params=params(8),
        cost_estimate=cost(6),
        name="faces",
    )(place, own, other, rim, cells[2])
    received = pltpu.with_memory_space_constraint(received, pltpu.HBM)
    stepped, _, received = pl.pallas_call(
        finish_kernel,
        out_shape=[
            jax.ShapeDtypeStruct(states.shape, f32),
            in_vmem(field),
            jax.ShapeDtypeStruct(coupled.shape, f32),
        ],
        in_specs=[SM] + [VM] * 2 + [HB] + [VM] * 7,
        out_specs=[HB, VM, HB],
        scratch_shapes=[
            pltpu.VMEM(field, f32),
            pltpu.VMEM(states.shape[1:], f32),
            pltpu.VMEM((32, LANES), f32),
            pltpu.SemaphoreType.DMA((PARTS + 1,)),
        ],
        input_output_aliases={2: 1, 3: 2},
        compiler_params=params(5),
        cost_estimate=cost(6),
        name="finish",
    )(place, v1, v2, received, coeffs, force, cells[6], diag, boundary, edge, rim)
    return (stepped, received)


def solution(mesh):
    paired = mesh.shape["ba"] == 2 and mesh.shape["code"] == 2
    return jax.shard_map(
        paired_body if paired else body,
        mesh=mesh,
        in_specs=(
            P("code", "ba", "aa"),
            P("code", None, "ba", "aa"),
            P("code", "ba", "aa"),
            P("code", "ba", "aa"),
            P("code", "ba", "aa"),
            P(),
            P(),
        ),
        out_specs=(P("code", "ba", "aa"), P("code", None, "ba", "aa")),
        check_vma=False,
    )
```

```python
import jax
import jax.numpy as jnp
from jax import lax
from jax.experimental import pallas as pl
from jax.experimental.pallas import tpu as pltpu
from jax.sharding import PartitionSpec as P

W = 64
NF = 6
ITERS = 4


STORAGE = 0.5
LOWER_BOUND = 0.05
INJECTION = 2.0
PRODUCT_INDEX = 1.0
WELL_PRESSURE = -1.0
FLOW_RATE = 1.0
CHILLED_INFLOW = 0.1
TIME_STEP = 0.05


def extended(block, sides, width):
    for axis, dim in sides:
        count = lax.axis_size(axis)
        forward = [(i, i + 1) for i in range(count - 1)]
        backward = [(target, source) for source, target in forward]
        low = lax.ppermute(
            lax.slice_in_dim(block, block.shape[dim] - width, None, axis=dim), axis, forward
        )
        high = lax.ppermute(lax.slice_in_dim(block, 0, width, axis=dim), axis, backward)
        block = jnp.concatenate([low, block, high], axis=dim)
    return block


def from_partner(value, axis, stride):
    mask = 2**stride
    pairs = [(source, source ^ mask) for source in range(lax.axis_size(axis))]
    return lax.ppermute(value, axis, pairs)


def brine_flowability(matrix_heat_level):
    return 0.2 + 0.8 * jax.nn.sigmoid(6.0 * (matrix_heat_level - 0.5))


def harmonic(left_val, eastern_neighbor_number, face_mask):
    return (
        face_mask
        * 2.0
        * left_val
        * eastern_neighbor_number
        / (left_val + eastern_neighbor_number + 1.0 - face_mask)
    )


def accumulate(terms):
    result = terms[0]
    for term in terms[1:]:
        result = result + term
    return result


def sweep_weights():
    centre_val = (2.0 + LOWER_BOUND) / 2.0
    half_width = (2.0 - LOWER_BOUND) / 2.0
    quotient_number = centre_val / half_width
    rho_old = 1.0 / quotient_number
    chebyshev = [(1.0 / centre_val, 0.0)]
    for index_k in range(1, ITERS):
        rho_new = 1.0 / (2.0 * quotient_number - rho_old)
        chebyshev.append((2.0 * rho_new / half_width, rho_new * rho_old))
        rho_old = rho_new
    explicit = []
    for index_k in range(ITERS):
        if index_k % 2 == 0:
            explicit.append((TIME_STEP, 0.0))
        else:
            explicit.append((0.5 * TIME_STEP, -0.5))
    return (chebyshev, explicit)


def pressure_terms(center, beside_all):
    masks = [center[2] * beside_all[direction][2] for direction in range(6)]
    perm_faces = [
        harmonic(center[1], beside_all[direction][1], masks[direction]) for direction in range(6)
    ]
    mobility = []
    for direction in range(6):
        field_component = 5 + direction // 2
        if direction % 2 == 0:
            mobility.append(center[field_component] * masks[direction])
        else:
            mobility.append(beside_all[direction][field_component] * masks[direction])
    coefficient = [perm_faces[direction] * mobility[direction] for direction in range(6)]
    diagonal_entries = accumulate(coefficient) + STORAGE + center[4]
    forcing = center[3] + STORAGE * center[0]
    scaling = 1.0 / diagonal_entries
    outgoing = [
        perm_faces[direction] * (center[0] - beside_all[direction][0]) for direction in (0, 2, 4)
    ]
    return (coefficient, diagonal_entries, forcing, scaling, outgoing)


def heat_terms(center, beside_all):
    masks = [center[2] * beside_all[direction][2] for direction in range(6)]
    conduct_faces = [
        harmonic(center[1], beside_all[direction][1], masks[direction]) for direction in range(6)
    ]
    own_fluid = brine_flowability(center[0])
    fluid_faces = [
        harmonic(own_fluid, brine_flowability(beside_all[direction][0]), masks[direction])
        for direction in range(6)
    ]
    velocity = []
    for direction in range(6):
        field_component = 5 + direction // 2
        if direction % 2 == 0:
            velocity.append(center[field_component] * fluid_faces[direction])
        else:
            velocity.append(-beside_all[direction][field_component] * fluid_faces[direction])
    coefficient = [
        conduct_faces[direction] - jnp.minimum(velocity[direction], 0.0) for direction in range(6)
    ]
    outflow = accumulate([jnp.maximum(velocity[direction], 0.0) for direction in range(6)])
    diagonal_entries = accumulate(conduct_faces) + outflow + center[4]
    forcing = center[3]
    scaling = jnp.ones_like(diagonal_entries)
    outgoing = [fluid_faces[direction] for direction in (0, 2, 4)]
    return (coefficient, diagonal_entries, forcing, scaling, outgoing)


def crop(values, margin):
    row_count = values.shape[-2]
    col_count = values.shape[-1]
    return values[..., margin : row_count - margin, margin * W : col_count - margin * W]


def beside(values):
    row_count = values.shape[-2]
    col_count = values.shape[-1]
    inner_cols = col_count - 2 * W
    column_pos = lax.broadcasted_iota(jnp.int32, (row_count - 2, inner_cols), 1) % W
    lower_mask = (column_pos > 0).astype(values.dtype)
    upper_mask = (column_pos < W - 1).astype(values.dtype)
    center = values[..., 1 : row_count - 1, W : col_count - W]
    beside_all = [
        values[..., 2:, W : col_count - W],
        values[..., : row_count - 2, W : col_count - W],
        values[..., 1 : row_count - 1, 2 * W :],
        values[..., 1 : row_count - 1, : col_count - 2 * W],
        values[..., 1 : row_count - 1, W + 1 : col_count - W + 1] * upper_mask,
        values[..., 1 : row_count - 1, W - 1 : col_count - W - 1] * lower_mask,
    ]
    return (beside_all, center)


def extend(values, margin):
    row_ext = extended(values, (("ba", 1),), margin)
    return extended(row_ext, (("aa", 2),), margin * W)


def regroup_layout(received_block):
    components = received_block.shape[0]
    turned = jnp.transpose(received_block, (0, 3, 2, 1))
    return turned.reshape(
        components, received_block.shape[3], received_block.shape[2] * received_block.shape[1]
    )


def body(states, coupled, facies, injectors, producers, perm_table, cond_table):
    is_press = lax.axis_index("code") == 0
    own_field = states[0]
    row_count = own_field.shape[0]
    col_count = own_field.shape[1]
    lithology_lookup = jnp.where(is_press, perm_table, cond_table)
    other_table = jnp.where(is_press, cond_table, perm_table)
    own_classes = facies[0]
    property_field = accumulate(
        [jnp.where(own_classes == index_c, lithology_lookup[index_c], 0.0) for index_c in range(NF)]
    )
    other_property = accumulate(
        [jnp.where(own_classes == index_c, other_table[index_c], 0.0) for index_c in range(NF)]
    )
    inject_cells = injectors[0].astype(jnp.float32)
    produce_cells = producers[0].astype(jnp.float32)
    source = inject_cells * jnp.where(
        is_press, INJECTION, FLOW_RATE * CHILLED_INFLOW
    ) + produce_cells * jnp.where(is_press, PRODUCT_INDEX * WELL_PRESSURE, 0.0)
    well_sink = produce_cells * jnp.where(
        is_press, PRODUCT_INDEX, FLOW_RATE
    ) + inject_cells * jnp.where(is_press, 0.0, FLOW_RATE)
    inside = jnp.ones_like(own_field)
    stacked = jnp.concatenate(
        [
            jnp.stack([own_field, property_field, inside, source, well_sink]),
            coupled[0],
            other_property[None],
        ],
        axis=0,
    )
    halo_depth = 1
    widened_stack = extend(stacked, halo_depth)
    beside_all, center = beside(widened_stack)
    coefficient, diagonal_entries, forcing, scaling, outgoing_list = lax.cond(
        is_press, pressure_terms, heat_terms, center, beside_all
    )
    outgoing = jnp.stack([crop(face_item, halo_depth - 1) for face_item in outgoing_list])
    payload = outgoing[::-1].reshape(3, row_count, col_count // W, W)
    regrouped = regroup_layout(
        lax.all_to_all(payload, "ba", split_axis=3, concat_axis=1, tiled=True)
    )
    received = from_partner(regrouped, "code", 0)
    chebyshev, explicit = sweep_weights()
    present_iterate = own_field
    previous = None
    prev_depth = 0
    counter = 0
    for sweep_block in range(ITERS // halo_depth):
        widened = extend(present_iterate[None], halo_depth)[0]
        if previous is None:
            previous = widened
            prev_depth = halo_depth
        region = halo_depth
        region = region - 1
        around_v, center_v = beside(widened)
        index_shift = halo_depth - 1 - region
        applied = crop(diagonal_entries, index_shift) * center_v - accumulate(
            [
                crop(coefficient[direction], index_shift) * around_v[direction]
                for direction in range(6)
            ]
        )
        residual = crop(scaling, index_shift) * (crop(forcing, index_shift) - applied)
        weight_new = jnp.where(is_press, chebyshev[counter][0], explicit[counter][0])
        weight_old = jnp.where(is_press, chebyshev[counter][1], explicit[counter][1])
        updated = (
            center_v
            + weight_new * residual
            + weight_old * (center_v - crop(previous, prev_depth - region))
        )
        previous = widened
        prev_depth = region + 1
        widened = updated
        counter = counter + 1
        present_iterate = widened
    return (present_iterate[None], received[None])


TINY = 1e-30
LANES = 128
HALF = 64
XH = 4
VM = pl.BlockSpec(memory_space=pltpu.VMEM)
SM = pl.BlockSpec(memory_space=pltpu.SMEM)
HB = pl.BlockSpec(memory_space=pltpu.HBM)
UNROLL = 4
PARTS = 4
LEAN = pltpu.CompilerParams(vmem_limit_bytes=6 * 2**20)


def params(megabytes):
    return pltpu.CompilerParams(vmem_limit_bytes=megabytes * 2**20)


def cost(micros):
    return pl.CostEstimate(
        flops=int(micros * 1.15e9), bytes_accessed=int(micros * 3.6e6), transcendentals=0
    )


def in_vmem(shape):
    return pltpu.VMEM(shape, jnp.float32)


def held(value):
    return pltpu.with_memory_space_constraint(value, pltpu.VMEM)


def lanes_at(tile, base=0):
    return pl.ds(pl.multiple_of(base + tile * LANES, LANES), LANES)


def lane_index(shape):
    return lax.broadcasted_iota(jnp.int32, shape, len(shape) - 1)


def inverse(value):
    return pl.reciprocal(value, approx=False)


def face_mean(left, right):
    return 2.0 * left * right * inverse(jnp.maximum(left + right, TINY))


def flowability(level):
    return 0.2 + 0.8 * inverse(1.0 + jnp.exp(-6.0 * (level - 0.5)))


def half_turn(value):
    return pltpu.roll(value, HALF, 1)


def next_lane(value):
    return pltpu.roll(value, LANES - 1, 1)


def prev_lane(value):
    return pltpu.roll(value, 1, 1)


def next_row(value):
    return pltpu.roll(value, value.shape[0] - 1, 0)


def prev_row(value):
    return pltpu.roll(value, 1, 0)


def look_up(table, codes):
    value = jnp.zeros(codes.shape, jnp.float32)
    for index_c in range(NF):
        value = jnp.where(codes == index_c + 1, table[index_c], value)
    return value


def placed_pair(pair, is_low):
    blank = jnp.zeros((6, pair.shape[1]), pair.dtype)
    return jnp.where(
        is_low, jnp.concatenate([pair, blank], 0), jnp.concatenate([blank, pair], 0)
    )


def placed_row(row, is_low):
    blank = jnp.zeros((7, row.shape[1]), row.dtype)
    return jnp.where(is_low, jnp.concatenate([row, blank], 0), jnp.concatenate([blank, row], 0))


def rim_slots(is_low, state, codes, f0, f1, f2, inject, produce):
    def pair(value):
        return jnp.where(is_low, value[6:8], value[0:2])

    def near(one, two):
        value = jnp.concatenate([one[0:8], two[0:8]], 0)
        return jnp.concatenate(
            [
                jnp.where(is_low, value[7:8], value[0:1]),
                jnp.where(is_low, value[15:16], value[8:9]),
            ],
            0,
        )

    return [
        pair(state),
        pair((codes + 1).astype(jnp.float32)),
        pair(f0),
        near(f1, f2),
        near(inject.astype(jnp.float32), produce.astype(jnp.float32)),
    ]


def corner_kernel(where_ref, st, cp, fa, ij, pr, corners, state, field, codes, sems):
    is_low = where_ref[1] == 0
    rows, cols = st.shape[1], st.shape[2]
    wide = XH * W
    at = pl.ds(pl.multiple_of(jnp.where(is_low, rows - 8, 0), 8), 8)
    copies = []
    for side, start in enumerate((0, cols - wide)):
        lanes = pl.ds(start, wide)
        for source, target in (
            (st.at[0, at, lanes], state.at[side]),
            (cp.at[0, :, at, lanes], field.at[side]),
            (fa.at[0, at, lanes], codes.at[side, 0]),
            (ij.at[0, at, lanes], codes.at[side, 1]),
            (pr.at[0, at, lanes], codes.at[side, 2]),
        ):
            copy = pltpu.make_async_copy(source, target, sems.at[len(copies)])
            copy.start()
            copies.append(copy)
    for copy in copies:
        copy.wait()
    for side in range(2):
        slots = rim_slots(
            is_low, state[side], codes[side, 0], field[side, 0], field[side, 1], field[side, 2],
            codes[side, 1], codes[side, 2],
        )
        for index, slot in enumerate(slots):
            start = (2 * index + side) * wide
            corners[:, start : start + wide] = slot


def edges_kernel(where_ref, st, cp, fa, ij, pr, to_right, to_left, across):
    is_low = where_ref[1] == 0
    rows, cols = st.shape[1], st.shape[2]
    wide = XH * W
    for target, start in ((to_right, cols - wide), (to_left, 0)):
        at = slice(start, start + wide)
        parts = [
            st[0, :, at],
            (fa[0, :, at] + 1).astype(jnp.float32),
            cp[0, 0, :, at],
            cp[0, 1, :, at],
            cp[0, 2, :, at],
            ij[0, :, at].astype(jnp.float32),
            pr[0, :, at].astype(jnp.float32),
        ]
        for index, part in enumerate(parts):
            target[:, index * wide : (index + 1) * wide] = part
    rim = pl.ds(pl.multiple_of(jnp.where(is_low, rows - 8, 0), 8), 8)
    slots = rim_slots(
        is_low, st[0, rim, :], fa[0, rim, :], cp[0, 0, rim, :], cp[0, 1, rim, :],
        cp[0, 2, rim, :], ij[0, rim, :], pr[0, rim, :],
    )
    for index, slot in enumerate(slots):
        across[:, index * cols : (index + 1) * cols] = slot


def pack_kernel(right_in, left_in, corners, to_right, to_left):
    wide = XH * W
    for side, (source, target) in enumerate(((left_in, to_left), (right_in, to_right))):
        target[:, : 7 * wide] = source[...]
        target[:, 7 * wide :] = jnp.zeros((32, LANES), jnp.float32)
        for index in range(5):
            for row in range(2):
                for half in range(2):
                    start = (2 * index + side) * wide + half * LANES
                    place = index * 4 + row * 2 + half
                    target[place : place + 1, 7 * wide :] = corners[
                        row : row + 1, start : start + LANES
                    ]


def put_cells(refs, is_press, tables, e, rows, cells):
    v0, prop, rock, c0, c1, c2, src, snk = refs
    state, codes, f0, f1, f2, inject, produce = cells
    v0[e + 1, rows, :] = state
    prop[e + 1, rows, :] = look_up(tables[0], codes)
    if is_press is not True:
        rock[e + 1, rows, :] = look_up(tables[1], codes)
    c0[e + 1, rows, :] = f0
    c1[e + 1, rows, :] = f1
    c2[e + 1, rows, :] = f2
    if is_press is True:
        src[e + 1, rows, :], snk[e + 1, rows, :] = 2.0 * inject - produce, produce
    elif is_press is False:
        src[e + 1, rows, :], snk[e + 1, rows, :] = 0.1 * inject, produce + inject
    else:
        src[e + 1, rows, :] = jnp.where(is_press, 2.0 * inject - produce, 0.1 * inject)
        snk[e + 1, rows, :] = jnp.where(is_press, produce, produce + inject)


def class_tables(is_press, perm_ref, cond_ref):
    perm = [perm_ref[index_c] for index_c in range(NF)]
    own = [jnp.where(is_press, perm[index_c], cond_ref[index_c]) for index_c in range(NF)]
    return own, perm


def fill_own(refs, is_press, tables, own_rows, raw):
    st, cp, fa, ij, pr = raw

    def fill(t, carry):
        at = lanes_at(t)
        cells = (
            st[0, :, at], fa[0, :, at] + 1, cp[0, 0, :, at], cp[0, 1, :, at], cp[0, 2, :, at],
            ij[0, :, at].astype(jnp.float32), pr[0, :, at].astype(jnp.float32),
        )
        put_cells(refs, is_press, tables, t + XH // 2, own_rows, cells)
        return carry

    lax.fori_loop(0, st.shape[2] // LANES, fill, 0, unroll=8)


def turn_kernel(
    where_ref, perm_ref, cond_ref, st, cp, fa, ij, pr, corners,
    own, other, rim, fluid, v0, prop, rock, c0, c1, c2, src, snk,
):
    del corners
    is_heat = where_ref[0] == 1
    is_low = where_ref[1] == 0
    own_rows = pl.ds(pl.multiple_of(jnp.where(is_low, 0, 8), 8), 32)
    groups = st.shape[2] // (4 * LANES)
    extra = groups * 2 * LANES
    row = lax.broadcasted_iota(jnp.int32, (32, LANES), 0)

    def step(group, rims):
        tall = jnp.concatenate(
            [st[0, :, lanes_at(4 * group + q)] for q in range(4)], axis=0
        )
        tall = jnp.where(is_heat, flowability(tall), tall)
        for q in range(4):
            fluid[4 * group + q + XH // 2 + 1, own_rows, :] = tall[32 * q : 32 * q + 32]
        turned = tall.T
        for par in range(2):
            low = turned[par * HALF : par * HALF + 32]
            high = turned[par * HALF + 32 : par * HALF + 64]
            own[:, lanes_at(group, par * groups * LANES)] = jnp.where(is_low, low, high)
            away = jnp.where(is_low, high, low)
            rim = high[0:1]

            other[:, lanes_at(group, par * groups * LANES)] = away
            rims = jnp.where(row == par * groups + group, rim, rims)
        return rims

    rims = lax.fori_loop(0, groups, step, jnp.zeros((32, LANES), jnp.float32), unroll=8)
    rim[:, :LANES] = jnp.where(is_low, rims, 0.0)
    other[:, extra : extra + LANES] = jnp.where(is_low, 0.0, rims)
    refs = (v0, prop, rock, c0, c1, c2, src, snk)
    tables = class_tables(jnp.logical_not(is_heat), perm_ref, cond_ref)

    @pl.when(is_heat)
    def _():
        fill_own(refs, False, tables, own_rows, (st, cp, fa, ij, pr))


def plane_kernel(where_ref, from_right, own_in, *rest):
    del own_in
    own = rest[-1]
    is_heat = where_ref[0] == 1
    is_low = where_ref[1] == 0
    wide = XH * W
    value = from_right[:, 0:LANES]
    inside = from_right[:, wide : wide + LANES] > 0.5
    value = jnp.where(is_heat, jnp.where(inside, flowability(value), 0.0), value)
    tall = jnp.concatenate([value, value, jnp.zeros((64, LANES), jnp.float32)], 0).T
    low, high = tall[0:32], tall[32:64]
    keep = lane_index((32, LANES)) < 32
    own[:, own.shape[1] - LANES :] = jnp.where(keep == is_low, low, high)


def send_kernel(boundary_in, rim, boundary):
    del boundary_in
    first = boundary.shape[1] - 16 * LANES
    for index in range(16):
        start = first + index * LANES
        boundary[:, start : start + LANES] = rim[2 * index : 2 * index + 2, LANES:]


def sweep(tiles, coeffs, force, diag, now, last, target, weight, pull, rows=slice(None)):
    first, stop = tiles
    shape = now[0, rows].shape
    low_lanes = lane_index(shape) < HALF

    def step(e, carry):
        before, here = carry
        tall = now[e + 1]
        value = tall[rows]
        after = half_turn(now[e + 2, rows])
        total = force[e + 1, rows]
        total += coeffs[0, e + 1, rows] * next_row(tall)[rows]
        total += coeffs[1, e + 1, rows] * prev_row(tall)[rows]
        total += coeffs[2, e + 1, rows] * jnp.where(low_lanes, here, after)
        total += coeffs[3, e + 1, rows] * jnp.where(low_lanes, before, here)
        total += coeffs[4, e + 1, rows] * next_lane(value)
        total += coeffs[5, e + 1, rows] * prev_lane(value)
        if diag is None:
            result = (1.0 + pull - weight) * value + weight * total
        else:
            result = (1.0 + pull) * value + weight * (total - diag[e + 1, rows] * value)
        if pull != 0.0:
            result -= pull * last[e + 1, rows]
        target(e, result)
        return here, after

    lax.fori_loop(
        first, stop, step,
        (half_turn(now[first, rows]), half_turn(now[first + 1, rows])),
        unroll=stop - first,
    )


def store_in(ref):
    def put(e, value):
        ref[e + 1] = value

    return put


def rim_cells(is_low, read):
    def pair(index):
        return placed_pair(jnp.concatenate([read(index, 0), read(index, 1)], 0), is_low)

    def near(index, row):
        return placed_row(read(index, row), is_low)

    return (
        pair(0), pair(1).astype(jnp.int32), pair(2),
        near(3, 0), near(3, 1), near(4, 0), near(4, 1),
    )


def rim_rows(is_low):
    return pl.ds(pl.multiple_of(jnp.where(is_low, 32, 0), 8), 8)


def put_level(fluid, cells, e, rows):
    prop, state = cells[1][e + 1, rows, :], cells[0][e + 1, rows, :]
    fluid[e + 1, rows, :] = jnp.where(prop > 0.0, flowability(state), 0.0)


def clear(refs, places):
    for ref in refs:
        for e in places:
            ref[e] = jnp.zeros(ref.shape[1:], jnp.float32)


def flow_pair(mean, flow, field):
    speed = flow * field
    gain = mean + jnp.maximum(speed, 0.0)
    return gain, gain - speed


def heat_b_terms(cells, made, e):
    v0, prop, rock, c0, c1, c2, src, snk = cells
    coeffs, force, diag, fluid = made
    value, level = prop[e + 1], fluid[e + 1]
    not_last = lane_index(value.shape) % W != W - 1
    gain, loss = flow_pair(
        face_mean(value, jnp.where(not_last, next_lane(value), 0.0)),
        face_mean(level, jnp.where(not_last, next_lane(level), 0.0)),
        c2[e + 1],
    )
    coeffs[4, e + 1] = loss
    coeffs[5, e + 1] = prev_lane(gain)
    diag[e + 1] = snk[e + 1] + gain + prev_lane(loss)


def face_terms(cells, made, is_press, ranges):
    v0, prop, rock, c0, c1, c2, src, snk = cells
    coeffs, force, diag, fluid = made
    shape = v0.shape[1:]
    lane = lane_index(shape)
    low_lanes = lane < HALF
    not_last = lane % W != W - 1
    blank = jnp.zeros(shape, jnp.float32)

    def run(step, first, stop, start):
        if stop - first > 8:
            unroll = max(n for n in range(1, 10) if (stop - first) % n == 0)
            return lax.fori_loop(first, stop, step, start, unroll=unroll)
        for e in range(first, stop):
            start = step(e, start)
        return start

    def beside(value, turns, after):
        return (
            jnp.where(low_lanes, turns[0], after[0]),
            jnp.where(not_last, turns[1], 0.0),
        )

    def press_range(first, stop):
        def turns(e):
            value = prop[e + 1]
            return half_turn(value), next_lane(value)

        def along(e, now, after):
            value = prop[e + 1]
            x_side, b_side = beside(value, now, after)
            return face_mean(value, x_side) * c1[e + 1], face_mean(value, b_side) * c2[e + 1]

        def close(e, before, plus, turned):
            value = prop[e + 1]
            plus = [face_mean(value, next_row(value)) * c0[e + 1], *plus]
            minus = [prev_row(plus[0]), jnp.where(low_lanes, before, turned[0]), turned[1]]
            scale = inverse(accumulate(plus + minus) + STORAGE + snk[e + 1])
            for dim in range(3):
                coeffs[2 * dim, e + 1] = scale * plus[dim]
                coeffs[2 * dim + 1, e + 1] = scale * minus[dim]
            force[e + 1] = scale * (src[e + 1] + STORAGE * v0[e + 1])

        def step(e, carry):
            before, plus, turned, now, after = carry
            close(e - 1, before, plus, turned)
            later = turns(e + 2)
            fresh = along(e, now, after)
            return turned[0], fresh, (half_turn(fresh[0]), prev_lane(fresh[1])), after, later

        now, after = turns(first), turns(first + 1)
        before = blank
        if first > 0:
            before = half_turn(along(first - 1, turns(first - 1), now)[0])
        fresh = along(first, now, after)
        carry = (
            before, fresh, (half_turn(fresh[0]), prev_lane(fresh[1])), after, turns(first + 2)
        )
        before, plus, turned, _, _ = run(step, first + 1, stop, carry)
        close(stop - 1, before, plus, turned)

    def heat_range(first, stop):
        def turns(e):
            return half_turn(prop[e + 1]), half_turn(fluid[e + 1])

        def along(e, now, after):
            value, level = prop[e + 1], fluid[e + 1]
            return flow_pair(
                face_mean(value, jnp.where(low_lanes, now[0], after[0])),
                face_mean(level, jnp.where(low_lanes, now[1], after[1])),
                c1[e + 1],
            )

        def close(e, before, turned):
            value, level = prop[e + 1], fluid[e + 1]
            gain, loss = flow_pair(
                face_mean(value, next_row(value)), face_mean(level, next_row(level)), c0[e + 1]
            )
            coeffs[0, e + 1] = loss
            coeffs[1, e + 1] = prev_row(gain)
            coeffs[3, e + 1] = jnp.where(low_lanes, before[0], turned[0])
            total = diag[e + 1] + gain + prev_row(loss)
            diag[e + 1] = total + turned[2] + jnp.where(low_lanes, before[1], turned[1])

        def opened(e, now, after):
            gain, loss = along(e, now, after)
            coeffs[2, e + 1] = loss
            return half_turn(gain), half_turn(loss), gain

        def step(e, carry):
            before, turned, now, after = carry
            close(e - 1, before, turned)
            later = turns(e + 2)
            return turned[:2], opened(e, now, after), after, later

        def b_steps(first, stop):
            def b_step(e, carry):
                heat_b_terms(cells, made, e)
                return carry

            if stop - first > 8:
                lax.fori_loop(first, stop, b_step, 0, unroll=8)
            else:
                for e in range(first, stop):
                    b_step(e, 0)

        b_steps(first, stop)
        now, after = turns(first), turns(first + 1)
        before = (blank, blank)
        if first > 0:
            gain, loss = along(first - 1, turns(first - 1), now)
            before = half_turn(gain), half_turn(loss)
        carry = (before, opened(first, now, after), after, turns(first + 2))
        before, turned, _, _ = run(step, first + 1, stop, carry)
        close(stop - 1, before, turned)

    @pl.when(is_press)
    def _():
        for first, stop in ranges:
            press_range(first, stop)

    @pl.when(jnp.logical_not(is_press))
    def _():
        for first, stop in ranges:
            heat_range(first, stop)


def inner_kernel(where_ref, perm_ref, cond_ref, across, st, cp, fa, ij, pr, *refs):
    coeffs, force, diag, fluid = refs[-12:-8]
    cells = refs[-8:]
    is_press = where_ref[0] == 0
    is_low = where_ref[1] == 0
    ext = cells[0].shape[0] - 2
    side = XH // 2
    tiles = ext - XH
    cols = tiles * LANES
    rows = rim_rows(is_low)
    tables = class_tables(is_press, perm_ref, cond_ref)
    clear(tuple(cells[:3]) + (fluid,), (0, 1, 2, ext - 1, ext, ext + 1))

    @pl.when(is_press)
    def _():
        own_rows = pl.ds(pl.multiple_of(jnp.where(is_low, 0, 8), 8), 32)
        fill_own(cells, True, tables, own_rows, (st, cp, fa, ij, pr))

    def fill(t, carry):
        read = lambda index, row: across[row : row + 1, lanes_at(t, index * cols)]
        put_cells(cells, is_press, tables, t + side, rows, rim_cells(is_low, read))
        put_level(fluid, cells, t + side, rows)
        return carry

    lax.fori_loop(0, tiles, fill, 0, unroll=8)
    made = (coeffs, force, diag, fluid)
    face_terms(cells, made, is_press, [(side, ext - side)])


def main_kernel(where_ref, perm_ref, cond_ref, from_left, from_right, *refs):
    v1, v2, boundary = refs[12:15]
    coeffs, force, diag, fluid = refs[15:19]
    cells = refs[19:]
    v0 = cells[0]
    is_press = where_ref[0] == 0
    is_low = where_ref[1] == 0
    ext = v0.shape[0] - 2
    wide = XH * W
    side = XH // 2
    own_rows = pl.ds(pl.multiple_of(jnp.where(is_low, 0, 8), 8), 32)
    tables = class_tables(is_press, perm_ref, cond_ref)

    for e, message, at in (
        (0, from_left, 0), (1, from_left, 1), (ext - 2, from_right, 0), (ext - 1, from_right, 1)
    ):
        parts = [message[:, lanes_at(at, index * wide)] for index in range(7)]
        parts[1] = parts[1].astype(jnp.int32)
        put_cells(cells, is_press, tables, e, own_rows, parts)
        corner = message[:, 7 * wide :]
        read = lambda index, row, corner=corner, at=at: corner[
            index * 4 + row * 2 + at : index * 4 + row * 2 + at + 1
        ]
        put_cells(cells, is_press, tables, e, rim_rows(is_low), rim_cells(is_low, read))
        put_level(fluid, cells, e, slice(None))
    clear((v1, v2), (0, ext + 1))
    clear((v2,), (1, ext))
    for e in (0, ext - 1):
        boundary[:, e * LANES : (e + 1) * LANES] = jnp.zeros((2, LANES), jnp.float32)
    made = (coeffs, force, diag, fluid)
    face_terms(cells, made, is_press, [(0, side + 1), (ext - side - 1, ext)])
    chebyshev, explicit = sweep_weights()
    src = cells[6]

    is_high = jnp.logical_not(is_low)

    for chosen, weights, centre, drive in (
        (is_press, chebyshev, None, force),
        (jnp.logical_not(is_press), explicit, diag, src),
    ):

        @pl.when(chosen)
        def _(weights=weights, centre=centre, force=drive):
            (w0, u0), (w1, u1) = weights[:2]
            sweep((0, ext), coeffs, force, centre, v0, v0, store_in(v1), w0, u0)
            for placed, rows, edge in (
                (is_low, slice(0, 32), slice(30, 32)), (is_high, slice(8, 40), slice(0, 2))
            ):

                @pl.when(placed)
                def _(rows=rows, edge=edge):
                    def put(e, value):
                        v2[e + 1, rows] = value
                        boundary[:, lanes_at(e)] = value[edge]

                    sweep((1, ext - 1), coeffs, force, centre, v1, v0, put, w1, u1, rows)


def finish_kernel(
    where_ref, v1, v2_in, received_in, coeffs, force, src, diag, boundary, edge, rim,
    out_ref, now, received, later, out, tile, sems,
):
    del v2_in, received_in
    is_press = where_ref[0] == 0
    is_low = where_ref[1] == 0
    ext = now.shape[0] - 2
    side = XH // 2
    tiles = ext - XH
    rows = rim_rows(is_low)
    clear((later,), (0, ext + 1))
    lane = lane_index((32, LANES))
    mine = rim[:, LANES:]
    start = boundary.shape[1] - 16 * LANES
    theirs = jnp.concatenate(
        [boundary[:, start + index * LANES : start + (index + 1) * LANES] for index in range(16)],
        0,
    )
    plane = jnp.where(
        is_low,
        jnp.where(lane < 32, mine, theirs),
        jnp.where(lane < 32, pltpu.roll(theirs, 96, 1), pltpu.roll(mine, 32, 1)),
    )
    here = edge[0]
    beside = jnp.where(lane < HALF, half_turn(here), half_turn(plane))
    tile[...] = jnp.where(is_press, face_mean(here, beside), edge[1] * (here - beside))
    last_tile = pl.ds((tiles - 1) * LANES, LANES)
    tile_copy = pltpu.make_async_copy(tile, received.at[0, 1, :, last_tile], sems.at[PARTS])
    tile_copy.start()

    def fill(e, carry):
        now[e + 1, rows, :] = placed_pair(boundary[:, lanes_at(e)], is_low)
        return carry

    lax.fori_loop(0, ext, fill, 0, unroll=17)
    chebyshev, explicit = sweep_weights()

    def put_out(e, value):
        out[:, lanes_at(e - side)] = value

    is_high = jnp.logical_not(is_low)
    for chosen, weights, centre, drive in (
        (is_press, chebyshev, None, force),
        (jnp.logical_not(is_press), explicit, diag, src),
    ):

        @pl.when(chosen)
        def _(weights=weights, centre=centre, force=drive):
            (w2, u2), (w3, u3) = weights[2:]
            sweep((1, ext - 1), coeffs, force, centre, now, v1, store_in(later), w2, u2)
            for placed, rows in ((is_low, slice(0, 32)), (is_high, slice(8, 40))):

                @pl.when(placed)
                def _(rows=rows):
                    part = tiles // PARTS
                    copies = []
                    for index in range(PARTS):
                        first = side + index * part
                        sweep(
                            (first, first + part), coeffs, force, centre, later, now, put_out,
                            w3, u3, rows,
                        )
                        at = pl.ds(index * part * LANES, part * LANES)
                        copy = pltpu.make_async_copy(
                            out.at[:, at], out_ref.at[0, :, at], sems.at[index]
                        )
                        copy.start()
                        copies.append(copy)
                    for copy in copies:
                        copy.wait()

    tile_copy.wait()


def regrouped(pieces):
    lane = lane_index(pieces[0].shape)
    result = []
    for q in range(4):
        value = None
        for place in range(4):
            piece = pieces[place]
            if place != q:
                piece = pltpu.roll(piece, ((place - q) * 32) % LANES, 1)
            value = piece if value is None else jnp.where(lane >= place * 32, piece, value)
        result.append(value)
    return result


def faces_kernel(
    where_ref, own, other, own_rim, rock, out_ref, edge, field, rim, out, sems
):
    is_press = where_ref[0] == 0
    is_low = where_ref[1] == 0
    tiles = out.shape[2] // LANES
    groups = tiles // 4
    side = XH // 2
    extra = groups * 2 * LANES

    def ordered(mine, theirs):
        return [jnp.where(is_low, mine, theirs), jnp.where(is_low, theirs, mine)]

    pieces = []
    for par in range(2):
        pieces += ordered(
            own_rim[par * groups : (par + 1) * groups, :LANES],
            other[par * groups : (par + 1) * groups, extra : extra + LANES],
        )
    for q, value in enumerate(regrouped(pieces)):
        rim[q] = value
    lane = lane_index((32, LANES))
    field[tiles] = jnp.zeros(field.shape[1:], jnp.float32)

    def gather(group, carry):
        pieces = []
        for par in range(2):
            at = lanes_at(group, par * groups * LANES)
            pieces += ordered(own[:, at], other[:, at])
        for q, value in enumerate(regrouped(pieces)):
            field[4 * group + q, 0:32, :] = value
            field[4 * group + q, 32:33, :] = rim[q, pl.ds(group, 1), :]
        return carry

    lax.fori_loop(0, groups, gather, 0, unroll=8)
    low_lanes = lane < HALF
    not_last = lane % W != W - 1

    def around(t, turned):
        value = field[t]
        here = value[0:32]
        after = half_turn(field[t + 1, 0:32, :])
        others = next_row(value)[0:32], jnp.where(low_lanes, turned, after), next_lane(here)
        return here, others, after

    def press(t, carry):
        here, others, after = around(t, carry)
        others = (others[0], others[1], jnp.where(not_last, others[2], 0.0))
        for dim in range(3):
            out[dim, :, lanes_at(t)] = face_mean(here, others[dim])
        return after

    def heat(t, carry):
        here, others, after = around(t, carry[0])
        stone = rock[t + side + 1, own_rows, :]
        stone_after = half_turn(rock[t + side + 2, own_rows, :])
        rim_row = jnp.where(is_low, rock[t + side + 1, 32:33, :], 0.0)
        near = (
            jnp.where(last_row, rim_row, next_row(stone)),
            jnp.where(low_lanes, carry[1], stone_after),
            jnp.where(not_last, next_lane(stone), 0.0),
        )
        for dim in range(3):
            mean = face_mean(stone, near[dim])
            out[dim, :, lanes_at(t)] = mean * (here - others[dim])
        return after, stone_after

    own_rows = pl.ds(pl.multiple_of(jnp.where(is_low, 0, 8), 8), 32)
    last_row = lax.broadcasted_iota(jnp.int32, (32, LANES), 0) == 31
    part = tiles // PARTS
    copies = []
    edge[0] = field[tiles - 1, 0:32, :]
    stone = rock[tiles - 1 + side + 1, own_rows, :]
    stone_after = half_turn(rock[tiles + side + 1, own_rows, :])
    edge[1] = face_mean(stone, jnp.where(low_lanes, half_turn(stone), stone_after))
    for index in range(PARTS):
        first = index * part

        @pl.when(is_press)
        def _(first=first):
            start = half_turn(field[first, 0:32, :])
            lax.fori_loop(first, first + part, press, start, unroll=16)

        @pl.when(jnp.logical_not(is_press))
        def _(first=first):
            start = half_turn(field[first, 0:32, :]), half_turn(rock[first + side + 1, own_rows, :])
            lax.fori_loop(first, first + part, heat, start, unroll=16)

        at = pl.ds(first * LANES, part * LANES)
        copy = pltpu.make_async_copy(out.at[:, :, at], out_ref.at[0, :, :, at], sems.at[index])
        copy.start()
        copies.append(copy)
    for copy in copies:
        copy.wait()


def paired_body(states, coupled, facies, injectors, producers, perm_table, cond_table):
    rows, cols = states.shape[1], states.shape[2]
    tiles = cols // LANES
    ext = tiles + XH
    wide = XH * W
    groups = tiles // 4
    loaded = [held(value) for value in (states, coupled, facies, injectors, producers)]
    place = jnp.stack([lax.axis_index("code"), lax.axis_index("ba")]).astype(jnp.int32)
    count = lax.axis_size("aa")
    up = [(i, i + 1) for i in range(count - 1)]
    down = [(b, a) for a, b in up]
    swap = [(0, 1), (1, 0)]
    opposite = [(0, 3), (1, 2), (2, 1), (3, 0)]
    f32, i32 = jnp.float32, jnp.int32
    states, coupled, facies, injectors, producers = [
        pltpu.with_memory_space_constraint(value, pltpu.HBM)
        for value in (states, coupled, facies, injectors, producers)
    ]

    corners = pl.pallas_call(
        corner_kernel,
        out_shape=in_vmem((2, 10 * wide)),
        in_specs=[SM] + [HB] * 5,
        out_specs=VM,
        scratch_shapes=[
            pltpu.VMEM((2, 8, wide), f32),
            pltpu.VMEM((2, 3, 8, wide), f32),
            pltpu.VMEM((2, 3, 8, wide), i32),
            pltpu.SemaphoreType.DMA((10,)),
        ],
        compiler_params=LEAN,
        cost_estimate=cost(1),
        name="corner",
    )(place, states, coupled, facies, injectors, producers)
    corners = held(lax.ppermute(corners, "ba", swap))
    to_right, to_left, across = pl.pallas_call(
        edges_kernel,
        out_shape=[
            in_vmem((rows, 7 * wide)),
            in_vmem((rows, 7 * wide)),
            in_vmem((2, 5 * cols)),
        ],
        in_specs=[SM] + [VM] * 5,
        out_specs=[VM] * 3,
        compiler_params=LEAN,
        cost_estimate=cost(2),
        name="edges",
    )(place, *loaded)
    from_across = held(lax.ppermute(across, "ba", swap))
    to_right, to_left = pl.pallas_call(
        pack_kernel,
        out_shape=[in_vmem((rows, 7 * wide + LANES))] * 2,
        in_specs=[VM] * 3,
        out_specs=[VM] * 2,
        compiler_params=LEAN,
        cost_estimate=cost(1),
        name="pack",
    )(to_right, to_left, corners)
    from_left = held(lax.ppermute(to_right, "aa", up))
    from_right = held(lax.ppermute(to_left, "aa", down))

    field = (ext + 2, rows + 8, LANES)
    turned_own, turned_other, rim, fluid, *cells = pl.pallas_call(
        turn_kernel,
        out_shape=[
            in_vmem((32, 2 * groups * LANES)),
            in_vmem((32, (2 * groups + 1) * LANES)),
            in_vmem((32, 2 * LANES)),
        ]
        + [in_vmem(field)] * 9,
        in_specs=[SM] * 3 + [VM] * 6,
        out_specs=[VM] * 12,
        compiler_params=params(2),
        cost_estimate=cost(2.5),
        name="turn",
    )(
        place, perm_table, cond_table, *loaded, to_left,
    )
    other = held(lax.ppermute(turned_other, ("code", "ba"), opposite))
    own = held(lax.ppermute(turned_own, "code", swap))
    coeffs, force, diag, fluid, *cells = pl.pallas_call(
        inner_kernel,
        out_shape=[in_vmem((6,) + field)] + [in_vmem(field)] * 11,
        in_specs=[SM] * 3 + [VM] * 15,
        out_specs=[VM] * 12,
        input_output_aliases={9 + index: 3 + index for index in range(9)},
        compiler_params=params(2),
        cost_estimate=cost(10),
        name="inner",
    )(place, perm_table, cond_table, from_across, *loaded, fluid, *cells)
    rim = pl.pallas_call(
        plane_kernel,
        out_shape=in_vmem(rim.shape),
        in_specs=[SM] + [VM] * 4,
        out_specs=VM,
        input_output_aliases={2: 0},
        compiler_params=LEAN,
        cost_estimate=cost(1),
        name="plane",
    )(place, from_right, rim, from_left, force)
    rim = held(lax.ppermute(rim, "code", swap))

    v1, v2, boundary, coeffs, force, diag, fluid, *cells = pl.pallas_call(
        main_kernel,
        out_shape=[in_vmem(field), in_vmem(field), in_vmem((2, (ext + 16) * LANES))]
        + [in_vmem((6,) + field)]
        + [in_vmem(field)] * 11,
        in_specs=[SM] * 3 + [VM] * 14,
        out_specs=[VM] * 15,
        input_output_aliases={5 + index: 3 + index for index in range(12)},
        compiler_params=params(2),
        cost_estimate=cost(10),
        name="main",
    )(
        place, perm_table, cond_table, from_left, from_right,
        coeffs, force, diag, fluid, *cells,
    )
    boundary = pl.pallas_call(
        send_kernel,
        out_shape=in_vmem(boundary.shape),
        in_specs=[VM] * 2,
        out_specs=VM,
        input_output_aliases={0: 0},
        compiler_params=LEAN,
        cost_estimate=cost(1),
        name="send",
    )(boundary, rim)
    boundary = held(lax.ppermute(boundary, "ba", swap))
    received, edge = pl.pallas_call(
        faces_kernel,
        out_shape=[jax.ShapeDtypeStruct(coupled.shape, f32), in_vmem((2, 32, LANES))],
        in_specs=[SM] + [VM] * 4,
        out_specs=[HB, VM],
        scratch_shapes=[
            pltpu.VMEM((tiles + 1, rows + 8, LANES), f32),
            pltpu.VMEM((4, groups, LANES), f32),
            pltpu.VMEM(coupled.shape[1:], f32),
            pltpu.SemaphoreType.DMA((PARTS,)),
        ],
        compiler_params=params(8),
        cost_estimate=cost(6),
        name="faces",
    )(place, own, other, rim, cells[2])
    received = pltpu.with_memory_space_constraint(received, pltpu.HBM)
    stepped, _, received = pl.pallas_call(
        finish_kernel,
        out_shape=[
            jax.ShapeDtypeStruct(states.shape, f32),
            in_vmem(field),
            jax.ShapeDtypeStruct(coupled.shape, f32),
        ],
        in_specs=[SM] + [VM] * 2 + [HB] + [VM] * 7,
        out_specs=[HB, VM, HB],
        scratch_shapes=[
            pltpu.VMEM(field, f32),
            pltpu.VMEM(states.shape[1:], f32),
            pltpu.VMEM((32, LANES), f32),
            pltpu.SemaphoreType.DMA((PARTS + 1,)),
        ],
        input_output_aliases={2: 1, 3: 2},
        compiler_params=params(5),
        cost_estimate=cost(6),
        name="finish",
    )(place, v1, v2, received, coeffs, force, cells[6], diag, boundary, edge, rim)
    return (stepped, received)


def solution(mesh):
    paired = mesh.shape["ba"] == 2 and mesh.shape["code"] == 2
    return jax.shard_map(
        paired_body if paired else body,
        mesh=mesh,
        in_specs=(
            P("code", "ba", "aa"),
            P("code", None, "ba", "aa"),
            P("code", "ba", "aa"),
            P("code", "ba", "aa"),
            P("code", "ba", "aa"),
            P(),
            P(),
        ),
        out_specs=(P("code", "ba", "aa"), P("code", None, "ba", "aa")),
        check_vma=False,
    )
```

```python
import jax
import jax.numpy as jnp
from jax import lax
from jax.experimental import pallas as pl
from jax.experimental.pallas import tpu as pltpu
from jax.sharding import PartitionSpec as P

W = 64
NF = 6
ITERS = 4


STORAGE = 0.5
LOWER_BOUND = 0.05
INJECTION = 2.0
PRODUCT_INDEX = 1.0
WELL_PRESSURE = -1.0
FLOW_RATE = 1.0
CHILLED_INFLOW = 0.1
TIME_STEP = 0.05


def extended(block, sides, width):
    for axis, dim in sides:
        count = lax.axis_size(axis)
        forward = [(i, i + 1) for i in range(count - 1)]
        backward = [(target, source) for source, target in forward]
        low = lax.ppermute(
            lax.slice_in_dim(block, block.shape[dim] - width, None, axis=dim), axis, forward
        )
        high = lax.ppermute(lax.slice_in_dim(block, 0, width, axis=dim), axis, backward)
        block = jnp.concatenate([low, block, high], axis=dim)
    return block


def from_partner(value, axis, stride):
    mask = 2**stride
    pairs = [(source, source ^ mask) for source in range(lax.axis_size(axis))]
    return lax.ppermute(value, axis, pairs)


def brine_flowability(matrix_heat_level):
    return 0.2 + 0.8 * jax.nn.sigmoid(6.0 * (matrix_heat_level - 0.5))


def harmonic(left_val, eastern_neighbor_number, face_mask):
    return (
        face_mask
        * 2.0
        * left_val
        * eastern_neighbor_number
        / (left_val + eastern_neighbor_number + 1.0 - face_mask)
    )


def accumulate(terms):
    result = terms[0]
    for term in terms[1:]:
        result = result + term
    return result


def sweep_weights():
    centre_val = (2.0 + LOWER_BOUND) / 2.0
    half_width = (2.0 - LOWER_BOUND) / 2.0
    quotient_number = centre_val / half_width
    rho_old = 1.0 / quotient_number
    chebyshev = [(1.0 / centre_val, 0.0)]
    for index_k in range(1, ITERS):
        rho_new = 1.0 / (2.0 * quotient_number - rho_old)
        chebyshev.append((2.0 * rho_new / half_width, rho_new * rho_old))
        rho_old = rho_new
    explicit = []
    for index_k in range(ITERS):
        if index_k % 2 == 0:
            explicit.append((TIME_STEP, 0.0))
        else:
            explicit.append((0.5 * TIME_STEP, -0.5))
    return (chebyshev, explicit)


def pressure_terms(center, beside_all):
    masks = [center[2] * beside_all[direction][2] for direction in range(6)]
    perm_faces = [
        harmonic(center[1], beside_all[direction][1], masks[direction]) for direction in range(6)
    ]
    mobility = []
    for direction in range(6):
        field_component = 5 + direction // 2
        if direction % 2 == 0:
            mobility.append(center[field_component] * masks[direction])
        else:
            mobility.append(beside_all[direction][field_component] * masks[direction])
    coefficient = [perm_faces[direction] * mobility[direction] for direction in range(6)]
    diagonal_entries = accumulate(coefficient) + STORAGE + center[4]
    forcing = center[3] + STORAGE * center[0]
    scaling = 1.0 / diagonal_entries
    outgoing = [
        perm_faces[direction] * (center[0] - beside_all[direction][0]) for direction in (0, 2, 4)
    ]
    return (coefficient, diagonal_entries, forcing, scaling, outgoing)


def heat_terms(center, beside_all):
    masks = [center[2] * beside_all[direction][2] for direction in range(6)]
    conduct_faces = [
        harmonic(center[1], beside_all[direction][1], masks[direction]) for direction in range(6)
    ]
    own_fluid = brine_flowability(center[0])
    fluid_faces = [
        harmonic(own_fluid, brine_flowability(beside_all[direction][0]), masks[direction])
        for direction in range(6)
    ]
    velocity = []
    for direction in range(6):
        field_component = 5 + direction // 2
        if direction % 2 == 0:
            velocity.append(center[field_component] * fluid_faces[direction])
        else:
            velocity.append(-beside_all[direction][field_component] * fluid_faces[direction])
    coefficient = [
        conduct_faces[direction] - jnp.minimum(velocity[direction], 0.0) for direction in range(6)
    ]
    outflow = accumulate([jnp.maximum(velocity[direction], 0.0) for direction in range(6)])
    diagonal_entries = accumulate(conduct_faces) + outflow + center[4]
    forcing = center[3]
    scaling = jnp.ones_like(diagonal_entries)
    outgoing = [fluid_faces[direction] for direction in (0, 2, 4)]
    return (coefficient, diagonal_entries, forcing, scaling, outgoing)


def crop(values, margin):
    row_count = values.shape[-2]
    col_count = values.shape[-1]
    return values[..., margin : row_count - margin, margin * W : col_count - margin * W]


def beside(values):
    row_count = values.shape[-2]
    col_count = values.shape[-1]
    inner_cols = col_count - 2 * W
    column_pos = lax.broadcasted_iota(jnp.int32, (row_count - 2, inner_cols), 1) % W
    lower_mask = (column_pos > 0).astype(values.dtype)
    upper_mask = (column_pos < W - 1).astype(values.dtype)
    center = values[..., 1 : row_count - 1, W : col_count - W]
    beside_all = [
        values[..., 2:, W : col_count - W],
        values[..., : row_count - 2, W : col_count - W],
        values[..., 1 : row_count - 1, 2 * W :],
        values[..., 1 : row_count - 1, : col_count - 2 * W],
        values[..., 1 : row_count - 1, W + 1 : col_count - W + 1] * upper_mask,
        values[..., 1 : row_count - 1, W - 1 : col_count - W - 1] * lower_mask,
    ]
    return (beside_all, center)


def extend(values, margin):
    row_ext = extended(values, (("ba", 1),), margin)
    return extended(row_ext, (("aa", 2),), margin * W)


def regroup_layout(received_block):
    components = received_block.shape[0]
    turned = jnp.transpose(received_block, (0, 3, 2, 1))
    return turned.reshape(
        components, received_block.shape[3], received_block.shape[2] * received_block.shape[1]
    )


def body(states, coupled, facies, injectors, producers, perm_table, cond_table):
    is_press = lax.axis_index("code") == 0
    own_field = states[0]
    row_count = own_field.shape[0]
    col_count = own_field.shape[1]
    lithology_lookup = jnp.where(is_press, perm_table, cond_table)
    other_table = jnp.where(is_press, cond_table, perm_table)
    own_classes = facies[0]
    property_field = accumulate(
        [jnp.where(own_classes == index_c, lithology_lookup[index_c], 0.0) for index_c in range(NF)]
    )
    other_property = accumulate(
        [jnp.where(own_classes == index_c, other_table[index_c], 0.0) for index_c in range(NF)]
    )
    inject_cells = injectors[0].astype(jnp.float32)
    produce_cells = producers[0].astype(jnp.float32)
    source = inject_cells * jnp.where(
        is_press, INJECTION, FLOW_RATE * CHILLED_INFLOW
    ) + produce_cells * jnp.where(is_press, PRODUCT_INDEX * WELL_PRESSURE, 0.0)
    well_sink = produce_cells * jnp.where(
        is_press, PRODUCT_INDEX, FLOW_RATE
    ) + inject_cells * jnp.where(is_press, 0.0, FLOW_RATE)
    inside = jnp.ones_like(own_field)
    stacked = jnp.concatenate(
        [
            jnp.stack([own_field, property_field, inside, source, well_sink]),
            coupled[0],
            other_property[None],
        ],
        axis=0,
    )
    halo_depth = 1
    widened_stack = extend(stacked, halo_depth)
    beside_all, center = beside(widened_stack)
    coefficient, diagonal_entries, forcing, scaling, outgoing_list = lax.cond(
        is_press, pressure_terms, heat_terms, center, beside_all
    )
    outgoing = jnp.stack([crop(face_item, halo_depth - 1) for face_item in outgoing_list])
    payload = outgoing[::-1].reshape(3, row_count, col_count // W, W)
    regrouped = regroup_layout(
        lax.all_to_all(payload, "ba", split_axis=3, concat_axis=1, tiled=True)
    )
    received = from_partner(regrouped, "code", 0)
    chebyshev, explicit = sweep_weights()
    present_iterate = own_field
    previous = None
    prev_depth = 0
    counter = 0
    for sweep_block in range(ITERS // halo_depth):
        widened = extend(present_iterate[None], halo_depth)[0]
        if previous is None:
            previous = widened
            prev_depth = halo_depth
        region = halo_depth
        region = region - 1
        around_v, center_v = beside(widened)
        index_shift = halo_depth - 1 - region
        applied = crop(diagonal_entries, index_shift) * center_v - accumulate(
            [
                crop(coefficient[direction], index_shift) * around_v[direction]
                for direction in range(6)
            ]
        )
        residual = crop(scaling, index_shift) * (crop(forcing, index_shift) - applied)
        weight_new = jnp.where(is_press, chebyshev[counter][0], explicit[counter][0])
        weight_old = jnp.where(is_press, chebyshev[counter][1], explicit[counter][1])
        updated = (
            center_v
            + weight_new * residual
            + weight_old * (center_v - crop(previous, prev_depth - region))
        )
        previous = widened
        prev_depth = region + 1
        widened = updated
        counter = counter + 1
        present_iterate = widened
    return (present_iterate[None], received[None])


TINY = 1e-30
LANES = 128
HALF = 64
XH = 4
VM = pl.BlockSpec(memory_space=pltpu.VMEM)
SM = pl.BlockSpec(memory_space=pltpu.SMEM)
HB = pl.BlockSpec(memory_space=pltpu.HBM)
UNROLL = 4
PARTS = 4
LEAN = pltpu.CompilerParams(vmem_limit_bytes=6 * 2**20)


def params(megabytes):
    return pltpu.CompilerParams(vmem_limit_bytes=megabytes * 2**20)


def cost(micros):
    return pl.CostEstimate(
        flops=int(micros * 1.15e9), bytes_accessed=int(micros * 3.6e6), transcendentals=0
    )


def in_vmem(shape):
    return pltpu.VMEM(shape, jnp.float32)


def held(value):
    return pltpu.with_memory_space_constraint(value, pltpu.VMEM)


def lanes_at(tile, base=0):
    return pl.ds(pl.multiple_of(base + tile * LANES, LANES), LANES)


def lane_index(shape):
    return lax.broadcasted_iota(jnp.int32, shape, len(shape) - 1)


def inverse(value):
    return pl.reciprocal(value, approx=False)


def face_mean(left, right):
    return 2.0 * left * right * inverse(jnp.maximum(left + right, TINY))


def flowability(level):
    return 0.2 + 0.8 * inverse(1.0 + jnp.exp(-6.0 * (level - 0.5)))


def half_turn(value):
    return pltpu.roll(value, HALF, 1)


def next_lane(value):
    return pltpu.roll(value, LANES - 1, 1)


def prev_lane(value):
    return pltpu.roll(value, 1, 1)


def next_row(value):
    return pltpu.roll(value, value.shape[0] - 1, 0)


def prev_row(value):
    return pltpu.roll(value, 1, 0)


def look_up(table, codes):
    value = jnp.zeros(codes.shape, jnp.float32)
    for index_c in range(NF):
        value = jnp.where(codes == index_c + 1, table[index_c], value)
    return value


def placed_pair(pair, is_low):
    blank = jnp.zeros((6, pair.shape[1]), pair.dtype)
    return jnp.where(
        is_low, jnp.concatenate([pair, blank], 0), jnp.concatenate([blank, pair], 0)
    )


def placed_row(row, is_low):
    blank = jnp.zeros((7, row.shape[1]), row.dtype)
    return jnp.where(is_low, jnp.concatenate([row, blank], 0), jnp.concatenate([blank, row], 0))


def rim_slots(is_low, state, codes, f0, f1, f2, inject, produce):
    def pair(value):
        return jnp.where(is_low, value[6:8], value[0:2])

    def near(one, two):
        value = jnp.concatenate([one[0:8], two[0:8]], 0)
        return jnp.concatenate(
            [
                jnp.where(is_low, value[7:8], value[0:1]),
                jnp.where(is_low, value[15:16], value[8:9]),
            ],
            0,
        )

    return [
        pair(state),
        pair((codes + 1).astype(jnp.float32)),
        pair(f0),
        near(f1, f2),
        near(inject.astype(jnp.float32), produce.astype(jnp.float32)),
    ]


def corner_kernel(where_ref, st, cp, fa, ij, pr, corners, state, field, codes, sems):
    is_low = where_ref[1] == 0
    rows, cols = st.shape[1], st.shape[2]
    wide = XH * W
    at = pl.ds(pl.multiple_of(jnp.where(is_low, rows - 8, 0), 8), 8)
    copies = []
    for side, start in enumerate((0, cols - wide)):
        lanes = pl.ds(start, wide)
        for source, target in (
            (st.at[0, at, lanes], state.at[side]),
            (cp.at[0, :, at, lanes], field.at[side]),
            (fa.at[0, at, lanes], codes.at[side, 0]),
            (ij.at[0, at, lanes], codes.at[side, 1]),
            (pr.at[0, at, lanes], codes.at[side, 2]),
        ):
            copy = pltpu.make_async_copy(source, target, sems.at[len(copies)])
            copy.start()
            copies.append(copy)
    for copy in copies:
        copy.wait()
    for side in range(2):
        slots = rim_slots(
            is_low, state[side], codes[side, 0], field[side, 0], field[side, 1], field[side, 2],
            codes[side, 1], codes[side, 2],
        )
        for index, slot in enumerate(slots):
            start = (2 * index + side) * wide
            corners[:, start : start + wide] = slot


def edges_kernel(where_ref, st, cp, fa, ij, pr, to_right, to_left, across):
    is_low = where_ref[1] == 0
    rows, cols = st.shape[1], st.shape[2]
    wide = XH * W
    for target, start in ((to_right, cols - wide), (to_left, 0)):
        at = slice(start, start + wide)
        parts = [
            st[0, :, at],
            (fa[0, :, at] + 1).astype(jnp.float32),
            cp[0, 0, :, at],
            cp[0, 1, :, at],
            cp[0, 2, :, at],
            ij[0, :, at].astype(jnp.float32),
            pr[0, :, at].astype(jnp.float32),
        ]
        for index, part in enumerate(parts):
            target[:, index * wide : (index + 1) * wide] = part
    rim = pl.ds(pl.multiple_of(jnp.where(is_low, rows - 8, 0), 8), 8)
    slots = rim_slots(
        is_low, st[0, rim, :], fa[0, rim, :], cp[0, 0, rim, :], cp[0, 1, rim, :],
        cp[0, 2, rim, :], ij[0, rim, :], pr[0, rim, :],
    )
    for index, slot in enumerate(slots):
        across[:, index * cols : (index + 1) * cols] = slot


def pack_kernel(right_in, left_in, corners, to_right, to_left):
    wide = XH * W
    for side, (source, target) in enumerate(((left_in, to_left), (right_in, to_right))):
        target[:, : 7 * wide] = source[...]
        target[:, 7 * wide :] = jnp.zeros((32, LANES), jnp.float32)
        for index in range(5):
            for row in range(2):
                for half in range(2):
                    start = (2 * index + side) * wide + half * LANES
                    place = index * 4 + row * 2 + half
                    target[place : place + 1, 7 * wide :] = corners[
                        row : row + 1, start : start + LANES
                    ]


def put_cells(refs, is_press, tables, e, rows, cells):
    v0, prop, rock, c0, c1, c2, src, snk = refs
    state, codes, f0, f1, f2, inject, produce = cells
    v0[e + 1, rows, :] = state
    prop[e + 1, rows, :] = look_up(tables[0], codes)
    if is_press is not True:
        rock[e + 1, rows, :] = look_up(tables[1], codes)
    c0[e + 1, rows, :] = f0
    c1[e + 1, rows, :] = f1
    c2[e + 1, rows, :] = f2
    if is_press is True:
        src[e + 1, rows, :], snk[e + 1, rows, :] = 2.0 * inject - produce, produce
    elif is_press is False:
        src[e + 1, rows, :], snk[e + 1, rows, :] = 0.1 * inject, produce + inject
    else:
        src[e + 1, rows, :] = jnp.where(is_press, 2.0 * inject - produce, 0.1 * inject)
        snk[e + 1, rows, :] = jnp.where(is_press, produce, produce + inject)


def class_tables(is_press, perm_ref, cond_ref):
    perm = [perm_ref[index_c] for index_c in range(NF)]
    own = [jnp.where(is_press, perm[index_c], cond_ref[index_c]) for index_c in range(NF)]
    return own, perm


def fill_own(refs, is_press, tables, own_rows, raw):
    st, cp, fa, ij, pr = raw

    def fill(t, carry):
        at = lanes_at(t)
        cells = (
            st[0, :, at], fa[0, :, at] + 1, cp[0, 0, :, at], cp[0, 1, :, at], cp[0, 2, :, at],
            ij[0, :, at].astype(jnp.float32), pr[0, :, at].astype(jnp.float32),
        )
        put_cells(refs, is_press, tables, t + XH // 2, own_rows, cells)
        return carry

    lax.fori_loop(0, st.shape[2] // LANES, fill, 0, unroll=8)


def turn_kernel(
    where_ref, perm_ref, cond_ref, st, cp, fa, ij, pr, corners,
    own, other, rim, fluid, v0, prop, rock, c0, c1, c2, src, snk,
):
    del corners
    is_heat = where_ref[0] == 1
    is_low = where_ref[1] == 0
    own_rows = pl.ds(pl.multiple_of(jnp.where(is_low, 0, 8), 8), 32)
    groups = st.shape[2] // (4 * LANES)
    extra = groups * 2 * LANES
    row = lax.broadcasted_iota(jnp.int32, (32, LANES), 0)

    def step(group, rims):
        tall = jnp.concatenate(
            [st[0, :, lanes_at(4 * group + q)] for q in range(4)], axis=0
        )
        tall = jnp.where(is_heat, flowability(tall), tall)
        for q in range(4):
            fluid[4 * group + q + XH // 2 + 1, own_rows, :] = tall[32 * q : 32 * q + 32]
        turned = tall.T
        for par in range(2):
            low = turned[par * HALF : par * HALF + 32]
            high = turned[par * HALF + 32 : par * HALF + 64]
            own[:, lanes_at(group, par * groups * LANES)] = jnp.where(is_low, low, high)
            away = jnp.where(is_low, high, low)
            rim = high[0:1]

            other[:, lanes_at(group, par * groups * LANES)] = away
            rims = jnp.where(row == par * groups + group, rim, rims)
        return rims

    rims = lax.fori_loop(0, groups, step, jnp.zeros((32, LANES), jnp.float32), unroll=8)
    rim[:, :LANES] = jnp.where(is_low, rims, 0.0)
    other[:, extra : extra + LANES] = jnp.where(is_low, 0.0, rims)
    refs = (v0, prop, rock, c0, c1, c2, src, snk)
    tables = class_tables(jnp.logical_not(is_heat), perm_ref, cond_ref)

    @pl.when(is_heat)
    def _():
        fill_own(refs, False, tables, own_rows, (st, cp, fa, ij, pr))


def plane_kernel(where_ref, from_right, own_in, *rest):
    del own_in
    own = rest[-1]
    is_heat = where_ref[0] == 1
    is_low = where_ref[1] == 0
    wide = XH * W
    value = from_right[:, 0:LANES]
    inside = from_right[:, wide : wide + LANES] > 0.5
    value = jnp.where(is_heat, jnp.where(inside, flowability(value), 0.0), value)
    tall = jnp.concatenate([value, value, jnp.zeros((64, LANES), jnp.float32)], 0).T
    low, high = tall[0:32], tall[32:64]
    keep = lane_index((32, LANES)) < 32
    own[:, own.shape[1] - LANES :] = jnp.where(keep == is_low, low, high)


def send_kernel(boundary_in, rim, boundary):
    del boundary_in
    first = boundary.shape[1] - 16 * LANES
    for index in range(16):
        start = first + index * LANES
        boundary[:, start : start + LANES] = rim[2 * index : 2 * index + 2, LANES:]


def sweep(tiles, coeffs, force, diag, now, last, target, weight, pull, rows=slice(None)):
    first, stop = tiles
    shape = now[0, rows].shape
    low_lanes = lane_index(shape) < HALF

    def step(e, carry):
        before, here = carry
        tall = now[e + 1]
        value = tall[rows]
        after = half_turn(now[e + 2, rows])
        total = force[e + 1, rows]
        total += coeffs[0, e + 1, rows] * next_row(tall)[rows]
        total += coeffs[1, e + 1, rows] * prev_row(tall)[rows]
        total += coeffs[2, e + 1, rows] * jnp.where(low_lanes, here, after)
        total += coeffs[3, e + 1, rows] * jnp.where(low_lanes, before, here)
        total += coeffs[4, e + 1, rows] * next_lane(value)
        total += coeffs[5, e + 1, rows] * prev_lane(value)
        if diag is None:
            result = (1.0 + pull - weight) * value + weight * total
        else:
            result = (1.0 + pull) * value + weight * (total - diag[e + 1, rows] * value)
        if pull != 0.0:
            result -= pull * last[e + 1, rows]
        target(e, result)
        return here, after

    lax.fori_loop(
        first, stop, step,
        (half_turn(now[first, rows]), half_turn(now[first + 1, rows])),
        unroll=stop - first,
    )


def store_in(ref):
    def put(e, value):
        ref[e + 1] = value

    return put


def rim_cells(is_low, read):
    def pair(index):
        return placed_pair(jnp.concatenate([read(index, 0), read(index, 1)], 0), is_low)

    def near(index, row):
        return placed_row(read(index, row), is_low)

    return (
        pair(0), pair(1).astype(jnp.int32), pair(2),
        near(3, 0), near(3, 1), near(4, 0), near(4, 1),
    )


def rim_rows(is_low):
    return pl.ds(pl.multiple_of(jnp.where(is_low, 32, 0), 8), 8)


def put_level(fluid, cells, e, rows):
    prop, state = cells[1][e + 1, rows, :], cells[0][e + 1, rows, :]
    fluid[e + 1, rows, :] = jnp.where(prop > 0.0, flowability(state), 0.0)


def clear(refs, places):
    for ref in refs:
        for e in places:
            ref[e] = jnp.zeros(ref.shape[1:], jnp.float32)


def flow_pair(mean, flow, field):
    speed = flow * field
    gain = mean + jnp.maximum(speed, 0.0)
    return gain, gain - speed


def heat_b_terms(cells, made, e):
    v0, prop, rock, c0, c1, c2, src, snk = cells
    coeffs, force, diag, fluid = made
    value, level = prop[e + 1], fluid[e + 1]
    not_last = lane_index(value.shape) % W != W - 1
    gain, loss = flow_pair(
        face_mean(value, jnp.where(not_last, next_lane(value), 0.0)),
        face_mean(level, jnp.where(not_last, next_lane(level), 0.0)),
        c2[e + 1],
    )
    coeffs[4, e + 1] = loss
    coeffs[5, e + 1] = prev_lane(gain)
    diag[e + 1] = snk[e + 1] + gain + prev_lane(loss)


def face_terms(cells, made, is_press, ranges):
    v0, prop, rock, c0, c1, c2, src, snk = cells
    coeffs, force, diag, fluid = made
    shape = v0.shape[1:]
    lane = lane_index(shape)
    low_lanes = lane < HALF
    not_last = lane % W != W - 1
    blank = jnp.zeros(shape, jnp.float32)

    last_tile = v0.shape[0] - 3

    def inside(e):
        return min(e, last_tile) if isinstance(e, int) else e

    def run(step, first, stop, start):
        if stop - first > 8:
            unroll = max(n for n in range(1, 10) if (stop - first) % n == 0)
            return lax.fori_loop(first, stop, step, start, unroll=unroll)
        for e in range(first, stop):
            start = step(e, start)
        return start

    def beside(value, turns, after):
        return (
            jnp.where(low_lanes, turns[0], after[0]),
            jnp.where(not_last, turns[1], 0.0),
        )

    def press_range(first, stop):
        def turns(e):
            value = prop[e + 1]
            return half_turn(value), next_lane(value)

        def along(e, now, after):
            value = prop[e + 1]
            x_side, b_side = beside(value, now, after)
            return face_mean(value, x_side) * c1[e + 1], face_mean(value, b_side) * c2[e + 1]

        def close(e, before, plus, turned):
            value = prop[e + 1]
            plus = [face_mean(value, next_row(value)) * c0[e + 1], *plus]
            minus = [prev_row(plus[0]), jnp.where(low_lanes, before, turned[0]), turned[1]]
            scale = inverse(accumulate(plus + minus) + STORAGE + snk[e + 1])
            for dim in range(3):
                coeffs[2 * dim, e + 1] = scale * plus[dim]
                coeffs[2 * dim + 1, e + 1] = scale * minus[dim]
            force[e + 1] = scale * (src[e + 1] + STORAGE * v0[e + 1])

        def step(e, carry):
            before, plus, turned, now, after = carry
            close(e - 1, before, plus, turned)
            later = turns(inside(e + 2))
            fresh = along(e, now, after)
            return turned[0], fresh, (half_turn(fresh[0]), prev_lane(fresh[1])), after, later

        now, after = turns(first), turns(first + 1)
        before = blank
        if first > 0:
            before = half_turn(along(first - 1, turns(first - 1), now)[0])
        fresh = along(first, now, after)
        carry = (
            before, fresh, (half_turn(fresh[0]), prev_lane(fresh[1])), after, turns(first + 2)
        )
        before, plus, turned, _, _ = run(step, first + 1, stop, carry)
        close(stop - 1, before, plus, turned)

    def heat_range(first, stop):
        def turns(e):
            return half_turn(prop[e + 1]), half_turn(fluid[e + 1])

        def along(e, now, after):
            value, level = prop[e + 1], fluid[e + 1]
            return flow_pair(
                face_mean(value, jnp.where(low_lanes, now[0], after[0])),
                face_mean(level, jnp.where(low_lanes, now[1], after[1])),
                c1[e + 1],
            )

        def close(e, before, turned):
            value, level = prop[e + 1], fluid[e + 1]
            gain, loss = flow_pair(
                face_mean(value, next_row(value)), face_mean(level, next_row(level)), c0[e + 1]
            )
            coeffs[0, e + 1] = loss
            coeffs[1, e + 1] = prev_row(gain)
            coeffs[3, e + 1] = jnp.where(low_lanes, before[0], turned[0])
            total = diag[e + 1] + gain + prev_row(loss)
            diag[e + 1] = total + turned[2] + jnp.where(low_lanes, before[1], turned[1])

        def opened(e, now, after):
            gain, loss = along(e, now, after)
            coeffs[2, e + 1] = loss
            return half_turn(gain), half_turn(loss), gain

        def step(e, carry):
            before, turned, now, after = carry
            close(e - 1, before, turned)
            later = turns(inside(e + 2))
            return turned[:2], opened(e, now, after), after, later

        def b_steps(first, stop):
            def b_step(e, carry):
                heat_b_terms(cells, made, e)
                return carry

            if stop - first > 8:
                lax.fori_loop(first, stop, b_step, 0, unroll=8)
            else:
                for e in range(first, stop):
                    b_step(e, 0)

        b_steps(first, stop)
        now, after = turns(first), turns(first + 1)
        before = (blank, blank)
        if first > 0:
            gain, loss = along(first - 1, turns(first - 1), now)
            before = half_turn(gain), half_turn(loss)
        carry = (before, opened(first, now, after), after, turns(first + 2))
        before, turned, _, _ = run(step, first + 1, stop, carry)
        close(stop - 1, before, turned)

    @pl.when(is_press)
    def _():
        for first, stop in ranges:
            press_range(first, stop)

    @pl.when(jnp.logical_not(is_press))
    def _():
        for first, stop in ranges:
            heat_range(first, stop)


def inner_kernel(where_ref, perm_ref, cond_ref, across, st, cp, fa, ij, pr, *refs):
    coeffs, force, diag, fluid = refs[-12:-8]
    cells = refs[-8:]
    is_press = where_ref[0] == 0
    is_low = where_ref[1] == 0
    ext = cells[0].shape[0] - 2
    side = XH // 2
    tiles = ext - XH
    cols = tiles * LANES
    rows = rim_rows(is_low)
    tables = class_tables(is_press, perm_ref, cond_ref)
    clear(tuple(cells[:3]) + (fluid,), (0, 1, 2, ext - 1, ext, ext + 1))

    @pl.when(is_press)
    def _():
        own_rows = pl.ds(pl.multiple_of(jnp.where(is_low, 0, 8), 8), 32)
        fill_own(cells, True, tables, own_rows, (st, cp, fa, ij, pr))

    def fill(t, carry):
        read = lambda index, row: across[row : row + 1, lanes_at(t, index * cols)]
        put_cells(cells, is_press, tables, t + side, rows, rim_cells(is_low, read))
        put_level(fluid, cells, t + side, rows)
        return carry

    lax.fori_loop(0, tiles, fill, 0, unroll=8)
    made = (coeffs, force, diag, fluid)
    face_terms(cells, made, is_press, [(side, ext - side)])


def main_kernel(where_ref, perm_ref, cond_ref, from_left, from_right, *refs):
    v1, v2, boundary = refs[12:15]
    coeffs, force, diag, fluid = refs[15:19]
    cells = refs[19:]
    v0 = cells[0]
    is_press = where_ref[0] == 0
    is_low = where_ref[1] == 0
    ext = v0.shape[0] - 2
    wide = XH * W
    side = XH // 2
    own_rows = pl.ds(pl.multiple_of(jnp.where(is_low, 0, 8), 8), 32)
    tables = class_tables(is_press, perm_ref, cond_ref)

    for e, message, at in (
        (0, from_left, 0), (1, from_left, 1), (ext - 2, from_right, 0), (ext - 1, from_right, 1)
    ):
        parts = [message[:, lanes_at(at, index * wide)] for index in range(7)]
        parts[1] = parts[1].astype(jnp.int32)
        put_cells(cells, is_press, tables, e, own_rows, parts)
        corner = message[:, 7 * wide :]
        read = lambda index, row, corner=corner, at=at: corner[
            index * 4 + row * 2 + at : index * 4 + row * 2 + at + 1
        ]
        put_cells(cells, is_press, tables, e, rim_rows(is_low), rim_cells(is_low, read))
        put_level(fluid, cells, e, slice(None))
    clear((v1, v2), (0, ext + 1))
    clear((v2,), (1, ext))
    for e in (0, ext - 1):
        boundary[:, e * LANES : (e + 1) * LANES] = jnp.zeros((2, LANES), jnp.float32)
    made = (coeffs, force, diag, fluid)
    face_terms(cells, made, is_press, [(0, side + 1), (ext - side - 1, ext)])
    chebyshev, explicit = sweep_weights()
    src = cells[6]

    is_high = jnp.logical_not(is_low)

    for chosen, weights, centre, drive in (
        (is_press, chebyshev, None, force),
        (jnp.logical_not(is_press), explicit, diag, src),
    ):

        @pl.when(chosen)
        def _(weights=weights, centre=centre, force=drive):
            (w0, u0), (w1, u1) = weights[:2]
            sweep((0, ext), coeffs, force, centre, v0, v0, store_in(v1), w0, u0)
            for placed, rows, edge in (
                (is_low, slice(0, 32), slice(30, 32)), (is_high, slice(8, 40), slice(0, 2))
            ):

                @pl.when(placed)
                def _(rows=rows, edge=edge):
                    def put(e, value):
                        v2[e + 1, rows] = value
                        boundary[:, lanes_at(e)] = value[edge]

                    sweep((1, ext - 1), coeffs, force, centre, v1, v0, put, w1, u1, rows)


def finish_kernel(
    where_ref, v1, v2_in, received_in, coeffs, force, src, diag, boundary, edge, rim,
    out_ref, now, received, later, out, tile, sems,
):
    del v2_in, received_in
    is_press = where_ref[0] == 0
    is_low = where_ref[1] == 0
    ext = now.shape[0] - 2
    side = XH // 2
    tiles = ext - XH
    rows = rim_rows(is_low)
    clear((later,), (0, ext + 1))
    lane = lane_index((32, LANES))
    mine = rim[:, LANES:]
    start = boundary.shape[1] - 16 * LANES
    theirs = jnp.concatenate(
        [boundary[:, start + index * LANES : start + (index + 1) * LANES] for index in range(16)],
        0,
    )
    plane = jnp.where(
        is_low,
        jnp.where(lane < 32, mine, theirs),
        jnp.where(lane < 32, pltpu.roll(theirs, 96, 1), pltpu.roll(mine, 32, 1)),
    )
    here = edge[0]
    beside = jnp.where(lane < HALF, half_turn(here), half_turn(plane))
    tile[...] = jnp.where(is_press, face_mean(here, beside), edge[1] * (here - beside))
    last_tile = pl.ds((tiles - 1) * LANES, LANES)
    tile_copy = pltpu.make_async_copy(tile, received.at[0, 1, :, last_tile], sems.at[PARTS])
    tile_copy.start()

    def fill(e, carry):
        now[e + 1, rows, :] = placed_pair(boundary[:, lanes_at(e)], is_low)
        return carry

    lax.fori_loop(0, ext, fill, 0, unroll=17)
    chebyshev, explicit = sweep_weights()

    def put_out(e, value):
        out[:, lanes_at(e - side)] = value

    is_high = jnp.logical_not(is_low)
    for chosen, weights, centre, drive in (
        (is_press, chebyshev, None, force),
        (jnp.logical_not(is_press), explicit, diag, src),
    ):

        @pl.when(chosen)
        def _(weights=weights, centre=centre, force=drive):
            (w2, u2), (w3, u3) = weights[2:]
            sweep((1, ext - 1), coeffs, force, centre, now, v1, store_in(later), w2, u2)
            for placed, rows in ((is_low, slice(0, 32)), (is_high, slice(8, 40))):

                @pl.when(placed)
                def _(rows=rows):
                    part = tiles // PARTS
                    copies = []
                    for index in range(PARTS):
                        first = side + index * part
                        sweep(
                            (first, first + part), coeffs, force, centre, later, now, put_out,
                            w3, u3, rows,
                        )
                        at = pl.ds(index * part * LANES, part * LANES)
                        copy = pltpu.make_async_copy(
                            out.at[:, at], out_ref.at[0, :, at], sems.at[index]
                        )
                        copy.start()
                        copies.append(copy)
                    for copy in copies:
                        copy.wait()

    tile_copy.wait()


def regrouped(pieces):
    lane = lane_index(pieces[0].shape)
    result = []
    for q in range(4):
        value = None
        for place in range(4):
            piece = pieces[place]
            if place != q:
                piece = pltpu.roll(piece, ((place - q) * 32) % LANES, 1)
            value = piece if value is None else jnp.where(lane >= place * 32, piece, value)
        result.append(value)
    return result


def faces_kernel(
    where_ref, own, other, own_rim, rock, out_ref, edge, field, rim, out, sems
):
    is_press = where_ref[0] == 0
    is_low = where_ref[1] == 0
    tiles = out.shape[2] // LANES
    groups = tiles // 4
    side = XH // 2
    extra = groups * 2 * LANES

    def ordered(mine, theirs):
        return [jnp.where(is_low, mine, theirs), jnp.where(is_low, theirs, mine)]

    pieces = []
    for par in range(2):
        pieces += ordered(
            own_rim[par * groups : (par + 1) * groups, :LANES],
            other[par * groups : (par + 1) * groups, extra : extra + LANES],
        )
    for q, value in enumerate(regrouped(pieces)):
        rim[q] = value
    lane = lane_index((32, LANES))
    field[tiles] = jnp.zeros(field.shape[1:], jnp.float32)

    def gather(group, carry):
        pieces = []
        for par in range(2):
            at = lanes_at(group, par * groups * LANES)
            pieces += ordered(own[:, at], other[:, at])
        for q, value in enumerate(regrouped(pieces)):
            field[4 * group + q, 0:32, :] = value
            field[4 * group + q, 32:33, :] = rim[q, pl.ds(group, 1), :]
        return carry

    lax.fori_loop(0, groups, gather, 0, unroll=8)
    low_lanes = lane < HALF
    not_last = lane % W != W - 1

    def around(t, turned):
        value = field[t]
        here = value[0:32]
        after = half_turn(field[t + 1, 0:32, :])
        others = next_row(value)[0:32], jnp.where(low_lanes, turned, after), next_lane(here)
        return here, others, after

    def press(t, carry):
        here, others, after = around(t, carry)
        others = (others[0], others[1], jnp.where(not_last, others[2], 0.0))
        for dim in range(3):
            out[dim, :, lanes_at(t)] = face_mean(here, others[dim])
        return after

    def heat(t, carry):
        here, others, after = around(t, carry[0])
        stone = rock[t + side + 1, own_rows, :]
        stone_after = half_turn(rock[t + side + 2, own_rows, :])
        rim_row = jnp.where(is_low, rock[t + side + 1, 32:33, :], 0.0)
        near = (
            jnp.where(last_row, rim_row, next_row(stone)),
            jnp.where(low_lanes, carry[1], stone_after),
            jnp.where(not_last, next_lane(stone), 0.0),
        )
        for dim in range(3):
            mean = face_mean(stone, near[dim])
            out[dim, :, lanes_at(t)] = mean * (here - others[dim])
        return after, stone_after

    own_rows = pl.ds(pl.multiple_of(jnp.where(is_low, 0, 8), 8), 32)
    last_row = lax.broadcasted_iota(jnp.int32, (32, LANES), 0) == 31
    part = tiles // PARTS
    copies = []
    edge[0] = field[tiles - 1, 0:32, :]
    stone = rock[tiles - 1 + side + 1, own_rows, :]
    stone_after = half_turn(rock[tiles + side + 1, own_rows, :])
    edge[1] = face_mean(stone, jnp.where(low_lanes, half_turn(stone), stone_after))
    for index in range(PARTS):
        first = index * part

        @pl.when(is_press)
        def _(first=first):
            start = half_turn(field[first, 0:32, :])
            lax.fori_loop(first, first + part, press, start, unroll=16)

        @pl.when(jnp.logical_not(is_press))
        def _(first=first):
            start = half_turn(field[first, 0:32, :]), half_turn(rock[first + side + 1, own_rows, :])
            lax.fori_loop(first, first + part, heat, start, unroll=16)

        at = pl.ds(first * LANES, part * LANES)
        copy = pltpu.make_async_copy(out.at[:, :, at], out_ref.at[0, :, :, at], sems.at[index])
        copy.start()
        copies.append(copy)
    for copy in copies:
        copy.wait()


def paired_body(states, coupled, facies, injectors, producers, perm_table, cond_table):
    rows, cols = states.shape[1], states.shape[2]
    tiles = cols // LANES
    ext = tiles + XH
    wide = XH * W
    groups = tiles // 4
    loaded = [held(value) for value in (states, coupled, facies, injectors, producers)]
    place = jnp.stack([lax.axis_index("code"), lax.axis_index("ba")]).astype(jnp.int32)
    count = lax.axis_size("aa")
    up = [(i, i + 1) for i in range(count - 1)]
    down = [(b, a) for a, b in up]
    swap = [(0, 1), (1, 0)]
    opposite = [(0, 3), (1, 2), (2, 1), (3, 0)]
    f32, i32 = jnp.float32, jnp.int32
    states, coupled, facies, injectors, producers = [
        pltpu.with_memory_space_constraint(value, pltpu.HBM)
        for value in (states, coupled, facies, injectors, producers)
    ]

    corners = pl.pallas_call(
        corner_kernel,
        out_shape=in_vmem((2, 10 * wide)),
        in_specs=[SM] + [HB] * 5,
        out_specs=VM,
        scratch_shapes=[
            pltpu.VMEM((2, 8, wide), f32),
            pltpu.VMEM((2, 3, 8, wide), f32),
            pltpu.VMEM((2, 3, 8, wide), i32),
            pltpu.SemaphoreType.DMA((10,)),
        ],
        compiler_params=LEAN,
        cost_estimate=cost(1),
        name="corner",
    )(place, states, coupled, facies, injectors, producers)
    corners = held(lax.ppermute(corners, "ba", swap))
    to_right, to_left, across = pl.pallas_call(
        edges_kernel,
        out_shape=[
            in_vmem((rows, 7 * wide)),
            in_vmem((rows, 7 * wide)),
            in_vmem((2, 5 * cols)),
        ],
        in_specs=[SM] + [VM] * 5,
        out_specs=[VM] * 3,
        compiler_params=LEAN,
        cost_estimate=cost(2),
        name="edges",
    )(place, *loaded)
    from_across = held(lax.ppermute(across, "ba", swap))
    to_right, to_left = pl.pallas_call(
        pack_kernel,
        out_shape=[in_vmem((rows, 7 * wide + LANES))] * 2,
        in_specs=[VM] * 3,
        out_specs=[VM] * 2,
        compiler_params=LEAN,
        cost_estimate=cost(1),
        name="pack",
    )(to_right, to_left, corners)
    from_left = held(lax.ppermute(to_right, "aa", up))
    from_right = held(lax.ppermute(to_left, "aa", down))

    field = (ext + 2, rows + 8, LANES)
    turned_own, turned_other, rim, fluid, *cells = pl.pallas_call(
        turn_kernel,
        out_shape=[
            in_vmem((32, 2 * groups * LANES)),
            in_vmem((32, (2 * groups + 1) * LANES)),
            in_vmem((32, 2 * LANES)),
        ]
        + [in_vmem(field)] * 9,
        in_specs=[SM] * 3 + [VM] * 6,
        out_specs=[VM] * 12,
        compiler_params=params(2),
        cost_estimate=cost(2.5),
        name="turn",
    )(
        place, perm_table, cond_table, *loaded, to_left,
    )
    other = held(lax.ppermute(turned_other, ("code", "ba"), opposite))
    own = held(lax.ppermute(turned_own, "code", swap))
    coeffs, force, diag, fluid, *cells = pl.pallas_call(
        inner_kernel,
        out_shape=[in_vmem((6,) + field)] + [in_vmem(field)] * 11,
        in_specs=[SM] * 3 + [VM] * 15,
        out_specs=[VM] * 12,
        input_output_aliases={9 + index: 3 + index for index in range(9)},
        compiler_params=params(2),
        cost_estimate=cost(10),
        name="inner",
    )(place, perm_table, cond_table, from_across, *loaded, fluid, *cells)
    rim = pl.pallas_call(
        plane_kernel,
        out_shape=in_vmem(rim.shape),
        in_specs=[SM] + [VM] * 4,
        out_specs=VM,
        input_output_aliases={2: 0},
        compiler_params=LEAN,
        cost_estimate=cost(1),
        name="plane",
    )(place, from_right, rim, from_left, force)
    rim = held(lax.ppermute(rim, "code", swap))

    v1, v2, boundary, coeffs, force, diag, fluid, *cells = pl.pallas_call(
        main_kernel,
        out_shape=[in_vmem(field), in_vmem(field), in_vmem((2, (ext + 16) * LANES))]
        + [in_vmem((6,) + field)]
        + [in_vmem(field)] * 11,
        in_specs=[SM] * 3 + [VM] * 14,
        out_specs=[VM] * 15,
        input_output_aliases={5 + index: 3 + index for index in range(12)},
        compiler_params=params(2),
        cost_estimate=cost(10),
        name="main",
    )(
        place, perm_table, cond_table, from_left, from_right,
        coeffs, force, diag, fluid, *cells,
    )
    boundary = pl.pallas_call(
        send_kernel,
        out_shape=in_vmem(boundary.shape),
        in_specs=[VM] * 2,
        out_specs=VM,
        input_output_aliases={0: 0},
        compiler_params=LEAN,
        cost_estimate=cost(1),
        name="send",
    )(boundary, rim)
    boundary = held(lax.ppermute(boundary, "ba", swap))
    received, edge = pl.pallas_call(
        faces_kernel,
        out_shape=[jax.ShapeDtypeStruct(coupled.shape, f32), in_vmem((2, 32, LANES))],
        in_specs=[SM] + [VM] * 4,
        out_specs=[HB, VM],
        scratch_shapes=[
            pltpu.VMEM((tiles + 1, rows + 8, LANES), f32),
            pltpu.VMEM((4, groups, LANES), f32),
            pltpu.VMEM(coupled.shape[1:], f32),
            pltpu.SemaphoreType.DMA((PARTS,)),
        ],
        compiler_params=params(8),
        cost_estimate=cost(6),
        name="faces",
    )(place, own, other, rim, cells[2])
    received = pltpu.with_memory_space_constraint(received, pltpu.HBM)
    stepped, _, received = pl.pallas_call(
        finish_kernel,
        out_shape=[
            jax.ShapeDtypeStruct(states.shape, f32),
            in_vmem(field),
            jax.ShapeDtypeStruct(coupled.shape, f32),
        ],
        in_specs=[SM] + [VM] * 2 + [HB] + [VM] * 7,
        out_specs=[HB, VM, HB],
        scratch_shapes=[
            pltpu.VMEM(field, f32),
            pltpu.VMEM(states.shape[1:], f32),
            pltpu.VMEM((32, LANES), f32),
            pltpu.SemaphoreType.DMA((PARTS + 1,)),
        ],
        input_output_aliases={2: 1, 3: 2},
        compiler_params=params(5),
        cost_estimate=cost(6),
        name="finish",
    )(place, v1, v2, received, coeffs, force, cells[6], diag, boundary, edge, rim)
    return (stepped, received)


def solution(mesh):
    paired = mesh.shape["ba"] == 2 and mesh.shape["code"] == 2
    return jax.shard_map(
        paired_body if paired else body,
        mesh=mesh,
        in_specs=(
            P("code", "ba", "aa"),
            P("code", None, "ba", "aa"),
            P("code", "ba", "aa"),
            P("code", "ba", "aa"),
            P("code", "ba", "aa"),
            P(),
            P(),
        ),
        out_specs=(P("code", "ba", "aa"), P("code", None, "ba", "aa")),
        check_vma=False,
    )
```

```python
import jax
import jax.numpy as jnp
from jax import lax
from jax.experimental import pallas as pl
from jax.experimental.pallas import tpu as pltpu
from jax.sharding import PartitionSpec as P

W = 64
NF = 6
ITERS = 4


STORAGE = 0.5
LOWER_BOUND = 0.05
INJECTION = 2.0
PRODUCT_INDEX = 1.0
WELL_PRESSURE = -1.0
FLOW_RATE = 1.0
CHILLED_INFLOW = 0.1
TIME_STEP = 0.05


def extended(block, sides, width):
    for axis, dim in sides:
        count = lax.axis_size(axis)
        forward = [(i, i + 1) for i in range(count - 1)]
        backward = [(target, source) for source, target in forward]
        low = lax.ppermute(
            lax.slice_in_dim(block, block.shape[dim] - width, None, axis=dim), axis, forward
        )
        high = lax.ppermute(lax.slice_in_dim(block, 0, width, axis=dim), axis, backward)
        block = jnp.concatenate([low, block, high], axis=dim)
    return block


def from_partner(value, axis, stride):
    mask = 2**stride
    pairs = [(source, source ^ mask) for source in range(lax.axis_size(axis))]
    return lax.ppermute(value, axis, pairs)


def brine_flowability(matrix_heat_level):
    return 0.2 + 0.8 * jax.nn.sigmoid(6.0 * (matrix_heat_level - 0.5))


def harmonic(left_val, eastern_neighbor_number, face_mask):
    return (
        face_mask
        * 2.0
        * left_val
        * eastern_neighbor_number
        / (left_val + eastern_neighbor_number + 1.0 - face_mask)
    )


def accumulate(terms):
    result = terms[0]
    for term in terms[1:]:
        result = result + term
    return result


def sweep_weights():
    centre_val = (2.0 + LOWER_BOUND) / 2.0
    half_width = (2.0 - LOWER_BOUND) / 2.0
    quotient_number = centre_val / half_width
    rho_old = 1.0 / quotient_number
    chebyshev = [(1.0 / centre_val, 0.0)]
    for index_k in range(1, ITERS):
        rho_new = 1.0 / (2.0 * quotient_number - rho_old)
        chebyshev.append((2.0 * rho_new / half_width, rho_new * rho_old))
        rho_old = rho_new
    explicit = []
    for index_k in range(ITERS):
        if index_k % 2 == 0:
            explicit.append((TIME_STEP, 0.0))
        else:
            explicit.append((0.5 * TIME_STEP, -0.5))
    return (chebyshev, explicit)


def pressure_terms(center, beside_all):
    masks = [center[2] * beside_all[direction][2] for direction in range(6)]
    perm_faces = [
        harmonic(center[1], beside_all[direction][1], masks[direction]) for direction in range(6)
    ]
    mobility = []
    for direction in range(6):
        field_component = 5 + direction // 2
        if direction % 2 == 0:
            mobility.append(center[field_component] * masks[direction])
        else:
            mobility.append(beside_all[direction][field_component] * masks[direction])
    coefficient = [perm_faces[direction] * mobility[direction] for direction in range(6)]
    diagonal_entries = accumulate(coefficient) + STORAGE + center[4]
    forcing = center[3] + STORAGE * center[0]
    scaling = 1.0 / diagonal_entries
    outgoing = [
        perm_faces[direction] * (center[0] - beside_all[direction][0]) for direction in (0, 2, 4)
    ]
    return (coefficient, diagonal_entries, forcing, scaling, outgoing)


def heat_terms(center, beside_all):
    masks = [center[2] * beside_all[direction][2] for direction in range(6)]
    conduct_faces = [
        harmonic(center[1], beside_all[direction][1], masks[direction]) for direction in range(6)
    ]
    own_fluid = brine_flowability(center[0])
    fluid_faces = [
        harmonic(own_fluid, brine_flowability(beside_all[direction][0]), masks[direction])
        for direction in range(6)
    ]
    velocity = []
    for direction in range(6):
        field_component = 5 + direction // 2
        if direction % 2 == 0:
            velocity.append(center[field_component] * fluid_faces[direction])
        else:
            velocity.append(-beside_all[direction][field_component] * fluid_faces[direction])
    coefficient = [
        conduct_faces[direction] - jnp.minimum(velocity[direction], 0.0) for direction in range(6)
    ]
    outflow = accumulate([jnp.maximum(velocity[direction], 0.0) for direction in range(6)])
    diagonal_entries = accumulate(conduct_faces) + outflow + center[4]
    forcing = center[3]
    scaling = jnp.ones_like(diagonal_entries)
    outgoing = [fluid_faces[direction] for direction in (0, 2, 4)]
    return (coefficient, diagonal_entries, forcing, scaling, outgoing)


def crop(values, margin):
    row_count = values.shape[-2]
    col_count = values.shape[-1]
    return values[..., margin : row_count - margin, margin * W : col_count - margin * W]


def beside(values):
    row_count = values.shape[-2]
    col_count = values.shape[-1]
    inner_cols = col_count - 2 * W
    column_pos = lax.broadcasted_iota(jnp.int32, (row_count - 2, inner_cols), 1) % W
    lower_mask = (column_pos > 0).astype(values.dtype)
    upper_mask = (column_pos < W - 1).astype(values.dtype)
    center = values[..., 1 : row_count - 1, W : col_count - W]
    beside_all = [
        values[..., 2:, W : col_count - W],
        values[..., : row_count - 2, W : col_count - W],
        values[..., 1 : row_count - 1, 2 * W :],
        values[..., 1 : row_count - 1, : col_count - 2 * W],
        values[..., 1 : row_count - 1, W + 1 : col_count - W + 1] * upper_mask,
        values[..., 1 : row_count - 1, W - 1 : col_count - W - 1] * lower_mask,
    ]
    return (beside_all, center)


def extend(values, margin):
    row_ext = extended(values, (("ba", 1),), margin)
    return extended(row_ext, (("aa", 2),), margin * W)


def regroup_layout(received_block):
    components = received_block.shape[0]
    turned = jnp.transpose(received_block, (0, 3, 2, 1))
    return turned.reshape(
        components, received_block.shape[3], received_block.shape[2] * received_block.shape[1]
    )


def body(states, coupled, facies, injectors, producers, perm_table, cond_table):
    is_press = lax.axis_index("code") == 0
    own_field = states[0]
    row_count = own_field.shape[0]
    col_count = own_field.shape[1]
    lithology_lookup = jnp.where(is_press, perm_table, cond_table)
    other_table = jnp.where(is_press, cond_table, perm_table)
    own_classes = facies[0]
    property_field = accumulate(
        [jnp.where(own_classes == index_c, lithology_lookup[index_c], 0.0) for index_c in range(NF)]
    )
    other_property = accumulate(
        [jnp.where(own_classes == index_c, other_table[index_c], 0.0) for index_c in range(NF)]
    )
    inject_cells = injectors[0].astype(jnp.float32)
    produce_cells = producers[0].astype(jnp.float32)
    source = inject_cells * jnp.where(
        is_press, INJECTION, FLOW_RATE * CHILLED_INFLOW
    ) + produce_cells * jnp.where(is_press, PRODUCT_INDEX * WELL_PRESSURE, 0.0)
    well_sink = produce_cells * jnp.where(
        is_press, PRODUCT_INDEX, FLOW_RATE
    ) + inject_cells * jnp.where(is_press, 0.0, FLOW_RATE)
    inside = jnp.ones_like(own_field)
    stacked = jnp.concatenate(
        [
            jnp.stack([own_field, property_field, inside, source, well_sink]),
            coupled[0],
            other_property[None],
        ],
        axis=0,
    )
    halo_depth = 1
    widened_stack = extend(stacked, halo_depth)
    beside_all, center = beside(widened_stack)
    coefficient, diagonal_entries, forcing, scaling, outgoing_list = lax.cond(
        is_press, pressure_terms, heat_terms, center, beside_all
    )
    outgoing = jnp.stack([crop(face_item, halo_depth - 1) for face_item in outgoing_list])
    payload = outgoing[::-1].reshape(3, row_count, col_count // W, W)
    regrouped = regroup_layout(
        lax.all_to_all(payload, "ba", split_axis=3, concat_axis=1, tiled=True)
    )
    received = from_partner(regrouped, "code", 0)
    chebyshev, explicit = sweep_weights()
    present_iterate = own_field
    previous = None
    prev_depth = 0
    counter = 0
    for sweep_block in range(ITERS // halo_depth):
        widened = extend(present_iterate[None], halo_depth)[0]
        if previous is None:
            previous = widened
            prev_depth = halo_depth
        region = halo_depth
        region = region - 1
        around_v, center_v = beside(widened)
        index_shift = halo_depth - 1 - region
        applied = crop(diagonal_entries, index_shift) * center_v - accumulate(
            [
                crop(coefficient[direction], index_shift) * around_v[direction]
                for direction in range(6)
            ]
        )
        residual = crop(scaling, index_shift) * (crop(forcing, index_shift) - applied)
        weight_new = jnp.where(is_press, chebyshev[counter][0], explicit[counter][0])
        weight_old = jnp.where(is_press, chebyshev[counter][1], explicit[counter][1])
        updated = (
            center_v
            + weight_new * residual
            + weight_old * (center_v - crop(previous, prev_depth - region))
        )
        previous = widened
        prev_depth = region + 1
        widened = updated
        counter = counter + 1
        present_iterate = widened
    return (present_iterate[None], received[None])


TINY = 1e-30
LANES = 128
HALF = 64
XH = 4
VM = pl.BlockSpec(memory_space=pltpu.VMEM)
SM = pl.BlockSpec(memory_space=pltpu.SMEM)
HB = pl.BlockSpec(memory_space=pltpu.HBM)
UNROLL = 4
PARTS = 4
LEAN = pltpu.CompilerParams(vmem_limit_bytes=6 * 2**20)


def params(megabytes):
    return pltpu.CompilerParams(vmem_limit_bytes=megabytes * 2**20)


def cost(micros):
    return pl.CostEstimate(
        flops=int(micros * 1.15e9), bytes_accessed=int(micros * 3.6e6), transcendentals=0
    )


def in_vmem(shape):
    return pltpu.VMEM(shape, jnp.float32)


def held(value):
    return pltpu.with_memory_space_constraint(value, pltpu.VMEM)


def lanes_at(tile, base=0):
    return pl.ds(pl.multiple_of(base + tile * LANES, LANES), LANES)


def lane_index(shape):
    return lax.broadcasted_iota(jnp.int32, shape, len(shape) - 1)


def inverse(value):
    return pl.reciprocal(value, approx=False)


def face_mean(left, right):
    return 2.0 * left * right * inverse(jnp.maximum(left + right, TINY))


def flowability(level):
    return 0.2 + 0.8 * inverse(1.0 + jnp.exp(-6.0 * (level - 0.5)))


def half_turn(value):
    return pltpu.roll(value, HALF, 1)


def next_lane(value):
    return pltpu.roll(value, LANES - 1, 1)


def prev_lane(value):
    return pltpu.roll(value, 1, 1)


def next_row(value):
    return pltpu.roll(value, value.shape[0] - 1, 0)


def prev_row(value):
    return pltpu.roll(value, 1, 0)


def look_up(table, codes):
    value = jnp.zeros(codes.shape, jnp.float32)
    for index_c in range(NF):
        value = jnp.where(codes == index_c + 1, table[index_c], value)
    return value


def placed_pair(pair, is_low):
    blank = jnp.zeros((6, pair.shape[1]), pair.dtype)
    return jnp.where(
        is_low, jnp.concatenate([pair, blank], 0), jnp.concatenate([blank, pair], 0)
    )


def placed_row(row, is_low):
    blank = jnp.zeros((7, row.shape[1]), row.dtype)
    return jnp.where(is_low, jnp.concatenate([row, blank], 0), jnp.concatenate([blank, row], 0))


def rim_slots(is_low, state, codes, f0, f1, f2, inject, produce):
    def pair(value):
        return jnp.where(is_low, value[6:8], value[0:2])

    def near(one, two):
        value = jnp.concatenate([one[0:8], two[0:8]], 0)
        return jnp.concatenate(
            [
                jnp.where(is_low, value[7:8], value[0:1]),
                jnp.where(is_low, value[15:16], value[8:9]),
            ],
            0,
        )

    return [
        pair(state),
        pair((codes + 1).astype(jnp.float32)),
        pair(f0),
        near(f1, f2),
        near(inject.astype(jnp.float32), produce.astype(jnp.float32)),
    ]


def corner_kernel(where_ref, st, cp, fa, ij, pr, corners, state, field, codes, sems):
    is_low = where_ref[1] == 0
    rows, cols = st.shape[1], st.shape[2]
    wide = XH * W
    at = pl.ds(pl.multiple_of(jnp.where(is_low, rows - 8, 0), 8), 8)
    copies = []
    for side, start in enumerate((0, cols - wide)):
        lanes = pl.ds(start, wide)
        for source, target in (
            (st.at[0, at, lanes], state.at[side]),
            (cp.at[0, :, at, lanes], field.at[side]),
            (fa.at[0, at, lanes], codes.at[side, 0]),
            (ij.at[0, at, lanes], codes.at[side, 1]),
            (pr.at[0, at, lanes], codes.at[side, 2]),
        ):
            copy = pltpu.make_async_copy(source, target, sems.at[len(copies)])
            copy.start()
            copies.append(copy)
    for copy in copies:
        copy.wait()
    for side in range(2):
        slots = rim_slots(
            is_low, state[side], codes[side, 0], field[side, 0], field[side, 1], field[side, 2],
            codes[side, 1], codes[side, 2],
        )
        for index, slot in enumerate(slots):
            start = (2 * index + side) * wide
            corners[:, start : start + wide] = slot


def edges_kernel(where_ref, st, cp, fa, ij, pr, to_right, to_left, across):
    is_low = where_ref[1] == 0
    rows, cols = st.shape[1], st.shape[2]
    wide = XH * W
    for target, start in ((to_right, cols - wide), (to_left, 0)):
        at = slice(start, start + wide)
        parts = [
            st[0, :, at],
            (fa[0, :, at] + 1).astype(jnp.float32),
            cp[0, 0, :, at],
            cp[0, 1, :, at],
            cp[0, 2, :, at],
            ij[0, :, at].astype(jnp.float32),
            pr[0, :, at].astype(jnp.float32),
        ]
        for index, part in enumerate(parts):
            target[:, index * wide : (index + 1) * wide] = part
    rim = pl.ds(pl.multiple_of(jnp.where(is_low, rows - 8, 0), 8), 8)
    slots = rim_slots(
        is_low, st[0, rim, :], fa[0, rim, :], cp[0, 0, rim, :], cp[0, 1, rim, :],
        cp[0, 2, rim, :], ij[0, rim, :], pr[0, rim, :],
    )
    for index, slot in enumerate(slots):
        across[:, index * cols : (index + 1) * cols] = slot


def pack_kernel(right_in, left_in, corners, to_right, to_left):
    wide = XH * W
    for side, (source, target) in enumerate(((left_in, to_left), (right_in, to_right))):
        target[:, : 7 * wide] = source[...]
        target[:, 7 * wide :] = jnp.zeros((32, LANES), jnp.float32)
        for index in range(5):
            for row in range(2):
                for half in range(2):
                    start = (2 * index + side) * wide + half * LANES
                    place = index * 4 + row * 2 + half
                    target[place : place + 1, 7 * wide :] = corners[
                        row : row + 1, start : start + LANES
                    ]


def put_cells(refs, is_press, tables, e, rows, cells):
    v0, prop, rock, c0, c1, c2, src, snk = refs
    state, codes, f0, f1, f2, inject, produce = cells
    v0[e + 1, rows, :] = state
    prop[e + 1, rows, :] = look_up(tables[0], codes)
    if is_press is not True:
        rock[e + 1, rows, :] = look_up(tables[1], codes)
    c0[e + 1, rows, :] = f0
    c1[e + 1, rows, :] = f1
    c2[e + 1, rows, :] = f2
    if is_press is True:
        src[e + 1, rows, :], snk[e + 1, rows, :] = 2.0 * inject - produce, produce
    elif is_press is False:
        src[e + 1, rows, :], snk[e + 1, rows, :] = 0.1 * inject, produce + inject
    else:
        src[e + 1, rows, :] = jnp.where(is_press, 2.0 * inject - produce, 0.1 * inject)
        snk[e + 1, rows, :] = jnp.where(is_press, produce, produce + inject)


def class_tables(is_press, perm_ref, cond_ref):
    perm = [perm_ref[index_c] for index_c in range(NF)]
    own = [jnp.where(is_press, perm[index_c], cond_ref[index_c]) for index_c in range(NF)]
    return own, perm


def fill_own(refs, is_press, tables, own_rows, raw):
    st, cp, fa, ij, pr = raw

    def fill(t, carry):
        at = lanes_at(t)
        cells = (
            st[0, :, at], fa[0, :, at] + 1, cp[0, 0, :, at], cp[0, 1, :, at], cp[0, 2, :, at],
            ij[0, :, at].astype(jnp.float32), pr[0, :, at].astype(jnp.float32),
        )
        put_cells(refs, is_press, tables, t + XH // 2, own_rows, cells)
        return carry

    lax.fori_loop(0, st.shape[2] // LANES, fill, 0, unroll=8)


def turn_kernel(
    where_ref, perm_ref, cond_ref, st, cp, fa, ij, pr, corners,
    own, other, rim, fluid, v0, prop, rock, c0, c1, c2, src, snk,
):
    del corners
    is_heat = where_ref[0] == 1
    is_low = where_ref[1] == 0
    own_rows = pl.ds(pl.multiple_of(jnp.where(is_low, 0, 8), 8), 32)
    groups = st.shape[2] // (4 * LANES)
    extra = groups * 2 * LANES
    row = lax.broadcasted_iota(jnp.int32, (32, LANES), 0)

    def step(group, rims):
        tall = jnp.concatenate(
            [st[0, :, lanes_at(4 * group + q)] for q in range(4)], axis=0
        )
        tall = jnp.where(is_heat, flowability(tall), tall)
        for q in range(4):
            fluid[4 * group + q + XH // 2 + 1, own_rows, :] = tall[32 * q : 32 * q + 32]
        turned = tall.T
        for par in range(2):
            low = turned[par * HALF : par * HALF + 32]
            high = turned[par * HALF + 32 : par * HALF + 64]
            own[:, lanes_at(group, par * groups * LANES)] = jnp.where(is_low, low, high)
            away = jnp.where(is_low, high, low)
            rim = high[0:1]

            other[:, lanes_at(group, par * groups * LANES)] = away
            rims = jnp.where(row == par * groups + group, rim, rims)
        return rims

    rims = lax.fori_loop(0, groups, step, jnp.zeros((32, LANES), jnp.float32), unroll=8)
    rim[:, :LANES] = jnp.where(is_low, rims, 0.0)
    other[:, extra : extra + LANES] = jnp.where(is_low, 0.0, rims)
    refs = (v0, prop, rock, c0, c1, c2, src, snk)
    tables = class_tables(jnp.logical_not(is_heat), perm_ref, cond_ref)

    @pl.when(is_heat)
    def _():
        fill_own(refs, False, tables, own_rows, (st, cp, fa, ij, pr))


def plane_kernel(where_ref, from_right, own_in, *rest):
    del own_in
    own = rest[-1]
    is_heat = where_ref[0] == 1
    is_low = where_ref[1] == 0
    wide = XH * W
    value = from_right[:, 0:LANES]
    inside = from_right[:, wide : wide + LANES] > 0.5
    value = jnp.where(is_heat, jnp.where(inside, flowability(value), 0.0), value)
    tall = jnp.concatenate([value, value, jnp.zeros((64, LANES), jnp.float32)], 0).T
    low, high = tall[0:32], tall[32:64]
    keep = lane_index((32, LANES)) < 32
    own[:, own.shape[1] - LANES :] = jnp.where(keep == is_low, low, high)


def send_kernel(boundary_in, rim, boundary):
    del boundary_in
    first = boundary.shape[1] - 16 * LANES
    for index in range(16):
        start = first + index * LANES
        boundary[:, start : start + LANES] = rim[2 * index : 2 * index + 2, LANES:]


def sweep(tiles, coeffs, force, diag, now, last, target, weight, pull, rows=slice(None)):
    first, stop = tiles
    shape = now[0, rows].shape
    low_lanes = lane_index(shape) < HALF

    def step(e, carry):
        before, here = carry
        tall = now[e + 1]
        value = tall[rows]
        after = half_turn(now[e + 2, rows])
        total = force[e + 1, rows]
        total += coeffs[0, e + 1, rows] * next_row(tall)[rows]
        total += coeffs[1, e + 1, rows] * prev_row(tall)[rows]
        total += coeffs[2, e + 1, rows] * jnp.where(low_lanes, here, after)
        total += coeffs[3, e + 1, rows] * jnp.where(low_lanes, before, here)
        total += coeffs[4, e + 1, rows] * next_lane(value)
        total += coeffs[5, e + 1, rows] * prev_lane(value)
        if diag is None:
            result = (1.0 + pull - weight) * value + weight * total
        else:
            result = (1.0 + pull) * value + weight * (total - diag[e + 1, rows] * value)
        if pull != 0.0:
            result -= pull * last[e + 1, rows]
        target(e, result)
        return here, after

    lax.fori_loop(
        first, stop, step,
        (half_turn(now[first, rows]), half_turn(now[first + 1, rows])),
        unroll=stop - first,
    )


def store_in(ref):
    def put(e, value):
        ref[e + 1] = value

    return put


def rim_cells(is_low, read):
    def pair(index):
        return placed_pair(jnp.concatenate([read(index, 0), read(index, 1)], 0), is_low)

    def near(index, row):
        return placed_row(read(index, row), is_low)

    return (
        pair(0), pair(1).astype(jnp.int32), pair(2),
        near(3, 0), near(3, 1), near(4, 0), near(4, 1),
    )


def rim_rows(is_low):
    return pl.ds(pl.multiple_of(jnp.where(is_low, 32, 0), 8), 8)


def put_level(fluid, cells, e, rows):
    prop, state = cells[1][e + 1, rows, :], cells[0][e + 1, rows, :]
    fluid[e + 1, rows, :] = jnp.where(prop > 0.0, flowability(state), 0.0)


def clear(refs, places):
    for ref in refs:
        for e in places:
            ref[e] = jnp.zeros(ref.shape[1:], jnp.float32)


def flow_pair(mean, flow, field):
    speed = flow * field
    gain = mean + jnp.maximum(speed, 0.0)
    return gain, gain - speed


def heat_b_terms(cells, made, e):
    v0, prop, rock, c0, c1, c2, src, snk = cells
    coeffs, force, diag, fluid = made
    value, level = prop[e + 1], fluid[e + 1]
    not_last = lane_index(value.shape) % W != W - 1
    gain, loss = flow_pair(
        face_mean(value, jnp.where(not_last, next_lane(value), 0.0)),
        face_mean(level, jnp.where(not_last, next_lane(level), 0.0)),
        c2[e + 1],
    )
    coeffs[4, e + 1] = loss
    coeffs[5, e + 1] = prev_lane(gain)
    diag[e + 1] = snk[e + 1] + gain + prev_lane(loss)


def face_terms(cells, made, is_press, ranges):
    v0, prop, rock, c0, c1, c2, src, snk = cells
    coeffs, force, diag, fluid = made
    shape = v0.shape[1:]
    lane = lane_index(shape)
    low_lanes = lane < HALF
    not_last = lane % W != W - 1
    blank = jnp.zeros(shape, jnp.float32)

    last_tile = v0.shape[0] - 3

    def inside(e):
        return min(e, last_tile) if isinstance(e, int) else e

    def run(step, first, stop, start):
        if stop - first > 8:
            unroll = max(n for n in range(1, 10) if (stop - first) % n == 0)
            return lax.fori_loop(first, stop, step, start, unroll=unroll)
        for e in range(first, stop):
            start = step(e, start)
        return start

    def beside(value, turns, after):
        return (
            jnp.where(low_lanes, turns[0], after[0]),
            jnp.where(not_last, turns[1], 0.0),
        )

    def press_range(first, stop):
        def turns(e):
            value = prop[e + 1]
            return half_turn(value), next_lane(value)

        def along(e, now, after):
            value = prop[e + 1]
            x_side, b_side = beside(value, now, after)
            return face_mean(value, x_side) * c1[e + 1], face_mean(value, b_side) * c2[e + 1]

        def close(e, before, plus, turned):
            value = prop[e + 1]
            plus = [face_mean(value, next_row(value)) * c0[e + 1], *plus]
            minus = [prev_row(plus[0]), jnp.where(low_lanes, before, turned[0]), turned[1]]
            scale = inverse(accumulate(plus + minus) + STORAGE + snk[e + 1])
            for dim in range(3):
                coeffs[2 * dim, e + 1] = scale * plus[dim]
                coeffs[2 * dim + 1, e + 1] = scale * minus[dim]
            force[e + 1] = scale * (src[e + 1] + STORAGE * v0[e + 1])

        def step(e, carry):
            before, plus, turned, now, after = carry
            close(e - 1, before, plus, turned)
            later = turns(inside(e + 2))
            fresh = along(e, now, after)
            return turned[0], fresh, (half_turn(fresh[0]), prev_lane(fresh[1])), after, later

        now, after = turns(first), turns(first + 1)
        before = blank
        if first > 0:
            before = half_turn(along(first - 1, turns(first - 1), now)[0])
        fresh = along(first, now, after)
        carry = (
            before, fresh, (half_turn(fresh[0]), prev_lane(fresh[1])), after, turns(first + 2)
        )
        before, plus, turned, _, _ = run(step, first + 1, stop, carry)
        close(stop - 1, before, plus, turned)

    def heat_range(first, stop):
        def turns(e):
            return half_turn(prop[e + 1]), half_turn(fluid[e + 1])

        def along(e, now, after):
            value, level = prop[e + 1], fluid[e + 1]
            return flow_pair(
                face_mean(value, jnp.where(low_lanes, now[0], after[0])),
                face_mean(level, jnp.where(low_lanes, now[1], after[1])),
                c1[e + 1],
            )

        def close(e, before, turned):
            value, level = prop[e + 1], fluid[e + 1]
            gain, loss = flow_pair(
                face_mean(value, next_row(value)), face_mean(level, next_row(level)), c0[e + 1]
            )
            coeffs[0, e + 1] = loss
            coeffs[1, e + 1] = prev_row(gain)
            coeffs[3, e + 1] = jnp.where(low_lanes, before[0], turned[0])
            total = diag[e + 1] + gain + prev_row(loss)
            diag[e + 1] = total + turned[2] + jnp.where(low_lanes, before[1], turned[1])

        def opened(e, now, after):
            gain, loss = along(e, now, after)
            coeffs[2, e + 1] = loss
            return half_turn(gain), half_turn(loss), gain

        def step(e, carry):
            before, turned, now, after = carry
            close(e - 1, before, turned)
            later = turns(inside(e + 2))
            return turned[:2], opened(e, now, after), after, later

        def b_steps(first, stop):
            def b_step(e, carry):
                heat_b_terms(cells, made, e)
                return carry

            if stop - first > 8:
                lax.fori_loop(first, stop, b_step, 0, unroll=8)
            else:
                for e in range(first, stop):
                    b_step(e, 0)

        b_steps(first, stop)
        now, after = turns(first), turns(first + 1)
        before = (blank, blank)
        if first > 0:
            gain, loss = along(first - 1, turns(first - 1), now)
            before = half_turn(gain), half_turn(loss)
        carry = (before, opened(first, now, after), after, turns(first + 2))
        before, turned, _, _ = run(step, first + 1, stop, carry)
        close(stop - 1, before, turned)

    @pl.when(is_press)
    def _():
        for first, stop in ranges:
            press_range(first, stop)

    @pl.when(jnp.logical_not(is_press))
    def _():
        for first, stop in ranges:
            heat_range(first, stop)


def inner_kernel(where_ref, perm_ref, cond_ref, across, st, cp, fa, ij, pr, *refs):
    coeffs, force, diag, fluid = refs[-12:-8]
    cells = refs[-8:]
    is_press = where_ref[0] == 0
    is_low = where_ref[1] == 0
    ext = cells[0].shape[0] - 2
    side = XH // 2
    tiles = ext - XH
    cols = tiles * LANES
    rows = rim_rows(is_low)
    tables = class_tables(is_press, perm_ref, cond_ref)
    clear(tuple(cells[:3]) + (fluid,), (0, 1, 2, ext - 1, ext, ext + 1))

    @pl.when(is_press)
    def _():
        own_rows = pl.ds(pl.multiple_of(jnp.where(is_low, 0, 8), 8), 32)
        fill_own(cells, True, tables, own_rows, (st, cp, fa, ij, pr))

    def fill(t, carry):
        read = lambda index, row: across[row : row + 1, lanes_at(t, index * cols)]
        put_cells(cells, is_press, tables, t + side, rows, rim_cells(is_low, read))
        put_level(fluid, cells, t + side, rows)
        return carry

    lax.fori_loop(0, tiles, fill, 0, unroll=16)
    made = (coeffs, force, diag, fluid)
    face_terms(cells, made, is_press, [(side, ext - side)])


def main_kernel(where_ref, perm_ref, cond_ref, from_left, from_right, *refs):
    v1, v2, boundary = refs[12:15]
    coeffs, force, diag, fluid = refs[15:19]
    cells = refs[19:]
    v0 = cells[0]
    is_press = where_ref[0] == 0
    is_low = where_ref[1] == 0
    ext = v0.shape[0] - 2
    wide = XH * W
    side = XH // 2
    own_rows = pl.ds(pl.multiple_of(jnp.where(is_low, 0, 8), 8), 32)
    tables = class_tables(is_press, perm_ref, cond_ref)

    for e, message, at in (
        (0, from_left, 0), (1, from_left, 1), (ext - 2, from_right, 0), (ext - 1, from_right, 1)
    ):
        parts = [message[:, lanes_at(at, index * wide)] for index in range(7)]
        parts[1] = parts[1].astype(jnp.int32)
        put_cells(cells, is_press, tables, e, own_rows, parts)
        corner = message[:, 7 * wide :]
        read = lambda index, row, corner=corner, at=at: corner[
            index * 4 + row * 2 + at : index * 4 + row * 2 + at + 1
        ]
        put_cells(cells, is_press, tables, e, rim_rows(is_low), rim_cells(is_low, read))
        put_level(fluid, cells, e, slice(None))
    clear((v1, v2), (0, ext + 1))
    clear((v2,), (1, ext))
    for e in (0, ext - 1):
        boundary[:, e * LANES : (e + 1) * LANES] = jnp.zeros((2, LANES), jnp.float32)
    made = (coeffs, force, diag, fluid)
    face_terms(cells, made, is_press, [(0, side + 1), (ext - side - 1, ext)])
    chebyshev, explicit = sweep_weights()
    src = cells[6]

    is_high = jnp.logical_not(is_low)

    for chosen, weights, centre, drive in (
        (is_press, chebyshev, None, force),
        (jnp.logical_not(is_press), explicit, diag, src),
    ):

        @pl.when(chosen)
        def _(weights=weights, centre=centre, force=drive):
            (w0, u0), (w1, u1) = weights[:2]
            sweep((0, ext), coeffs, force, centre, v0, v0, store_in(v1), w0, u0)
            for placed, rows, edge in (
                (is_low, slice(0, 32), slice(30, 32)), (is_high, slice(8, 40), slice(0, 2))
            ):

                @pl.when(placed)
                def _(rows=rows, edge=edge):
                    def put(e, value):
                        v2[e + 1, rows] = value
                        boundary[:, lanes_at(e)] = value[edge]

                    sweep((1, ext - 1), coeffs, force, centre, v1, v0, put, w1, u1, rows)


def finish_kernel(
    where_ref, v1, v2_in, fresh, coeffs, force, src, diag, boundary, edge, rim,
    out_ref, now, received, later, out, tile, sems,
):
    del v2_in
    is_press = where_ref[0] == 0
    is_low = where_ref[1] == 0
    ext = now.shape[0] - 2
    side = XH // 2
    tiles = ext - XH
    rows = rim_rows(is_low)
    most = pl.ds(0, (tiles - 1) * LANES)
    face_copies = [
        pltpu.make_async_copy(fresh.at[0], received.at[0, 0], sems.at[PARTS + 1]),
        pltpu.make_async_copy(
            fresh.at[1, :, most], received.at[0, 1, :, most], sems.at[PARTS + 2]
        ),
        pltpu.make_async_copy(fresh.at[2], received.at[0, 2], sems.at[PARTS + 3]),
    ]
    for copy in face_copies:
        copy.start()
    clear((later,), (0, ext + 1))
    lane = lane_index((32, LANES))
    mine = rim[:, LANES:]
    start = boundary.shape[1] - 16 * LANES
    theirs = jnp.concatenate(
        [boundary[:, start + index * LANES : start + (index + 1) * LANES] for index in range(16)],
        0,
    )
    plane = jnp.where(
        is_low,
        jnp.where(lane < 32, mine, theirs),
        jnp.where(lane < 32, pltpu.roll(theirs, 96, 1), pltpu.roll(mine, 32, 1)),
    )
    here = edge[0]
    beside = jnp.where(lane < HALF, half_turn(here), half_turn(plane))
    tile[...] = jnp.where(is_press, face_mean(here, beside), edge[1] * (here - beside))
    last_tile = pl.ds((tiles - 1) * LANES, LANES)
    tile_copy = pltpu.make_async_copy(tile, received.at[0, 1, :, last_tile], sems.at[PARTS])
    tile_copy.start()

    def fill(e, carry):
        now[e + 1, rows, :] = placed_pair(boundary[:, lanes_at(e)], is_low)
        return carry

    lax.fori_loop(0, ext, fill, 0, unroll=17)
    chebyshev, explicit = sweep_weights()

    def put_out(e, value):
        out[:, lanes_at(e - side)] = value

    is_high = jnp.logical_not(is_low)
    for chosen, weights, centre, drive in (
        (is_press, chebyshev, None, force),
        (jnp.logical_not(is_press), explicit, diag, src),
    ):

        @pl.when(chosen)
        def _(weights=weights, centre=centre, force=drive):
            (w2, u2), (w3, u3) = weights[2:]
            sweep((1, ext - 1), coeffs, force, centre, now, v1, store_in(later), w2, u2)
            for placed, rows in ((is_low, slice(0, 32)), (is_high, slice(8, 40))):

                @pl.when(placed)
                def _(rows=rows):
                    part = tiles // PARTS
                    copies = []
                    for index in range(PARTS):
                        first = side + index * part
                        sweep(
                            (first, first + part), coeffs, force, centre, later, now, put_out,
                            w3, u3, rows,
                        )
                        at = pl.ds(index * part * LANES, part * LANES)
                        copy = pltpu.make_async_copy(
                            out.at[:, at], out_ref.at[0, :, at], sems.at[index]
                        )
                        copy.start()
                        copies.append(copy)
                    for copy in copies:
                        copy.wait()

    for copy in face_copies:
        copy.wait()
    tile_copy.wait()


def regrouped(pieces):
    lane = lane_index(pieces[0].shape)
    result = []
    for q in range(4):
        value = None
        for place in range(4):
            piece = pieces[place]
            if place != q:
                piece = pltpu.roll(piece, ((place - q) * 32) % LANES, 1)
            value = piece if value is None else jnp.where(lane >= place * 32, piece, value)
        result.append(value)
    return result


def faces_kernel(
    where_ref, own, other, own_rim, rock, out, edge, field, rim
):
    is_press = where_ref[0] == 0
    is_low = where_ref[1] == 0
    tiles = out.shape[2] // LANES
    groups = tiles // 4
    side = XH // 2
    extra = groups * 2 * LANES

    def ordered(mine, theirs):
        return [jnp.where(is_low, mine, theirs), jnp.where(is_low, theirs, mine)]

    pieces = []
    for par in range(2):
        pieces += ordered(
            own_rim[par * groups : (par + 1) * groups, :LANES],
            other[par * groups : (par + 1) * groups, extra : extra + LANES],
        )
    for q, value in enumerate(regrouped(pieces)):
        rim[q] = value
    lane = lane_index((32, LANES))
    field[tiles] = jnp.zeros(field.shape[1:], jnp.float32)

    def gather(group, carry):
        pieces = []
        for par in range(2):
            at = lanes_at(group, par * groups * LANES)
            pieces += ordered(own[:, at], other[:, at])
        for q, value in enumerate(regrouped(pieces)):
            field[4 * group + q, 0:32, :] = value
            field[4 * group + q, 32:33, :] = rim[q, pl.ds(group, 1), :]
        return carry

    lax.fori_loop(0, groups, gather, 0, unroll=16)
    low_lanes = lane < HALF
    not_last = lane % W != W - 1

    def around(t, turned):
        value = field[t]
        here = value[0:32]
        after = half_turn(field[t + 1, 0:32, :])
        others = next_row(value)[0:32], jnp.where(low_lanes, turned, after), next_lane(here)
        return here, others, after

    def press(t, carry):
        here, others, after = around(t, carry)
        others = (others[0], others[1], jnp.where(not_last, others[2], 0.0))
        for dim in range(3):
            out[dim, :, lanes_at(t)] = face_mean(here, others[dim])
        return after

    def heat(t, carry):
        here, others, after = around(t, carry[0])
        stone = rock[t + side + 1, own_rows, :]
        stone_after = half_turn(rock[t + side + 2, own_rows, :])
        rim_row = jnp.where(is_low, rock[t + side + 1, 32:33, :], 0.0)
        near = (
            jnp.where(last_row, rim_row, next_row(stone)),
            jnp.where(low_lanes, carry[1], stone_after),
            jnp.where(not_last, next_lane(stone), 0.0),
        )
        for dim in range(3):
            mean = face_mean(stone, near[dim])
            out[dim, :, lanes_at(t)] = mean * (here - others[dim])
        return after, stone_after

    own_rows = pl.ds(pl.multiple_of(jnp.where(is_low, 0, 8), 8), 32)
    last_row = lax.broadcasted_iota(jnp.int32, (32, LANES), 0) == 31
    edge[0] = field[tiles - 1, 0:32, :]
    stone = rock[tiles - 1 + side + 1, own_rows, :]
    stone_after = half_turn(rock[tiles + side + 1, own_rows, :])
    edge[1] = face_mean(stone, jnp.where(low_lanes, half_turn(stone), stone_after))

    @pl.when(is_press)
    def _():
        lax.fori_loop(0, tiles, press, half_turn(field[0, 0:32, :]), unroll=16)

    @pl.when(jnp.logical_not(is_press))
    def _():
        start = half_turn(field[0, 0:32, :]), half_turn(rock[side + 1, own_rows, :])
        lax.fori_loop(0, tiles, heat, start, unroll=16)


def paired_body(states, coupled, facies, injectors, producers, perm_table, cond_table):
    rows, cols = states.shape[1], states.shape[2]
    tiles = cols // LANES
    ext = tiles + XH
    wide = XH * W
    groups = tiles // 4
    loaded = [held(value) for value in (states, coupled, facies, injectors, producers)]
    place = jnp.stack([lax.axis_index("code"), lax.axis_index("ba")]).astype(jnp.int32)
    count = lax.axis_size("aa")
    up = [(i, i + 1) for i in range(count - 1)]
    down = [(b, a) for a, b in up]
    swap = [(0, 1), (1, 0)]
    opposite = [(0, 3), (1, 2), (2, 1), (3, 0)]
    f32, i32 = jnp.float32, jnp.int32
    states, coupled, facies, injectors, producers = [
        pltpu.with_memory_space_constraint(value, pltpu.HBM)
        for value in (states, coupled, facies, injectors, producers)
    ]

    corners = pl.pallas_call(
        corner_kernel,
        out_shape=in_vmem((2, 10 * wide)),
        in_specs=[SM] + [HB] * 5,
        out_specs=VM,
        scratch_shapes=[
            pltpu.VMEM((2, 8, wide), f32),
            pltpu.VMEM((2, 3, 8, wide), f32),
            pltpu.VMEM((2, 3, 8, wide), i32),
            pltpu.SemaphoreType.DMA((10,)),
        ],
        compiler_params=LEAN,
        cost_estimate=cost(1),
        name="corner",
    )(place, states, coupled, facies, injectors, producers)
    corners = held(lax.ppermute(corners, "ba", swap))
    to_right, to_left, across = pl.pallas_call(
        edges_kernel,
        out_shape=[
            in_vmem((rows, 7 * wide)),
            in_vmem((rows, 7 * wide)),
            in_vmem((2, 5 * cols)),
        ],
        in_specs=[SM] + [VM] * 5,
        out_specs=[VM] * 3,
        compiler_params=LEAN,
        cost_estimate=cost(2),
        name="edges",
    )(place, *loaded)
    from_across = held(lax.ppermute(across, "ba", swap))
    to_right, to_left = pl.pallas_call(
        pack_kernel,
        out_shape=[in_vmem((rows, 7 * wide + LANES))] * 2,
        in_specs=[VM] * 3,
        out_specs=[VM] * 2,
        compiler_params=LEAN,
        cost_estimate=cost(1),
        name="pack",
    )(to_right, to_left, corners)
    from_left = held(lax.ppermute(to_right, "aa", up))
    from_right = held(lax.ppermute(to_left, "aa", down))

    field = (ext + 2, rows + 8, LANES)
    turned_own, turned_other, rim, fluid, *cells = pl.pallas_call(
        turn_kernel,
        out_shape=[
            in_vmem((32, 2 * groups * LANES)),
            in_vmem((32, (2 * groups + 1) * LANES)),
            in_vmem((32, 2 * LANES)),
        ]
        + [in_vmem(field)] * 9,
        in_specs=[SM] * 3 + [VM] * 6,
        out_specs=[VM] * 12,
        compiler_params=params(2),
        cost_estimate=cost(2.5),
        name="turn",
    )(
        place, perm_table, cond_table, *loaded, to_left,
    )
    other = held(lax.ppermute(turned_other, ("code", "ba"), opposite))
    own = held(lax.ppermute(turned_own, "code", swap))
    coeffs, force, diag, fluid, *cells = pl.pallas_call(
        inner_kernel,
        out_shape=[in_vmem((6,) + field)] + [in_vmem(field)] * 11,
        in_specs=[SM] * 3 + [VM] * 15,
        out_specs=[VM] * 12,
        input_output_aliases={9 + index: 3 + index for index in range(9)},
        compiler_params=params(2),
        cost_estimate=cost(10),
        name="inner",
    )(place, perm_table, cond_table, from_across, *loaded, fluid, *cells)
    rim = pl.pallas_call(
        plane_kernel,
        out_shape=in_vmem(rim.shape),
        in_specs=[SM] + [VM] * 4,
        out_specs=VM,
        input_output_aliases={2: 0},
        compiler_params=LEAN,
        cost_estimate=cost(1),
        name="plane",
    )(place, from_right, rim, from_left, force)
    rim = held(lax.ppermute(rim, "code", swap))

    v1, v2, boundary, coeffs, force, diag, fluid, *cells = pl.pallas_call(
        main_kernel,
        out_shape=[in_vmem(field), in_vmem(field), in_vmem((2, (ext + 16) * LANES))]
        + [in_vmem((6,) + field)]
        + [in_vmem(field)] * 11,
        in_specs=[SM] * 3 + [VM] * 14,
        out_specs=[VM] * 15,
        input_output_aliases={5 + index: 3 + index for index in range(12)},
        compiler_params=params(2),
        cost_estimate=cost(10),
        name="main",
    )(
        place, perm_table, cond_table, from_left, from_right,
        coeffs, force, diag, fluid, *cells,
    )
    boundary = pl.pallas_call(
        send_kernel,
        out_shape=in_vmem(boundary.shape),
        in_specs=[VM] * 2,
        out_specs=VM,
        input_output_aliases={0: 0},
        compiler_params=LEAN,
        cost_estimate=cost(1),
        name="send",
    )(boundary, rim)
    boundary = held(lax.ppermute(boundary, "ba", swap))
    fresh, edge = pl.pallas_call(
        faces_kernel,
        out_shape=[in_vmem(coupled.shape[1:]), in_vmem((2, 32, LANES))],
        in_specs=[SM] + [VM] * 4,
        out_specs=[VM] * 2,
        scratch_shapes=[
            pltpu.VMEM((tiles + 1, rows + 8, LANES), f32),
            pltpu.VMEM((4, groups, LANES), f32),
        ],
        compiler_params=params(5),
        cost_estimate=cost(6),
        name="faces",
    )(place, own, other, rim, cells[2])
    stepped, _, received = pl.pallas_call(
        finish_kernel,
        out_shape=[
            jax.ShapeDtypeStruct(states.shape, f32),
            in_vmem(field),
            jax.ShapeDtypeStruct(coupled.shape, f32),
        ],
        in_specs=[SM] + [VM] * 10,
        out_specs=[HB, VM, HB],
        scratch_shapes=[
            pltpu.VMEM(field, f32),
            pltpu.VMEM(states.shape[1:], f32),
            pltpu.VMEM((32, LANES), f32),
            pltpu.SemaphoreType.DMA((PARTS + 4,)),
        ],
        input_output_aliases={2: 1},
        compiler_params=params(5),
        cost_estimate=cost(6),
        name="finish",
    )(place, v1, v2, fresh, coeffs, force, cells[6], diag, boundary, edge, rim)
    return (stepped, received)


def solution(mesh):
    paired = mesh.shape["ba"] == 2 and mesh.shape["code"] == 2
    return jax.shard_map(
        paired_body if paired else body,
        mesh=mesh,
        in_specs=(
            P("code", "ba", "aa"),
            P("code", None, "ba", "aa"),
            P("code", "ba", "aa"),
            P("code", "ba", "aa"),
            P("code", "ba", "aa"),
            P(),
            P(),
        ),
        out_specs=(P("code", "ba", "aa"), P("code", None, "ba", "aa")),
        check_vma=False,
    )
```
